32 devices in a mesh: groups: 2 (over y), inst: 4 (over x, core), tp: 4 (over z).
Axes of the slice: x: 2, y: 2, z: 4, core: 2. Of those that a mesh axis runs over, the one named last changes fastest.
Arguments:
- hidden: bfloat16 [2048, 5120], P(('groups', 'inst'), 'tp'), parts along dimension 0, may hold values from -6 to 6
- k_weight: bfloat16 [5120, 1024], P('inst', 'tp'), may hold values from -0.078125 to 0.078125
- v_weight: bfloat16 [5120, 1024], P('inst', 'tp'), may hold values from -0.078125 to 0.078125
- k_gain: float32 [128], replicated, may hold values from 0.25 to 1.75
- queries: bfloat16 [2048, 8192], P(('groups', 'inst'), 'tp'), parts along dimension 0, may hold values from -8 to 8
- kv_pool: bfloat16 [2, 432, 128, 1024], P(None, ('groups', 'inst'), None, 'tp'), parts along dimension 1, may hold values from -8 to 8
- page_holder: int32 [8, 48], P(('groups', 'inst')), parts along dimension 0, may hold values from 0 to 3, as said below
- page_slot: int32 [8, 48], P(('groups', 'inst')), parts along dimension 0, may hold values from 0 to 53, as said below
- page_count: int32 [8], P(('groups', 'inst')), parts along dimension 0, may hold values from 12 to 48, as said below
- write_owner: int32 [8, 2], P(('groups', 'inst')), parts along dimension 0, may hold values from 0 to 3, as said below
- write_slot: int32 [8, 2], P(('groups', 'inst')), parts along dimension 0, may hold values from 0 to 53, as said below
Outputs:
- attention_out: bfloat16 [2048, 8192], P(('groups', 'inst'), 'tp'), parts along dimension 0
- new_pool: bfloat16 [2, 432, 128, 1024], P(None, ('groups', 'inst'), None, 'tp'), parts along dimension 1
The draws below stay inside these ranges and needn't reach their ends.
There are 2 independent parts, one for each index of `groups`. The reference program is written for one: setup_inputs(seed, part) draws one part's arguments, and reference() takes and returns one part's arrays. A program takes and returns all parts, laid end to end along the dimension named above; an argument that names none is the same for every part. Nothing has to cross between parts.
Inputs may be any that keep to these rules, and one draw needn't show every extreme that they name: `page_holder`: no request has more than 18 of its pages j < page_count on one instance; the request with 48 pages has exactly 18 on one instance. `page_slot`: the history pages in use and the new pages' slots are distinct slots of their instance. `page_count`: one request has exactly 48 pages. `write_owner`: the 2 new pages of one request go to distinct instances. `write_slot`: distinct from every slot in use on the same instance.
All inputs are finite; a program needn't handle non-finite values.
Results may differ from the reference program's by a relative error of at most 0.0039.
Values may be sent and summed in bfloat16 or wider, within the bound.
No kernel may reach another device: no remote copies, remote signals or barrier semaphores. Data moves between devices by JAX's collectives and lax.ppermute only.
A program may use at most 192 MiB of HBM per device.

```python
import math
import jax
import jax.numpy as jnp
from jax import lax

D = 5120
QH = 64
KVH = 8
HD = 128
PAGE = 128
NEWP = 2
MAXP = 48
GROUP = 8
NEWTOK = 256
REQS = 4
TOKENS = 1024
CAP = 18
SLOTS = 54
N_INST = 4


def page_tables(key):
    subkeys = jax.random.split(key, 7)
    requests = jnp.arange(N_INST, dtype=jnp.int32)
    counts = jax.random.randint(subkeys[0], (N_INST,), MAXP // 4, MAXP + 1)
    longest = jax.random.randint(subkeys[1], (), 0, N_INST)
    counts = jnp.where(requests == longest, MAXP, counts).astype(jnp.int32)
    base = jax.random.permutation(subkeys[2], N_INST).astype(jnp.int32)
    others = jax.vmap(lambda subkey: jax.random.permutation(subkey, N_INST - 1))(jax.random.split(subkeys[3], N_INST)).astype(jnp.int32)
    positions = jnp.arange(MAXP, dtype=jnp.int32)
    extra = jnp.maximum(positions - CAP, 0)
    column = extra % (N_INST - 1)
    turn = extra // (N_INST - 1)
    picked = jnp.take_along_axis(others, jnp.broadcast_to(column[None, :], (N_INST, MAXP)), axis=1)
    away = (base[:, None] + 1 + picked) % N_INST
    holder = jnp.where(positions[None, :] < CAP, base[:, None], away).astype(jnp.int32)
    spare = (MAXP - CAP + N_INST - 2) // (N_INST - 1)
    owner_of = jnp.argsort(base).astype(jnp.int32)
    page_rank = requests[:, None] - (requests[:, None] > owner_of[holder]).astype(jnp.int32)
    raw_slot = jnp.where(positions[None, :] < CAP, positions[None, :], CAP + page_rank * spare + turn[None, :])
    first_owner = jax.random.permutation(subkeys[4], N_INST).astype(jnp.int32)
    offsets = jnp.concatenate([jnp.zeros((1,), jnp.int32), 1 + jax.random.permutation(subkeys[6], N_INST - 1).astype(jnp.int32)])[:NEWP]
    owner = ((first_owner[:, None] + offsets[None, :]) % N_INST).astype(jnp.int32)
    raw_new = jnp.broadcast_to(SLOTS - NEWP + jnp.arange(NEWP, dtype=jnp.int32)[None, :], (N_INST, NEWP))
    shuffles = jax.vmap(lambda subkey: jax.random.permutation(subkey, SLOTS))(jax.random.split(subkeys[5], N_INST)).astype(jnp.int32)
    slot = shuffles[holder, raw_slot].astype(jnp.int32)
    new_slot = shuffles[owner, raw_new].astype(jnp.int32)
    return (holder, slot, counts, owner, new_slot)


def draw_page_holder(key, part):
    return page_tables(key)[0]


def draw_page_slot(key, part):
    return page_tables(key)[1]


def draw_page_count(key, part):
    return page_tables(key)[2]


def draw_write_owner(key, part):
    return page_tables(key)[3]


def draw_write_slot(key, part):
    return page_tables(key)[4]


def draw_kv_pool(key, part):
    key = jax.random.fold_in(key, 21)
    shape = (2, N_INST * SLOTS, PAGE, KVH * HD)
    values = jnp.clip(jax.random.normal(key, shape, jnp.float32), -8.0, 8.0)
    return values.astype(jnp.bfloat16)


def draw_queries(key, part):
    key = jax.random.fold_in(key, 22)
    shape = (N_INST * NEWTOK, QH * HD)
    values = jnp.clip(2.5 * jax.random.normal(key, shape, jnp.float32), -8.0, 8.0)
    return values.astype(jnp.bfloat16)


def steps_of(stream_key, dims, cuts, low, top_value):
    gain, own = 1.0, jax.random.fold_in(stream_key, 6)
    for dim, parts in cuts:
        heights = jnp.exp(jax.random.uniform(jax.random.fold_in(own, dim), (parts,), jnp.float32, low / len(cuts), top_value / len(cuts)))
        gain = gain * jnp.repeat(heights, dims[dim] // parts).reshape([-1 if axis == dim else 1 for axis in range(len(dims))])
    return gain


def bell_draw(stream_key, dims, scale, bound, cuts=(), held_as=jnp.bfloat16):
    level = steps_of(stream_key, dims, cuts, -0.22, 0.18) if cuts else 1.0
    drawn = jax.random.normal(stream_key, dims, jnp.float32) * scale * level
    return jnp.minimum(jnp.maximum(drawn, -bound), bound).astype(held_as)


def setup_inputs(seed: int = 0, part: int = 0) -> dict:
    seeds = jax.random.split(jax.random.key(seed), 12)
    part_keys = jax.random.split(jax.random.fold_in(seeds[11], part), 12)
    hidden = bell_draw(part_keys[0], (TOKENS, D), 1.0, 6.0, ((0, 4), (1, 4)))
    k_weight = bell_draw(seeds[1], (D, KVH * HD), D ** -0.5, 0.078125, ((0, 4), (1, 4)))
    v_weight = bell_draw(seeds[2], (D, KVH * HD), D ** -0.5, 0.078125, ((0, 4), (1, 4)))
    k_gain = jnp.clip(1.0 + 0.15 * jax.random.normal(seeds[3], (HD,), jnp.float32), 0.25, 1.75)
    queries = draw_queries(jax.random.fold_in(jax.random.fold_in(seeds[11], part), 71), part)
    kv_pool = draw_kv_pool(jax.random.fold_in(jax.random.fold_in(seeds[11], part), 71), part)
    page_holder = draw_page_holder(jax.random.fold_in(jax.random.fold_in(seeds[11], part), 71), part)
    page_slot = draw_page_slot(jax.random.fold_in(jax.random.fold_in(seeds[11], part), 71), part)
    page_count = draw_page_count(jax.random.fold_in(jax.random.fold_in(seeds[11], part), 71), part)
    write_owner = draw_write_owner(jax.random.fold_in(jax.random.fold_in(seeds[11], part), 71), part)
    write_slot = draw_write_slot(jax.random.fold_in(jax.random.fold_in(seeds[11], part), 71), part)
    return {"hidden": hidden, "k_weight": k_weight, "v_weight": v_weight, "k_gain": k_gain, "queries": queries, "kv_pool": kv_pool, "page_holder": page_holder, "page_slot": page_slot, "page_count": page_count, "write_owner": write_owner, "write_slot": write_slot}


def normalize_rotate(raw_keys, k_gain, positions):
    per_head = raw_keys.reshape(raw_keys.shape[0], -1, HD)
    inverse_rms = lax.rsqrt(lax.optimization_barrier(jnp.mean(per_head * per_head, axis=-1, keepdims=True)) + 1e-06)
    per_head = per_head * inverse_rms * k_gain
    frequency = 1000000.0 ** (-(jnp.arange(HD // 2, dtype=jnp.float32) * 2.0) / HD)
    angles = positions.astype(jnp.float32)[:, None] * frequency[None, :]
    cosine = jnp.cos(angles)[:, None, :]
    sine_part = jnp.sin(angles)[:, None, :]
    first_half = per_head[..., :HD // 2]
    second = per_head[..., HD // 2:]
    rotated = jnp.concatenate([first_half * cosine - second * sine_part, second * cosine + first_half * sine_part], axis=-1)
    return rotated.reshape(raw_keys.shape)

def attend_head(operands):
    query_block, hist_keys, hist_values, fresh_keys, fresh_values, allowed = operands
    all_keys = jnp.concatenate([hist_keys, fresh_keys], axis=0).astype(jnp.float32)
    all_values = jnp.concatenate([hist_values, fresh_values], axis=0).astype(jnp.float32)
    scores = jnp.einsum('qgd,kd->gqk', query_block.astype(jnp.float32), all_keys) / math.sqrt(HD)
    scores = jnp.where(allowed[None], scores, -jnp.inf)
    row_max = lax.optimization_barrier(jnp.max(scores, axis=-1, keepdims=True))
    probabilities = jnp.exp(scores - row_max)
    totals = lax.optimization_barrier(jnp.sum(probabilities, axis=-1, keepdims=True))
    weights = lax.optimization_barrier(probabilities.astype(jnp.bfloat16)).astype(jnp.float32)
    return jnp.einsum('gqk,kd->gqd', weights, all_values) / totals

def reference(hidden, k_weight, v_weight, k_gain, queries, kv_pool, page_holder, page_slot, page_count, write_owner, write_slot):
    token_index = jnp.tile(jnp.arange(NEWTOK, dtype=jnp.int32), REQS)
    positions = jnp.repeat(page_count * PAGE, NEWTOK) + token_index
    raw_keys = jnp.dot(hidden, k_weight, preferred_element_type=jnp.float32)
    raw_values = jnp.dot(hidden, v_weight, preferred_element_type=jnp.float32)
    new_keys = normalize_rotate(raw_keys, k_gain, positions).astype(jnp.bfloat16)
    new_values = raw_values.astype(jnp.bfloat16)
    causal = jnp.arange(NEWTOK)[None, :] <= jnp.arange(NEWTOK)[:, None]

    def one_request(request):
        pool_rows = page_holder[request] * SLOTS + page_slot[request]
        history = kv_pool[:, pool_rows].reshape(2, MAXP * PAGE, KVH, HD)
        live_pages = jnp.repeat(jnp.arange(MAXP, dtype=jnp.int32) < page_count[request], PAGE)
        allowed = jnp.concatenate([jnp.broadcast_to(live_pages[None, :], (NEWTOK, MAXP * PAGE)), causal], axis=1)
        first_row = (request * NEWTOK).astype(jnp.int32)
        query_rows = lax.dynamic_slice_in_dim(queries, first_row, NEWTOK, 0).reshape(NEWTOK, KVH, GROUP, HD)
        fresh_keys = lax.dynamic_slice_in_dim(new_keys, first_row, NEWTOK, 0).reshape(NEWTOK, KVH, HD)
        fresh_values = lax.dynamic_slice_in_dim(new_values, first_row, NEWTOK, 0).reshape(NEWTOK, KVH, HD)
        per_head = lax.map(attend_head, (query_rows.transpose(1, 0, 2, 3), history[0].transpose(1, 0, 2), history[1].transpose(1, 0, 2), fresh_keys.transpose(1, 0, 2), fresh_values.transpose(1, 0, 2), jnp.broadcast_to(allowed[None], (KVH,) + allowed.shape)))
        return per_head.transpose(2, 0, 1, 3).reshape(NEWTOK, QH * HD)
    attention = lax.map(one_request, jnp.arange(REQS, dtype=jnp.int32))
    attention_out = attention.reshape(TOKENS, QH * HD).astype(jnp.bfloat16)
    target_rows = (write_owner * SLOTS + write_slot).reshape(-1)
    key_pages = new_keys.reshape(REQS * NEWP, PAGE, KVH * HD)
    value_pages = new_values.reshape(REQS * NEWP, PAGE, KVH * HD)
    new_pool = kv_pool.at[0, target_rows].set(key_pages).at[1, target_rows].set(value_pages)
    return (attention_out, new_pool)
```

```python
import functools
import math

import jax
import jax.numpy as jnp
from jax import lax
from jax.experimental import pallas as pl
from jax.experimental.pallas import tpu as pltpu
from jax.sharding import PartitionSpec as P

HD = 128
PAGE = 128
GROUP = 8
BLOCK = GROUP * HD
EXTRA = 128
TABLE_ROWS = 16
EMPTY = -1e30
LOG2E = 1.4426950408889634
SCALE = LOG2E / math.sqrt(HD)
CHUNK = 4
ANY = pl.BlockSpec(memory_space=pl.ANY)
SMEM = pl.BlockSpec(memory_space=pltpu.SMEM)
VMEM_LIMIT = 56 * 1024 * 1024


def row_dot(a, b):
    return lax.dot_general(a, b, (((1,), (1,)), ((), ())), preferred_element_type=jnp.float32)


def plain_dot(a, b):
    return lax.dot_general(a, b, (((1,), (0,)), ((), ())), preferred_element_type=jnp.float32)


def split_stats(stat, head, lanes):
    high = stat.astype(jnp.bfloat16).astype(jnp.float32)
    rest = stat - high
    middle = rest.astype(jnp.bfloat16).astype(jnp.float32)
    low = rest - middle
    zero = jnp.zeros(lanes.shape, jnp.float32)
    terms = jnp.where(lanes == 3 * head, high, zero)
    terms = jnp.where(lanes == 3 * head + 1, middle, terms)
    return jnp.where(lanes == 3 * head + 2, low, terms)


def joined_stats(payload, head):
    term = lax.broadcasted_iota(jnp.int32, (EXTRA, HD), 0)
    picked = jnp.where((term >= 3 * head) & (term < 3 * head + 3), 1.0, 0.0).astype(jnp.bfloat16)
    return plain_dot(payload[:, BLOCK : BLOCK + EXTRA], picked)


def attend_kernel(
    pages_listed, capacity, requests, kv_heads, copy_pool, me_ref, table_ref, *refs
):
    items = requests * len(kv_heads)
    q_refs = refs[:items]
    pool_ref, out_ref = refs[items], refs[items + 1]
    rest = refs[items + 2 :]
    if copy_pool:
        new_pool_ref, rest = rest[0], rest[1:]
    q_buf, kv_buf, acc, maxima, totals, out_buf, slots, q_sem, kv_sem, out_sem, pool_sem = rest
    width = len(kv_heads)
    new_count = q_buf.shape[2]

    def q_copies(item):
        source, offset = q_refs[item]
        return [
            pltpu.make_async_copy(
                source.at[pl.ds(0, new_count), pl.ds(offset + head * HD, HD)],
                q_buf.at[item, head],
                q_sem.at[item, head],
            )
            for head in range(GROUP)
        ]

    def page_copy(request, place, slot):
        return [
            pltpu.make_async_copy(
                pool_ref.at[:, slot, :, pl.ds(kv_head * HD, HD)],
                kv_buf.at[request, column, :, place],
                kv_sem.at[request, column, place],
            )
            for column, kv_head in enumerate(kv_heads)
        ]

    me = me_ref[0]
    for request in range(requests):

        def look(page, found, request=request):
            mine = (page < table_ref[request, 2 * pages_listed]) & (table_ref[request, page] == me)

            @pl.when(mine)
            def _():
                for copy in page_copy(request, found, table_ref[request, pages_listed + page]):
                    copy.start()

            return found + mine.astype(jnp.int32)

        slots[request] = lax.fori_loop(0, pages_listed, look, 0)
    for item in range(items):
        for copy in q_copies(item):
            copy.start()
    pool_copies = []
    if copy_pool:
        slot_total = pool_ref.shape[1]
        parts = 6 if slot_total % 6 == 0 else 1
        step = slot_total // parts
        pool_copies = [
            pltpu.make_async_copy(
                pool_ref.at[index, pl.ds(part * step, step)],
                new_pool_ref.at[index, pl.ds(part * step, step)],
                pool_sem.at[index, part],
            )
            for index in range(2)
            for part in range(parts)
        ]
        for copy in pool_copies:
            copy.start()
    for item in range(items):
        for copy in q_copies(item):
            copy.wait()

    lanes = lax.broadcasted_iota(jnp.int32, (new_count, EXTRA), 1)

    def one_item(item, carry):
        request = item // width
        column = item % width
        found = slots[request]

        @pl.when(column == 0)
        def _():
            def arrived(place, carry):
                for copy in page_copy(request, place, 0):
                    copy.wait()
                return carry

            lax.fori_loop(0, found, arrived, 0)

        acc[...] = jnp.zeros(acc.shape, jnp.float32)
        totals[...] = jnp.zeros(totals.shape, jnp.float32)
        maxima[...] = jnp.full(maxima.shape, EMPTY, jnp.float32)

        def chunk(first, count):
            keys = kv_buf[request, column, 0, pl.ds(first, count)].reshape(count * PAGE, HD)
            values = kv_buf[request, column, 1, pl.ds(first, count)].reshape(count * PAGE, HD)
            for head in range(GROUP):
                scores = row_dot(q_buf[item, head], keys)
                old = maxima[head]
                top = jnp.maximum(old, jnp.max(scores, axis=1, keepdims=True) * SCALE)
                rescale = jnp.exp2(old - top)
                total = totals[head] * rescale
                parts = []
                for part in range(count):
                    piece = jnp.exp2(scores[:, part * PAGE : (part + 1) * PAGE] * SCALE - top)
                    total = total + piece
                    parts.append(piece.astype(jnp.bfloat16))
                weights = jnp.concatenate(parts, axis=1) if count > 1 else parts[0]
                maxima[head] = top
                totals[head] = total
                acc[head] = acc[head] * rescale + plain_dot(weights, values)

        whole = found // CHUNK
        left = found % CHUNK

        def step(index, carry):
            chunk(index * CHUNK, CHUNK)
            return carry

        lax.fori_loop(0, whole, step, 0)
        for count in range(1, CHUNK):

            @pl.when(left == count)
            def _(count=count):
                chunk(whole * CHUNK, count)

        def finish(head, terms):
            total = jnp.sum(totals[head], axis=1, keepdims=True)
            some = total > 0.0
            inverse = jnp.where(some, 1.0 / jnp.where(some, total, 1.0), 0.0)
            out_buf[item, head] = (acc[head] * inverse).astype(jnp.bfloat16)
            stat = jnp.where(
                some, maxima[head] + jnp.log2(jnp.where(some, total, 1.0)), EMPTY
            )
            return terms + split_stats(stat, head, lanes)

        terms = lax.fori_loop(
            0, GROUP, finish, jnp.zeros((new_count, EXTRA), jnp.float32)
        )
        out_buf[item, GROUP] = terms.astype(jnp.bfloat16)
        for copy in out_copies(item):
            copy.start()
        return carry

    def out_copies(item):
        return [
            pltpu.make_async_copy(
                out_buf.at[item, head],
                out_ref.at[item, :, pl.ds(head * HD, HD)],
                out_sem.at[item, head],
            )
            for head in range(GROUP + 1)
        ]

    lax.fori_loop(0, items, one_item, 0)
    for item in range(items):
        for copy in out_copies(item):
            copy.wait()
    for copy in pool_copies:
        copy.wait()


def attend(me, tables, q_items, kv_heads, pool, pages_listed, capacity, new_count, copy_pool=False):
    requests, width = tables.shape[0], len(kv_heads)
    items = requests * width
    out_shape = [jax.ShapeDtypeStruct((items, new_count, BLOCK + EXTRA), jnp.bfloat16)]
    out_specs = [ANY]
    if copy_pool:
        out_shape.append(jax.ShapeDtypeStruct(pool.shape, pool.dtype))
        out_specs.append(ANY)
    offsets = [offset for _, offset in q_items]

    def kernel(me_ref, table_ref, *refs):
        paired = [(ref, offset) for ref, offset in zip(refs[:items], offsets)]
        attend_kernel(
            pages_listed, capacity, requests, kv_heads, copy_pool, me_ref, table_ref,
            *paired, *refs[items:],
        )

    assumed = items * 8 * PAGE * GROUP * new_count
    result = pl.pallas_call(
        kernel,
        out_shape=out_shape,
        in_specs=[SMEM, SMEM] + [ANY] * (items + 1),
        out_specs=out_specs,
        scratch_shapes=[
            pltpu.VMEM((items, GROUP, new_count, HD), jnp.bfloat16),
            pltpu.VMEM((requests, width, 2, capacity, PAGE, HD), jnp.bfloat16),
            pltpu.VMEM((GROUP, new_count, HD), jnp.float32),
            pltpu.VMEM((GROUP, new_count, HD), jnp.float32),
            pltpu.VMEM((GROUP, new_count, HD), jnp.float32),
            pltpu.VMEM((items, GROUP + 1, new_count, HD), jnp.bfloat16),
            pltpu.SMEM((requests,), jnp.int32),
            pltpu.SemaphoreType.DMA((items, GROUP)),
            pltpu.SemaphoreType.DMA((requests, width, capacity)),
            pltpu.SemaphoreType.DMA((items, GROUP + 1)),
            pltpu.SemaphoreType.DMA((2, 6)),
        ],
        compiler_params=pltpu.CompilerParams(vmem_limit_bytes=VMEM_LIMIT),
        cost_estimate=pl.CostEstimate(
            flops=8 * assumed * HD, bytes_accessed=items * 4 * 1024 * 1024, transcendentals=assumed
        ),
    )(me, tables, *[array for array, _ in q_items], pool)
    return result if copy_pool else result[0]


def merge_kernel(a_ref, b_ref, out_ref):
    new_count = a_ref.shape[0]
    lanes = lax.broadcasted_iota(jnp.int32, (new_count, EXTRA), 1)
    terms = jnp.zeros((new_count, EXTRA), jnp.float32)
    for head in range(GROUP):
        stat_a, stat_b = joined_stats(a_ref, head), joined_stats(b_ref, head)
        top = jnp.maximum(stat_a, stat_b)
        share_a, share_b = jnp.exp2(stat_a - top), jnp.exp2(stat_b - top)
        total = share_a + share_b
        columns = pl.ds(head * HD, HD)
        mixed = (
            a_ref[:, columns].astype(jnp.float32) * share_a
            + b_ref[:, columns].astype(jnp.float32) * share_b
        ) / total
        out_ref[:, columns] = mixed.astype(jnp.bfloat16)
        terms = terms + split_stats(top + jnp.log2(total), head, lanes)
    out_ref[:, pl.ds(BLOCK, EXTRA)] = terms.astype(jnp.bfloat16)


def merge(a, b):
    return pl.pallas_call(
        merge_kernel,
        out_shape=jax.ShapeDtypeStruct(a.shape, a.dtype),
        compiler_params=pltpu.CompilerParams(vmem_limit_bytes=VMEM_LIMIT),
        cost_estimate=pl.CostEstimate(
            flops=16 * a.size, bytes_accessed=6 * a.size, transcendentals=2 * a.size
        ),
    )(a, b)


def project_kernel(shards, holders, place_ref, cos_ref, sin_ref, gain_ref, *refs):
    own_ref = refs[0]
    right = refs[1:shards]
    left = refs[shards : 2 * shards - 1]
    weights = refs[2 * shards - 1 : 2 * shards - 1 + 2 * holders]
    out_ref, features, gathered, feature_sem, weight_sem = refs[2 * shards - 1 + 2 * holders :]
    rank, me, group = place_ref[0], place_ref[1], place_ref[2]
    depth = weights[0].shape[0]

    def weight_copies(step):
        owner = me ^ step
        return [
            pltpu.make_async_copy(
                weights[2 * step + kind],
                gathered.at[kind, pl.ds(owner * depth, depth)],
                weight_sem.at[kind, step],
            )
            for kind in range(2)
        ]

    copies = [copy for step in range(holders) for copy in weight_copies(step)]
    for copy in copies:
        copy.start()
    pltpu.make_async_copy(own_ref, features.at[rank], feature_sem.at[0]).start()
    for step in range(1, shards):

        @pl.when(rank >= step)
        def _(step=step):
            pltpu.make_async_copy(
                right[step - 1], features.at[rank - step], feature_sem.at[step]
            ).start()

        @pl.when(rank < step)
        def _(step=step):
            pltpu.make_async_copy(
                left[shards - step - 1], features.at[rank + shards - step], feature_sem.at[step]
            ).start()

    for step in range(shards):
        pltpu.make_async_copy(own_ref, features.at[rank], feature_sem.at[step]).wait()
    for copy in copies:
        copy.wait()
    span = features.shape[2]
    raw = [
        sum(
            plain_dot(features[shard], gathered[kind, pl.ds(shard * span, span)])
            for shard in range(shards)
        )
        for kind in range(2)
    ]
    first = group == 0
    raw_keys = jnp.where(first, raw[0], raw[1])
    raw_values = jnp.where(first, raw[1], raw[0])
    columns = []
    for head in range(raw_keys.shape[1] // HD):
        one = raw_keys[:, head * HD : (head + 1) * HD]
        mean = jnp.sum(one * one, axis=1, keepdims=True) * (1.0 / HD)
        one = one * lax.rsqrt(mean + 1e-06) * gain_ref[...]
        columns.append(one * cos_ref[...] + pltpu.roll(one, HD // 2, 1) * sin_ref[...])
    new_keys = jnp.concatenate(columns, axis=1) if len(columns) > 1 else columns[0]
    out_ref[0] = new_keys.astype(jnp.bfloat16)
    out_ref[1] = raw_values.astype(jnp.bfloat16)


def project(place, cos, sin, gain, own, right, left, weights):
    shards, holders = len(right) + 1, len(weights) // 2
    new_count, span = own.shape
    depth, width = weights[0].shape
    vmem = pl.BlockSpec(memory_space=pltpu.VMEM)
    total = shards * span
    return pl.pallas_call(
        functools.partial(project_kernel, shards, holders),
        out_shape=jax.ShapeDtypeStruct((2, new_count, width), jnp.bfloat16),
        in_specs=[SMEM, vmem, vmem, vmem] + [ANY] * (2 * shards - 1 + 2 * holders),
        out_specs=vmem,
        scratch_shapes=[
            pltpu.VMEM((shards, new_count, span), jnp.bfloat16),
            pltpu.VMEM((2, holders * depth, width), jnp.bfloat16),
            pltpu.SemaphoreType.DMA((shards,)),
            pltpu.SemaphoreType.DMA((2, holders)),
        ],
        compiler_params=pltpu.CompilerParams(vmem_limit_bytes=VMEM_LIMIT),
        cost_estimate=pl.CostEstimate(
            flops=4 * new_count * total * width,
            bytes_accessed=2 * total * (new_count + 2 * width),
            transcendentals=0,
        ),
    )(place, cos, sin, gain, own, *right, *left, *weights)


def final_kernel(kv_local, parts, q_ref, fresh_ref, *refs):
    out_ref = refs[-1]
    new_count = q_ref.shape[0]
    row = lax.broadcasted_iota(jnp.int32, (new_count, new_count), 0)
    column = lax.broadcasted_iota(jnp.int32, (new_count, new_count), 1)
    causal = column <= row
    for kv_head in range(kv_local):
        span = slice(kv_head * HD, (kv_head + 1) * HD)
        keys, values = fresh_ref[0, :, span], fresh_ref[1, :, span]
        partials = refs[kv_head * parts : (kv_head + 1) * parts]
        for head in range(GROUP):
            columns = pl.ds((kv_head * GROUP + head) * HD, HD)
            here = pl.ds(head * HD, HD)
            scores = jnp.where(causal, row_dot(q_ref[:, columns], keys) * SCALE, EMPTY)
            stats = [joined_stats(partial, head) for partial in partials]
            top = jnp.max(scores, axis=1, keepdims=True)
            for stat in stats:
                top = jnp.maximum(top, stat)
            probabilities = [
                jnp.exp2(scores[:, start : start + HD] - top) for start in range(0, new_count, HD)
            ]
            total = jnp.sum(sum(probabilities), axis=1, keepdims=True)
            weights = jnp.concatenate(probabilities, axis=1).astype(jnp.bfloat16)
            mixed = plain_dot(weights, values)
            for stat, partial in zip(stats, partials):
                share = jnp.exp2(stat - top)
                total = total + share
                mixed = mixed + share * partial[:, here].astype(jnp.float32)
            out_ref[:, columns] = (mixed / total).astype(jnp.bfloat16)


def final(queries, fresh, partials):
    kv_local, parts = len(partials), len(partials[0])
    flat = [array for group in partials for array in group]
    size = queries.size
    return pl.pallas_call(
        functools.partial(final_kernel, kv_local, parts),
        out_shape=jax.ShapeDtypeStruct(queries.shape, queries.dtype),
        compiler_params=pltpu.CompilerParams(vmem_limit_bytes=VMEM_LIMIT),
        cost_estimate=pl.CostEstimate(
            flops=4 * size * queries.shape[0],
            bytes_accessed=2 * size * (parts + 2),
            transcendentals=4 * size,
        ),
    )(queries, fresh, *flat)


def write_kernel(holders, new_pages, base, me_ref, table_ref, *refs):
    pages = refs[:holders]
    out_ref, sem = refs[holders + 1], refs[holders + 2]
    me = me_ref[0]

    def each(action):
        for holder in range(holders):
            for page in range(new_pages):

                @pl.when(table_ref[holder, base + page] == me)
                def _(holder=holder, page=page):
                    slot = table_ref[holder, base + new_pages + page]
                    copy = pltpu.make_async_copy(
                        pages[holder].at[:, pl.ds(page * PAGE, PAGE)],
                        out_ref.at[:, slot],
                        sem.at[holder, page],
                    )
                    getattr(copy, action)()

    each("start")
    each("wait")


def write(me, tables, fresh, pool, new_pages, base):
    holders = len(fresh)
    return pl.pallas_call(
        functools.partial(write_kernel, holders, new_pages, base),
        out_shape=jax.ShapeDtypeStruct(pool.shape, pool.dtype),
        in_specs=[SMEM, SMEM] + [ANY] * (holders + 1),
        out_specs=ANY,
        input_output_aliases={2 + holders: 0},
        scratch_shapes=[pltpu.SemaphoreType.DMA((holders, new_pages))],
        compiler_params=pltpu.CompilerParams(vmem_limit_bytes=VMEM_LIMIT),
        cost_estimate=pl.CostEstimate(flops=0, bytes_accessed=4 * fresh[0].size, transcendentals=0),
    )(me, tables, *fresh, pool)


def per_device(
    hidden,
    k_weight,
    v_weight,
    k_gain,
    queries,
    kv_pool,
    page_holder,
    page_slot,
    page_count,
    write_owner,
    write_slot,
):
    inst_count = lax.axis_size("inst")
    shards = lax.axis_size("tp")
    groups = lax.axis_size("groups")
    me = lax.axis_index("inst").astype(jnp.int32)
    rank = lax.axis_index("tp").astype(jnp.int32)
    group = lax.axis_index("groups").astype(jnp.int32)
    pages_listed = page_holder.shape[1]
    new_pages = write_owner.shape[1]
    capacity = 3 * pages_listed // (2 * inst_count)
    new_count = hidden.shape[0]
    kv_local = k_weight.shape[1] // HD
    me_list = me.reshape(1)

    def swap(array, step):
        return lax.ppermute(array, "inst", [(i, i ^ step) for i in range(inst_count)])

    def shift(array, step):
        pairs = [(i, i + step) for i in range(shards) if 0 <= i + step < shards]
        return lax.ppermute(array, "tp", pairs)

    base = 2 * pages_listed + 1
    own_table = jnp.concatenate(
        [page_holder[0], page_slot[0], page_count, write_owner[0], write_slot[0]]
    )
    own_table = jnp.pad(own_table, (0, 128 - own_table.shape[0]))
    table_rows = jnp.pad(
        own_table.astype(jnp.bfloat16)[None, :], ((0, TABLE_ROWS - 1), (0, BLOCK - 128))
    )

    def table_of(payload):
        return payload[new_count, :128].astype(jnp.int32)

    packed = [
        jnp.concatenate([queries[:, k * BLOCK : (k + 1) * BLOCK], table_rows], axis=0)
        for k in range(kv_local)
    ]
    heads = list(range(kv_local))

    asked = {0: packed, 1: [swap(one, 1) for one in packed]}
    for step in range(2, inst_count, 2):
        asked[step] = [swap(one, step) for one in packed]
        asked[step + 1] = [swap(one, 1) for one in asked[step]]
    tables = {0: own_table}
    for step in range(1, inst_count):
        tables[step] = table_of(asked[step][0])

    right, left = [], []
    to_right = to_left = hidden
    for step in range(1, shards):
        to_right, to_left = shift(to_right, 1), shift(to_left, -1)
        right.append(to_right)
        left.append(to_left)

    first = jnp.where(group == 0, k_weight, v_weight)
    second = jnp.where(group == 0, v_weight, k_weight)
    pieces = {0: (first, second), 1: (swap(first, 1), swap(second, 1))}
    for step in range(2, inst_count, 2):
        carried = swap(first, step)
        if groups == 2:
            other = lax.ppermute(carried, "groups", [(0, 1), (1, 0)])
        else:
            other = swap(second, step)
        pieces[step] = (carried, other)
        pieces[step + 1] = (swap(carried, 1), swap(other, 1))
    weights = [piece for step in range(inst_count) for piece in pieces[step]]

    common = dict(
        pool=kv_pool, pages_listed=pages_listed, capacity=capacity, new_count=new_count
    )
    own_part, pool_copy = attend(
        me_list, own_table[None], [(queries, k * BLOCK) for k in heads], heads, copy_pool=True,
        **common,
    )
    mate_part = attend(me_list, tables[1][None], [(one, 0) for one in asked[1]], heads, **common)
    from_mate = swap(mate_part, 1)
    partials = [[own_part[k], from_mate[k]] for k in heads]
    for step in range(2, inst_count, 2):
        pair = jnp.stack([tables[step + 1], tables[step]])
        for k in heads:
            both = attend(
                me_list, pair, [(asked[step + 1][k], 0), (asked[step][k], 0)], [k], **common
            )
            merged = merge(both[1], swap(both[0], 1))
            partials[k].append(swap(merged, step))

    frequency = 1000000.0 ** (-(jnp.arange(HD // 2, dtype=jnp.float32) * 2.0) / HD)
    positions = page_count[0] * PAGE + jnp.arange(new_count, dtype=jnp.int32)
    angles = positions.astype(jnp.float32)[:, None] * frequency[None, :]
    cosine, sine = jnp.cos(angles), jnp.sin(angles)
    fresh = project(
        jnp.stack([rank, me, group]),
        jnp.concatenate([cosine, cosine], axis=1),
        jnp.concatenate([-sine, sine], axis=1),
        k_gain[None, :],
        hidden,
        right,
        left,
        weights,
    )
    attention_out = final(queries, fresh, partials)
    pages = {0: fresh, 1: swap(fresh, 1)}
    for step in range(2, inst_count, 2):
        pages[step] = swap(fresh, step)
        pages[step + 1] = swap(pages[step], 1)
    new_pool = write(
        me_list,
        jnp.stack([tables[step] for step in range(inst_count)]),
        [pages[step] for step in range(inst_count)],
        pool_copy,
        new_pages,
        base,
    )
    return (attention_out, new_pool)


def solution(mesh):
    return jax.shard_map(
        per_device,
        mesh=mesh,
        in_specs=(
            P(("groups", "inst"), "tp"),
            P("inst", "tp"),
            P("inst", "tp"),
            P(),
            P(("groups", "inst"), "tp"),
            P(None, ("groups", "inst"), None, "tp"),
            P(("groups", "inst"), None),
            P(("groups", "inst"), None),
            P(("groups", "inst")),
            P(("groups", "inst"), None),
            P(("groups", "inst"), None),
        ),
        out_specs=(P(("groups", "inst"), "tp"), P(None, ("groups", "inst"), None, "tp")),
        check_vma=False,
    )
```

```python
import functools
import math

import jax
import jax.numpy as jnp
from jax import lax
from jax.experimental import pallas as pl
from jax.experimental.pallas import tpu as pltpu
from jax.sharding import PartitionSpec as P

HD = 128
PAGE = 128
GROUP = 8
BLOCK = GROUP * HD
EXTRA = 128
TABLE_ROWS = 16
EMPTY = -1e30
LOG2E = 1.4426950408889634
SCALE = LOG2E / math.sqrt(HD)
CHUNK = 4
ANY = pl.BlockSpec(memory_space=pl.ANY)
SMEM = pl.BlockSpec(memory_space=pltpu.SMEM)
VMEM_LIMIT = 56 * 1024 * 1024


def row_dot(a, b):
    return lax.dot_general(a, b, (((1,), (1,)), ((), ())), preferred_element_type=jnp.float32)


def plain_dot(a, b):
    return lax.dot_general(a, b, (((1,), (0,)), ((), ())), preferred_element_type=jnp.float32)


def split_stats(stat, head, lanes):
    high = stat.astype(jnp.bfloat16).astype(jnp.float32)
    rest = stat - high
    middle = rest.astype(jnp.bfloat16).astype(jnp.float32)
    low = rest - middle
    terms = jnp.where(lanes == 3 * head, high, 0.0)
    terms = jnp.where(lanes == 3 * head + 1, middle, terms)
    return jnp.where(lanes == 3 * head + 2, low, terms)


def joined_stats(payload, head):
    term = lax.broadcasted_iota(jnp.int32, (EXTRA, HD), 0)
    picked = jnp.where((term >= 3 * head) & (term < 3 * head + 3), 1.0, 0.0).astype(jnp.bfloat16)
    return plain_dot(payload[:, BLOCK : BLOCK + EXTRA], picked)


def state_stats(extra, head):
    return extra[:, head : head + 1], extra[:, GROUP + head : GROUP + head + 1]


def attend_kernel(plan, refs):
    items, requests, kv_heads, offsets = plan["items"], plan["requests"], plan["kv_heads"], plan["offsets"]
    pages_listed, copy_pool, resume = plan["pages_listed"], plan["copy_pool"], plan["resume"]
    refs = list(refs)
    me_ref, table_ref = refs.pop(0), refs.pop(0)
    q_refs = [refs.pop(0) for _ in range(items)]
    state_ref = refs.pop(0) if resume else None
    pool_ref, out_ref = refs.pop(0), refs.pop(0)
    new_pool_ref = refs.pop(0) if copy_pool else None
    q_buf, kv_buf, acc, maxima, totals, extra, slots, q_sem, kv_sem, out_sem = refs[:10]
    refs = refs[10:]
    send_buf = refs.pop(0) if resume else None
    width = len(kv_heads)
    new_count = q_buf.shape[2]
    rows = GROUP * new_count
    lanes = lax.broadcasted_iota(jnp.int32, (new_count, EXTRA), 1)

    def q_copies(item):
        return [
            pltpu.make_async_copy(
                q_refs[item].at[pl.ds(0, new_count), pl.ds(offsets[item] + head * HD, HD)],
                q_buf.at[item, head],
                q_sem.at[item, head],
            )
            for head in range(GROUP)
        ]

    def page_copies(request, place, slot):
        return [
            pltpu.make_async_copy(
                pool_ref.at[:, slot, :, pl.ds(kv_head * HD, HD)],
                kv_buf.at[request, column, :, place],
                kv_sem.at[request, column, place],
            )
            for column, kv_head in enumerate(kv_heads)
        ]

    def state_copies(item):
        return [
            pltpu.make_async_copy(
                state_ref.at[item, :, pl.ds(head * HD, HD)],
                acc.at[item, head] if head < GROUP else extra.at[item],
                out_sem.at[item, head],
            )
            for head in range(GROUP + 1)
        ]

    def out_copies(item):
        if resume:
            sources = [send_buf.at[item, head] for head in range(GROUP + 1)]
        else:
            sources = [acc.at[item, head] for head in range(GROUP)] + [extra.at[item]]
        return [
            pltpu.make_async_copy(
                sources[head], out_ref.at[item, :, pl.ds(head * HD, HD)], out_sem.at[item, head]
            )
            for head in range(GROUP + 1)
        ]

    for item in range(items):
        for copy in q_copies(item):
            copy.start()
        if resume:
            for copy in state_copies(item):
                copy.start()
    me = me_ref[0]
    for request in range(requests):

        def look(page, found, request=request):
            mine = (page < table_ref[request, 2 * pages_listed]) & (table_ref[request, page] == me)

            @pl.when(mine)
            def _():
                for copy in page_copies(request, found, table_ref[request, pages_listed + page]):
                    copy.start()

            return found + mine.astype(jnp.int32)

        slots[request] = lax.fori_loop(0, pages_listed, look, 0)
    pool_in, pool_out = [], []
    if copy_pool:
        pool_buf, pool_sem = refs
        slot_total = pool_ref.shape[1]
        parts = pool_sem.shape[1]
        step = slot_total // parts
        for index in range(2):
            for part in range(parts):
                piece = (index, pl.ds(part * step, step))
                sem = pool_sem.at[index, part]
                pool_in.append(pltpu.make_async_copy(pool_ref.at[piece], pool_buf.at[piece], sem))
                pool_out.append(
                    pltpu.make_async_copy(pool_buf.at[piece], new_pool_ref.at[piece], sem)
                )
        for copy in pool_in:
            copy.start()
    for item in range(items):
        for copy in q_copies(item):
            copy.wait()
        if resume:
            for copy in state_copies(item):
                copy.wait()

    def one_item(item, carry):
        request = item // width
        column = item % width
        found = slots[request]

        @pl.when(column == 0)
        def _():
            def arrived(place, carry):
                for copy in page_copies(request, place, 0):
                    copy.wait()
                return carry

            lax.fori_loop(0, found, arrived, 0)

        if resume:
            for head in range(GROUP):
                top, total = state_stats(extra[item], head)
                maxima[head] = jnp.broadcast_to(top, (new_count, HD))
                totals[head] = jnp.where(lanes == 0, total, 0.0)
        else:
            acc[item] = jnp.zeros(acc.shape[1:], jnp.float32)
            totals[...] = jnp.zeros(totals.shape, jnp.float32)
            maxima[...] = jnp.full(maxima.shape, EMPTY, jnp.float32)

        def chunk(first, count):
            keys = kv_buf[request, column, 0, pl.ds(first, count)].reshape(count * PAGE, HD)
            values = kv_buf[request, column, 1, pl.ds(first, count)].reshape(count * PAGE, HD)
            scores = row_dot(q_buf[item].reshape(rows, HD), keys)
            old = maxima[...].reshape(rows, HD)
            top = jnp.maximum(old, jnp.max(scores, axis=1, keepdims=True) * SCALE)
            rescale = jnp.exp2(old - top)
            total = totals[...].reshape(rows, HD) * rescale
            pieces = []
            for part in range(count):
                piece = jnp.exp2(scores[:, part * PAGE : (part + 1) * PAGE] * SCALE - top)
                total = total + piece
                pieces.append(piece.astype(jnp.bfloat16))
            weights = jnp.concatenate(pieces, axis=1) if count > 1 else pieces[0]
            shape = (GROUP, new_count, HD)
            maxima[...] = top.reshape(shape)
            totals[...] = total.reshape(shape)
            acc[item] = acc[item] * rescale.reshape(shape) + plain_dot(weights, values).reshape(shape)

        whole = found // CHUNK
        left = found % CHUNK

        def step(index, carry):
            chunk(index * CHUNK, CHUNK)
            return carry

        lax.fori_loop(0, whole, step, 0)
        for count in range(1, CHUNK):

            @pl.when(left == count)
            def _(count=count):
                chunk(whole * CHUNK, count)

        terms = jnp.zeros((new_count, EXTRA), jnp.float32)
        for head in range(GROUP):
            top = maxima[head]
            total = jnp.sum(totals[head], axis=1, keepdims=True)
            if resume:
                some = total > 0.0
                safe = jnp.where(some, total, 1.0)
                send_buf[item, head] = (acc[item, head] * (1.0 / safe)).astype(jnp.bfloat16)
                stat = jnp.where(some, top + jnp.log2(safe), EMPTY)
                terms = terms + split_stats(stat, head, lanes)
            else:
                terms = jnp.where(lanes == head, top, terms)
                terms = jnp.where(lanes == GROUP + head, total, terms)
        if resume:
            send_buf[item, GROUP] = terms.astype(jnp.bfloat16)
        else:
            extra[item] = terms
        for copy in out_copies(item):
            copy.start()
        if copy_pool:

            @pl.when(item == 0)
            def _():
                for copy_in, copy_out in zip(pool_in, pool_out):
                    copy_in.wait()
                    copy_out.start()

        return carry

    lax.fori_loop(0, items, one_item, 0)
    for item in range(items):
        for copy in out_copies(item):
            copy.wait()
    for copy in pool_out:
        copy.wait()


def attend(
    me, tables, q_items, kv_heads, pool, pages_listed, capacity, new_count, state=None, copy_pool=False
):
    requests, width = tables.shape[0], len(kv_heads)
    items = requests * width
    resume = state is not None
    payload = (items, new_count, BLOCK + EXTRA)
    out_shape = [jax.ShapeDtypeStruct(payload, jnp.bfloat16 if resume else jnp.float32)]
    out_specs = [ANY]
    scratch = [
        pltpu.VMEM((items, GROUP, new_count, HD), jnp.bfloat16),
        pltpu.VMEM((requests, width, 2, capacity, PAGE, HD), jnp.bfloat16),
        pltpu.VMEM((items, GROUP, new_count, HD), jnp.float32),
        pltpu.VMEM((GROUP, new_count, HD), jnp.float32),
        pltpu.VMEM((GROUP, new_count, HD), jnp.float32),
        pltpu.VMEM((items, new_count, EXTRA), jnp.float32),
        pltpu.SMEM((requests,), jnp.int32),
        pltpu.SemaphoreType.DMA((items, GROUP)),
        pltpu.SemaphoreType.DMA((requests, width, capacity)),
        pltpu.SemaphoreType.DMA((items, GROUP + 1)),
    ]
    if resume:
        scratch.append(pltpu.VMEM((items, GROUP + 1, new_count, HD), jnp.bfloat16))
    if copy_pool:
        out_shape.append(jax.ShapeDtypeStruct(pool.shape, pool.dtype))
        out_specs.append(ANY)
        parts = next(part for part in (6, 3, 2, 1) if pool.shape[1] % part == 0)
        scratch += [pltpu.VMEM(pool.shape, pool.dtype), pltpu.SemaphoreType.DMA((2, parts))]
    plan = dict(
        items=items, requests=requests, kv_heads=kv_heads, offsets=[offset for _, offset in q_items],
        pages_listed=pages_listed, copy_pool=copy_pool, resume=resume,
    )
    assumed = items * 9 * PAGE * GROUP * new_count
    result = pl.pallas_call(
        lambda *refs: attend_kernel(plan, refs),
        out_shape=out_shape,
        in_specs=[SMEM, SMEM] + [ANY] * (items + 1 + resume),
        out_specs=out_specs,
        scratch_shapes=scratch,
        compiler_params=pltpu.CompilerParams(vmem_limit_bytes=VMEM_LIMIT),
        cost_estimate=pl.CostEstimate(
            flops=8 * assumed * HD, bytes_accessed=items * 4 * 1024 * 1024, transcendentals=assumed
        ),
    )(me, tables, *[array for array, _ in q_items], *([state] if resume else []), pool)
    return result if copy_pool else result[0]


def project_kernel(shards, holders, place_ref, cos_ref, sin_ref, gain_ref, *refs):
    own_ref = refs[0]
    right = refs[1:shards]
    left = refs[shards : 2 * shards - 1]
    weights = refs[2 * shards - 1 : 2 * shards - 1 + 2 * holders]
    out_ref, features, gathered, feature_sem, weight_sem = refs[2 * shards - 1 + 2 * holders :]
    rank, me, group = place_ref[0], place_ref[1], place_ref[2]
    depth = weights[0].shape[0]

    def weight_copies(step):
        owner = me ^ step
        return [
            pltpu.make_async_copy(
                weights[2 * step + kind],
                gathered.at[kind, pl.ds(owner * depth, depth)],
                weight_sem.at[kind, step],
            )
            for kind in range(2)
        ]

    copies = [copy for step in range(holders) for copy in weight_copies(step)]
    for copy in copies:
        copy.start()
    pltpu.make_async_copy(own_ref, features.at[rank], feature_sem.at[0]).start()
    for step in range(1, shards):

        @pl.when(rank >= step)
        def _(step=step):
            pltpu.make_async_copy(
                right[step - 1], features.at[rank - step], feature_sem.at[step]
            ).start()

        @pl.when(rank < step)
        def _(step=step):
            pltpu.make_async_copy(
                left[shards - step - 1], features.at[rank + shards - step], feature_sem.at[step]
            ).start()

    for step in range(shards):
        pltpu.make_async_copy(own_ref, features.at[rank], feature_sem.at[step]).wait()
    for copy in copies:
        copy.wait()
    span = features.shape[2]
    raw = [
        sum(
            plain_dot(features[shard], gathered[kind, pl.ds(shard * span, span)])
            for shard in range(shards)
        )
        for kind in range(2)
    ]
    first = group == 0
    raw_keys = jnp.where(first, raw[0], raw[1])
    raw_values = jnp.where(first, raw[1], raw[0])
    columns = []
    for head in range(raw_keys.shape[1] // HD):
        one = raw_keys[:, head * HD : (head + 1) * HD]
        mean = jnp.sum(one * one, axis=1, keepdims=True) * (1.0 / HD)
        one = one * lax.rsqrt(mean + 1e-06) * gain_ref[...]
        columns.append(one * cos_ref[...] + pltpu.roll(one, HD // 2, 1) * sin_ref[...])
    new_keys = jnp.concatenate(columns, axis=1) if len(columns) > 1 else columns[0]
    out_ref[0] = new_keys.astype(jnp.bfloat16)
    out_ref[1] = raw_values.astype(jnp.bfloat16)


def project(place, cos, sin, gain, own, right, left, weights):
    shards, holders = len(right) + 1, len(weights) // 2
    new_count, span = own.shape
    depth, width = weights[0].shape
    vmem = pl.BlockSpec(memory_space=pltpu.VMEM)
    total = shards * span
    return pl.pallas_call(
        functools.partial(project_kernel, shards, holders),
        out_shape=jax.ShapeDtypeStruct((2, new_count, width), jnp.bfloat16),
        in_specs=[SMEM, vmem, vmem, vmem] + [ANY] * (2 * shards - 1 + 2 * holders),
        out_specs=vmem,
        scratch_shapes=[
            pltpu.VMEM((shards, new_count, span), jnp.bfloat16),
            pltpu.VMEM((2, holders * depth, width), jnp.bfloat16),
            pltpu.SemaphoreType.DMA((shards,)),
            pltpu.SemaphoreType.DMA((2, holders)),
        ],
        compiler_params=pltpu.CompilerParams(vmem_limit_bytes=VMEM_LIMIT),
        cost_estimate=pl.CostEstimate(
            flops=4 * new_count * total * width,
            bytes_accessed=2 * total * (new_count + 2 * width),
            transcendentals=0,
        ),
    )(place, cos, sin, gain, own, *right, *left, *weights)


def fresh_kernel(q_ref, fresh_ref, own_ref, mate_ref, out_ref):
    new_count = q_ref.shape[0]
    rows = GROUP * new_count
    row = lax.broadcasted_iota(jnp.int32, (new_count, new_count), 0)
    column = lax.broadcasted_iota(jnp.int32, (new_count, new_count), 1)
    lanes = lax.broadcasted_iota(jnp.int32, (new_count, EXTRA), 1)
    heads = [slice(head * HD, (head + 1) * HD) for head in range(GROUP)]
    stacked = jnp.concatenate([q_ref[:, span] for span in heads], axis=0)
    scores = row_dot(stacked, fresh_ref[0]).reshape(GROUP, new_count, new_count)
    scores = jnp.where((column <= row)[None], scores * SCALE, EMPTY)
    extras = [ref[0, :, BLOCK:] for ref in (own_ref, mate_ref)]
    terms = jnp.zeros((new_count, EXTRA), jnp.float32)
    weights, shares = [], []
    for head in range(GROUP):
        stats = [state_stats(extra, head) for extra in extras]
        top = jnp.max(scores[head], axis=1, keepdims=True)
        for other, _ in stats:
            top = jnp.maximum(top, other)
        probabilities = jnp.exp2(scores[head] - top)
        total = jnp.sum(probabilities, axis=1, keepdims=True)
        shares.append([jnp.exp2(other - top) for other, _ in stats])
        for share, (_, part) in zip(shares[-1], stats):
            total = total + share * part
        terms = jnp.where(lanes == head, top, terms)
        terms = jnp.where(lanes == GROUP + head, total, terms)
        weights.append(probabilities.astype(jnp.bfloat16))
    sums = plain_dot(jnp.concatenate(weights, axis=0), fresh_ref[1]).reshape(GROUP, new_count, HD)
    for head, span in enumerate(heads):
        out_ref[0, :, span] = (
            sums[head] + shares[head][0] * own_ref[0, :, span] + shares[head][1] * mate_ref[0, :, span]
        )
    out_ref[0, :, BLOCK:] = terms


def attend_fresh(queries, fresh, own, mate):
    kv_local, new_count = own.shape[0], queries.shape[0]
    state = pl.BlockSpec((1, new_count, BLOCK + EXTRA), lambda k: (k, 0, 0))
    return pl.pallas_call(
        fresh_kernel,
        grid=(kv_local,),
        out_shape=jax.ShapeDtypeStruct(own.shape, jnp.float32),
        in_specs=[
            pl.BlockSpec((new_count, BLOCK), lambda k: (0, k)),
            pl.BlockSpec((2, new_count, HD), lambda k: (0, 0, k)),
            state,
            state,
        ],
        out_specs=state,
        compiler_params=pltpu.CompilerParams(vmem_limit_bytes=VMEM_LIMIT),
        cost_estimate=pl.CostEstimate(
            flops=4 * queries.size * new_count,
            bytes_accessed=12 * own.size,
            transcendentals=queries.size * 2,
        ),
    )(queries, fresh, own, mate)


def final_kernel(parts, *refs):
    state_ref, partials, out_ref = refs[0], refs[1 : 1 + parts], refs[-1]
    extra = state_ref[0, :, BLOCK:]
    for head in range(GROUP):
        span = slice(head * HD, (head + 1) * HD)
        top, total = state_stats(extra, head)
        stats = [joined_stats(partial.at[0], head) for partial in partials]
        best = top
        for stat in stats:
            best = jnp.maximum(best, stat)
        share = jnp.exp2(top - best)
        mixed, total = share * state_ref[0, :, span], share * total
        for stat, partial in zip(stats, partials):
            share = jnp.exp2(stat - best)
            total = total + share
            mixed = mixed + share * partial[0, :, span].astype(jnp.float32)
        out_ref[:, span] = (mixed / total).astype(jnp.bfloat16)


def final(shape, kv_head, states, partials, before):
    new_count = states.shape[1]
    whole = pl.BlockSpec((1, new_count, BLOCK + EXTRA), lambda step: (0, 0, 0))
    given = [] if before is None else [before]
    return pl.pallas_call(
        functools.partial(final_kernel, len(partials)),
        grid=(1,),
        out_shape=jax.ShapeDtypeStruct(shape, jnp.bfloat16),
        in_specs=[pl.BlockSpec((1, new_count, BLOCK + EXTRA), lambda step: (kv_head, 0, 0))]
        + [whole] * len(partials)
        + [ANY] * len(given),
        out_specs=pl.BlockSpec((new_count, BLOCK), lambda step: (0, kv_head)),
        input_output_aliases={1 + len(partials): 0} if given else {},
        compiler_params=pltpu.CompilerParams(vmem_limit_bytes=VMEM_LIMIT),
        cost_estimate=pl.CostEstimate(
            flops=16 * new_count * BLOCK,
            bytes_accessed=8 * new_count * BLOCK,
            transcendentals=2 * new_count * BLOCK,
        ),
    )(states, *partials, *given)


def write_kernel(holders, new_pages, base, me_ref, table_ref, *refs):
    pages = refs[:holders]
    out_ref, sem = refs[holders + 1], refs[holders + 2]
    me = me_ref[0]

    def each(action):
        for holder in range(holders):
            for page in range(new_pages):

                @pl.when(table_ref[holder, base + page] == me)
                def _(holder=holder, page=page):
                    slot = table_ref[holder, base + new_pages + page]
                    copy = pltpu.make_async_copy(
                        pages[holder].at[:, pl.ds(page * PAGE, PAGE)],
                        out_ref.at[:, slot],
                        sem.at[holder, page],
                    )
                    getattr(copy, action)()

    each("start")
    each("wait")


def write(me, tables, fresh, pool, new_pages, base):
    holders = len(fresh)
    return pl.pallas_call(
        functools.partial(write_kernel, holders, new_pages, base),
        out_shape=jax.ShapeDtypeStruct(pool.shape, pool.dtype),
        in_specs=[SMEM, SMEM]
        + [pl.BlockSpec(memory_space=pltpu.VMEM)] * holders
        + [ANY],
        out_specs=ANY,
        input_output_aliases={2 + holders: 0},
        scratch_shapes=[pltpu.SemaphoreType.DMA((holders, new_pages))],
        compiler_params=pltpu.CompilerParams(vmem_limit_bytes=VMEM_LIMIT),
        cost_estimate=pl.CostEstimate(flops=0, bytes_accessed=4 * fresh[0].size, transcendentals=0),
    )(me, tables, *fresh, pool)


def per_device(
    hidden,
    k_weight,
    v_weight,
    k_gain,
    queries,
    kv_pool,
    page_holder,
    page_slot,
    page_count,
    write_owner,
    write_slot,
):
    inst_count = lax.axis_size("inst")
    shards = lax.axis_size("tp")
    groups = lax.axis_size("groups")
    me = lax.axis_index("inst").astype(jnp.int32)
    rank = lax.axis_index("tp").astype(jnp.int32)
    group = lax.axis_index("groups").astype(jnp.int32)
    pages_listed = page_holder.shape[1]
    new_pages = write_owner.shape[1]
    capacity = 3 * pages_listed // (2 * inst_count)
    new_count = hidden.shape[0]
    kv_local = k_weight.shape[1] // HD
    me_list = me.reshape(1)

    def swap(array, step):
        return lax.ppermute(array, "inst", [(i, i ^ step) for i in range(inst_count)])

    def shift(array, step):
        pairs = [(i, i + step) for i in range(shards) if 0 <= i + step < shards]
        return lax.ppermute(array, "tp", pairs)

    base = 2 * pages_listed + 1
    own_table = jnp.concatenate(
        [page_holder[0], page_slot[0], page_count, write_owner[0], write_slot[0]]
    )
    own_table = jnp.pad(own_table, (0, 128 - own_table.shape[0]))
    table_rows = jnp.pad(
        own_table.astype(jnp.bfloat16)[None, :], ((0, TABLE_ROWS - 1), (0, BLOCK - 128))
    )

    def table_of(payload):
        return payload[new_count, :128].astype(jnp.int32)

    packed = [
        jnp.concatenate([queries[:, k * BLOCK : (k + 1) * BLOCK], table_rows], axis=0)
        for k in range(kv_local)
    ]
    heads = list(range(kv_local))

    asked = {0: packed, 1: [swap(one, 1) for one in packed]}
    for step in range(2, inst_count, 2):
        asked[step] = [swap(one, step) for one in packed]
        asked[step + 1] = [swap(one, 1) for one in asked[step]]
    tables = {0: own_table}
    for step in range(1, inst_count):
        tables[step] = table_of(asked[step][0])

    right, left = [], []
    to_right = to_left = hidden
    for step in range(1, shards):
        to_right, to_left = shift(to_right, 1), shift(to_left, -1)
        right.append(to_right)
        left.append(to_left)

    first = jnp.where(group == 0, k_weight, v_weight)
    second = jnp.where(group == 0, v_weight, k_weight)
    pieces = {0: (first, second), 1: (swap(first, 1), swap(second, 1))}
    for step in range(2, inst_count, 2):
        carried = swap(first, step)
        if groups == 2:
            other = lax.ppermute(carried, "groups", [(0, 1), (1, 0)])
        else:
            other = swap(second, step)
        pieces[step] = (carried, other)
        pieces[step + 1] = (swap(carried, 1), swap(other, 1))
    weights = [piece for step in range(inst_count) for piece in pieces[step]]

    common = dict(
        pool=kv_pool, pages_listed=pages_listed, capacity=capacity, new_count=new_count
    )
    own_state, pool_copy = attend(
        me_list, own_table[None], [(queries, k * BLOCK) for k in heads], heads, copy_pool=True,
        **common,
    )
    mate_state = attend(me_list, tables[1][None], [(one, 0) for one in asked[1]], heads, **common)
    from_mate = swap(mate_state, 1)
    partials = [[] for k in heads]
    for step in range(2, inst_count, 2):
        for k in heads:
            begun = attend(me_list, tables[step + 1][None], [(asked[step + 1][k], 0)], [k], **common)
            ended = attend(
                me_list, tables[step][None], [(asked[step][k], 0)], [k], state=swap(begun, 1), **common
            )
            partials[k].append(swap(ended, step))

    frequency = 1000000.0 ** (-(jnp.arange(HD // 2, dtype=jnp.float32) * 2.0) / HD)
    positions = page_count[0] * PAGE + jnp.arange(new_count, dtype=jnp.int32)
    angles = positions.astype(jnp.float32)[:, None] * frequency[None, :]
    cosine, sine = jnp.cos(angles), jnp.sin(angles)
    fresh = project(
        jnp.stack([rank, me, group]),
        jnp.concatenate([cosine, cosine], axis=1),
        jnp.concatenate([-sine, sine], axis=1),
        k_gain[None, :],
        hidden,
        right,
        left,
        weights,
    )
    states = attend_fresh(queries, fresh, own_state, from_mate)
    attention_out = None
    for k in heads:
        attention_out = final(queries.shape, k, states, partials[k], attention_out)
    pages = {0: fresh, 1: swap(fresh, 1)}
    for step in range(2, inst_count, 2):
        pages[step] = swap(fresh, step)
        pages[step + 1] = swap(pages[step], 1)
    new_pool = write(
        me_list,
        jnp.stack([tables[step] for step in range(inst_count)]),
        [pages[step] for step in range(inst_count)],
        pool_copy,
        new_pages,
        base,
    )
    return (attention_out, new_pool)


def solution(mesh):
    return jax.shard_map(
        per_device,
        mesh=mesh,
        in_specs=(
            P(("groups", "inst"), "tp"),
            P("inst", "tp"),
            P("inst", "tp"),
            P(),
            P(("groups", "inst"), "tp"),
            P(None, ("groups", "inst"), None, "tp"),
            P(("groups", "inst"), None),
            P(("groups", "inst"), None),
            P(("groups", "inst")),
            P(("groups", "inst"), None),
            P(("groups", "inst"), None),
        ),
        out_specs=(P(("groups", "inst"), "tp"), P(None, ("groups", "inst"), None, "tp")),
        check_vma=False,
    )
```

```python
import functools
import math

import jax
import jax.numpy as jnp
from jax import lax
from jax.experimental import pallas as pl
from jax.experimental.pallas import tpu as pltpu
from jax.sharding import PartitionSpec as P

HD = 128
PAGE = 128
GROUP = 8
BLOCK = GROUP * HD
EXTRA = 128
TABLE_ROWS = 16
EMPTY = -1e30
LOG2E = 1.4426950408889634
SCALE = LOG2E / math.sqrt(HD)
CHUNK = 4
ANY = pl.BlockSpec(memory_space=pl.ANY)
SMEM = pl.BlockSpec(memory_space=pltpu.SMEM)
VMEM_LIMIT = 56 * 1024 * 1024
SMALL = pl.CostEstimate(flops=0, bytes_accessed=4096, transcendentals=0)


def row_dot(a, b):
    return lax.dot_general(a, b, (((1,), (1,)), ((), ())), preferred_element_type=jnp.float32)


def plain_dot(a, b):
    return lax.dot_general(a, b, (((1,), (0,)), ((), ())), preferred_element_type=jnp.float32)


def split_stats(stat, head, lanes):
    high = stat.astype(jnp.bfloat16).astype(jnp.float32)
    rest = stat - high
    middle = rest.astype(jnp.bfloat16).astype(jnp.float32)
    low = rest - middle
    terms = jnp.where(lanes == 3 * head, high, 0.0)
    terms = jnp.where(lanes == 3 * head + 1, middle, terms)
    return jnp.where(lanes == 3 * head + 2, low, terms)


def joined_stats(payload, head):
    term = lax.broadcasted_iota(jnp.int32, (EXTRA, HD), 0)
    picked = jnp.where((term >= 3 * head) & (term < 3 * head + 3), 1.0, 0.0).astype(jnp.bfloat16)
    return plain_dot(payload[:, BLOCK : BLOCK + EXTRA], picked)


def state_stats(extra, head):
    return [
        jnp.broadcast_to(extra[:, lane : lane + 1], extra.shape) for lane in (head, GROUP + head)
    ]


def attend_kernel(plan, refs):
    items, requests, kv_heads, offsets = plan["items"], plan["requests"], plan["kv_heads"], plan["offsets"]
    pages_listed, copy_pool = plan["pages_listed"], plan["copy_pool"]
    refs = list(refs)
    me_ref, table_ref = refs.pop(0), refs.pop(0)
    q_refs = [refs.pop(0) for _ in range(requests)]
    pool_ref, out_ref = refs.pop(0), refs.pop(0)
    new_pool_ref = refs.pop(0) if copy_pool else None
    q_buf, kv_buf, acc, maxima, totals, extra, slots, q_sem, kv_sem, out_sem = refs[:10]
    width = len(kv_heads)
    new_count = q_buf.shape[2]
    rows = GROUP * new_count
    shape = (GROUP, new_count, HD)
    lanes = lax.broadcasted_iota(jnp.int32, (new_count, EXTRA), 1)

    def q_copies(item):
        return [
            pltpu.make_async_copy(
                q_refs[item // width].at[:, pl.ds(offsets[item] + head * HD, HD)],
                q_buf.at[item, head],
                q_sem.at[item, head],
            )
            for head in range(GROUP)
        ]

    def page_copies(request, place, slot):
        return [
            pltpu.make_async_copy(
                pool_ref.at[:, slot, :, pl.ds(kv_head * HD, HD)],
                kv_buf.at[request, column, :, place],
                kv_sem.at[request, column, place],
            )
            for column, kv_head in enumerate(kv_heads)
        ]

    def out_copies(item):
        return [
            pltpu.make_async_copy(
                acc.at[item, head] if head < GROUP else extra.at[item],
                out_ref.at[item, :, pl.ds(head * HD, HD)],
                out_sem.at[item, head],
            )
            for head in range(GROUP + 1)
        ]

    for item in range(items):
        for copy in q_copies(item):
            copy.start()
    me = me_ref[0]
    for request in range(requests):
        count = table_ref[request, 2 * pages_listed]

        def look(page, found, request=request, count=count):
            mine = (page < count) & (table_ref[request, page] == me)

            @pl.when(mine)
            def _():
                for copy in page_copies(request, found, table_ref[request, pages_listed + page]):
                    copy.start()

            return found + mine.astype(jnp.int32)

        slots[request] = lax.fori_loop(0, count, look, 0)
    pool_in, pool_out = [], []
    if copy_pool:
        pool_buf, pool_sem = refs[10:]
        slot_total = pool_ref.shape[1]
        parts = pool_sem.shape[1]
        step = slot_total // parts
        for index in range(2):
            for part in range(parts):
                piece = (index, pl.ds(part * step, step))
                sem = pool_sem.at[index, part]
                pool_in.append(pltpu.make_async_copy(pool_ref.at[piece], pool_buf.at[piece], sem))
                pool_out.append(
                    pltpu.make_async_copy(pool_buf.at[piece], new_pool_ref.at[piece], sem)
                )
        for copy in pool_in:
            copy.start()

    def one_item(item, carry):
        request = item // width
        column = item % width
        found = slots[request]
        acc[item] = jnp.zeros(shape, jnp.float32)
        totals[...] = jnp.zeros(shape, jnp.float32)
        maxima[...] = jnp.full(shape, EMPTY, jnp.float32)

        @pl.when(item == 0)
        def _():
            for each in range(items):
                for copy in q_copies(each):
                    copy.wait()

        @pl.when(column == 0)
        def _():
            def arrived(place, carry):
                for copy in page_copies(request, place, 0):
                    copy.wait()
                return carry

            lax.fori_loop(0, found, arrived, 0)

        def chunk(first, count):
            keys = kv_buf[request, column, 0, pl.ds(first, count)].reshape(count * PAGE, HD)
            values = kv_buf[request, column, 1, pl.ds(first, count)].reshape(count * PAGE, HD)
            scores = row_dot(q_buf[item].reshape(rows, HD), keys)
            old = maxima[...].reshape(rows, HD)
            top = jnp.maximum(old, jnp.max(scores, axis=1, keepdims=True) * SCALE)
            rescale = jnp.exp2(old - top)
            total = totals[...].reshape(rows, HD) * rescale
            pieces = []
            for part in range(count):
                piece = jnp.exp2(scores[:, part * PAGE : (part + 1) * PAGE] * SCALE - top)
                total = total + piece
                pieces.append(piece.astype(jnp.bfloat16))
            weights = jnp.concatenate(pieces, axis=1) if count > 1 else pieces[0]
            maxima[...] = top.reshape(shape)
            totals[...] = total.reshape(shape)
            acc[item] = acc[item] * rescale.reshape(shape) + plain_dot(weights, values).reshape(shape)

        whole = found // CHUNK
        left = found % CHUNK

        def step(index, carry):
            chunk(index * CHUNK, CHUNK)
            return carry

        lax.fori_loop(0, whole, step, 0)
        for count in range(1, CHUNK):

            @pl.when(left == count)
            def _(count=count):
                chunk(whole * CHUNK, count)

        copies = out_copies(item)
        for copy in copies[:GROUP]:
            copy.start()
        terms = jnp.zeros((new_count, EXTRA), jnp.float32)
        for head in range(GROUP):
            total = jnp.sum(totals[head], axis=1, keepdims=True)
            terms = jnp.where(lanes == head, maxima[head], terms)
            terms = jnp.where(lanes == GROUP + head, total, terms)
        extra[item] = terms
        copies[GROUP].start()
        if copy_pool:

            @pl.when(item == 0)
            def _():
                for copy_in, copy_out in zip(pool_in, pool_out):
                    copy_in.wait()
                    copy_out.start()

        return carry

    lax.fori_loop(0, items, one_item, 0)
    for item in range(items):
        for copy in out_copies(item):
            copy.wait()
    for copy in pool_out:
        copy.wait()


def attend(me, tables, asked, kv_heads, pool, pages_listed, capacity, copy_pool=False):
    requests, width, new_count = tables.shape[0], len(kv_heads), asked[0].shape[0]
    items = requests * width
    out_shape = [jax.ShapeDtypeStruct((items, new_count, BLOCK + EXTRA), jnp.float32)]
    out_specs = [ANY]
    scratch = [
        pltpu.VMEM((items, GROUP, new_count, HD), jnp.bfloat16),
        pltpu.VMEM((requests, width, 2, capacity, PAGE, HD), jnp.bfloat16),
        pltpu.VMEM((items, GROUP, new_count, HD), jnp.float32),
        pltpu.VMEM((GROUP, new_count, HD), jnp.float32),
        pltpu.VMEM((GROUP, new_count, HD), jnp.float32),
        pltpu.VMEM((items, new_count, EXTRA), jnp.float32),
        pltpu.SMEM((requests,), jnp.int32),
        pltpu.SemaphoreType.DMA((items, GROUP)),
        pltpu.SemaphoreType.DMA((requests, width, capacity)),
        pltpu.SemaphoreType.DMA((items, GROUP + 1)),
    ]
    if copy_pool:
        out_shape.append(jax.ShapeDtypeStruct(pool.shape, pool.dtype))
        out_specs.append(ANY)
        parts = next(part for part in (6, 3, 2, 1) if pool.shape[1] % part == 0)
        scratch += [pltpu.VMEM(pool.shape, pool.dtype), pltpu.SemaphoreType.DMA((2, parts))]
    plan = dict(
        items=items, requests=requests, kv_heads=kv_heads,
        offsets=[kv_head * BLOCK for kv_head in kv_heads] * requests,
        pages_listed=pages_listed, copy_pool=copy_pool,
    )
    result = pl.pallas_call(
        lambda *refs: attend_kernel(plan, refs),
        out_shape=out_shape,
        in_specs=[SMEM, SMEM] + [ANY] * (requests + 1),
        out_specs=out_specs,
        scratch_shapes=scratch,
        compiler_params=pltpu.CompilerParams(vmem_limit_bytes=VMEM_LIMIT),
        cost_estimate=SMALL,
    )(me, tables, *asked, pool)
    return result if copy_pool else result[0]


def merge_kernel(a_ref, b_ref, out_ref):
    new_count = a_ref.shape[1]
    lanes = lax.broadcasted_iota(jnp.int32, (new_count, EXTRA), 1)
    extra_a, extra_b = a_ref[0, :, BLOCK:], b_ref[0, :, BLOCK:]
    terms = jnp.zeros((new_count, EXTRA), jnp.float32)
    for head in range(GROUP):
        span = slice(head * HD, (head + 1) * HD)
        top_a, total_a = state_stats(extra_a, head)
        top_b, total_b = state_stats(extra_b, head)
        top = jnp.maximum(top_a, top_b)
        share_a, share_b = jnp.exp2(top_a - top), jnp.exp2(top_b - top)
        total = share_a * total_a + share_b * total_b
        some = total > 0.0
        safe = jnp.where(some, total, 1.0)
        mixed = (share_a * a_ref[0, :, span] + share_b * b_ref[0, :, span]) / safe
        out_ref[:, span] = mixed.astype(jnp.bfloat16)
        terms = terms + split_stats(jnp.where(some, top + jnp.log2(safe), EMPTY), head, lanes)
    out_ref[:, BLOCK:] = terms.astype(jnp.bfloat16)


def merge(a, b, kv_head):
    shape = (a.shape[1], BLOCK + EXTRA)
    spec = pl.BlockSpec((1,) + shape, lambda step: (kv_head, 0, 0))
    return pl.pallas_call(
        merge_kernel,
        grid=(1,),
        out_shape=jax.ShapeDtypeStruct(shape, jnp.bfloat16),
        in_specs=[spec if a.shape[0] > 1 else pl.BlockSpec((1,) + shape, lambda step: (0, 0, 0)),
                  spec if b.shape[0] > 1 else pl.BlockSpec((1,) + shape, lambda step: (0, 0, 0))],
        out_specs=pl.BlockSpec(shape, lambda step: (0, 0)),
        compiler_params=pltpu.CompilerParams(vmem_limit_bytes=VMEM_LIMIT),
        cost_estimate=SMALL,
    )(a, b)


def project_kernel(shards, holders, place_ref, cos_ref, sin_ref, gain_ref, *refs):
    own_ref = refs[0]
    right = refs[1:shards]
    left = refs[shards : 2 * shards - 1]
    weights = refs[2 * shards - 1 : 2 * shards - 1 + 2 * holders]
    out_ref, features, gathered, feature_sem, weight_sem = refs[2 * shards - 1 + 2 * holders :]
    rank, me, group = place_ref[0], place_ref[1], place_ref[2]
    depth = weights[0].shape[0]

    def weight_copies(step):
        owner = me ^ step
        return [
            pltpu.make_async_copy(
                weights[2 * step + kind],
                gathered.at[kind, pl.ds(owner * depth, depth)],
                weight_sem.at[kind, step],
            )
            for kind in range(2)
        ]

    copies = [copy for step in range(holders) for copy in weight_copies(step)]
    for copy in copies:
        copy.start()
    pltpu.make_async_copy(own_ref, features.at[rank], feature_sem.at[0]).start()
    for step in range(1, shards):

        @pl.when(rank >= step)
        def _(step=step):
            pltpu.make_async_copy(
                right[step - 1], features.at[rank - step], feature_sem.at[step]
            ).start()

        @pl.when(rank < step)
        def _(step=step):
            pltpu.make_async_copy(
                left[shards - step - 1], features.at[rank + shards - step], feature_sem.at[step]
            ).start()

    for step in range(shards):
        pltpu.make_async_copy(own_ref, features.at[rank], feature_sem.at[step]).wait()
    for copy in copies:
        copy.wait()
    span = features.shape[2]
    raw = [
        sum(
            plain_dot(features[shard], gathered[kind, pl.ds(shard * span, span)])
            for shard in range(shards)
        )
        for kind in range(2)
    ]
    first = group == 0
    raw_keys = jnp.where(first, raw[0], raw[1])
    raw_values = jnp.where(first, raw[1], raw[0])
    columns = []
    for head in range(raw_keys.shape[1] // HD):
        one = raw_keys[:, head * HD : (head + 1) * HD]
        mean = jnp.sum(one * one, axis=1, keepdims=True) * (1.0 / HD)
        one = one * lax.rsqrt(mean + 1e-06) * gain_ref[...]
        columns.append(one * cos_ref[...] + pltpu.roll(one, HD // 2, 1) * sin_ref[...])
    new_keys = jnp.concatenate(columns, axis=1) if len(columns) > 1 else columns[0]
    out_ref[0] = new_keys.astype(jnp.bfloat16)
    out_ref[1] = raw_values.astype(jnp.bfloat16)


def project(place, cos, sin, gain, own, right, left, weights):
    shards, holders = len(right) + 1, len(weights) // 2
    new_count, span = own.shape
    depth, width = weights[0].shape
    vmem = pl.BlockSpec(memory_space=pltpu.VMEM)
    total = shards * span
    return pl.pallas_call(
        functools.partial(project_kernel, shards, holders),
        out_shape=jax.ShapeDtypeStruct((2, new_count, width), jnp.bfloat16),
        in_specs=[SMEM, vmem, vmem, vmem] + [ANY] * (2 * shards - 1 + 2 * holders),
        out_specs=vmem,
        scratch_shapes=[
            pltpu.VMEM((shards, new_count, span), jnp.bfloat16),
            pltpu.VMEM((2, holders * depth, width), jnp.bfloat16),
            pltpu.SemaphoreType.DMA((shards,)),
            pltpu.SemaphoreType.DMA((2, holders)),
        ],
        compiler_params=pltpu.CompilerParams(vmem_limit_bytes=VMEM_LIMIT),
        cost_estimate=SMALL,
    )(place, cos, sin, gain, own, *right, *left, *weights)


def fresh_kernel(q_ref, fresh_ref, own_ref, mate_ref, out_ref):
    new_count = q_ref.shape[0]
    rows = GROUP * new_count
    row = lax.broadcasted_iota(jnp.int32, (new_count, new_count), 0)
    column = lax.broadcasted_iota(jnp.int32, (new_count, new_count), 1)
    lanes = lax.broadcasted_iota(jnp.int32, (new_count, EXTRA), 1)
    heads = [slice(head * HD, (head + 1) * HD) for head in range(GROUP)]
    stacked = jnp.concatenate([q_ref[:, span] for span in heads], axis=0)
    scores = row_dot(stacked, fresh_ref[0]).reshape(GROUP, new_count, new_count)
    scores = jnp.where((column <= row)[None], scores * SCALE, EMPTY)
    extras = [ref[0, :, BLOCK:] for ref in (own_ref, mate_ref)]
    terms = jnp.zeros((new_count, EXTRA), jnp.float32)
    weights, shares = [], []
    for head in range(GROUP):
        stats = [state_stats(extra, head) for extra in extras]
        top = jnp.broadcast_to(jnp.max(scores[head], axis=1, keepdims=True), lanes.shape)
        for other, _ in stats:
            top = jnp.maximum(top, other)
        pieces = [jnp.exp2(scores[head, :, start : start + HD] - top) for start in range(0, new_count, HD)]
        total = jnp.broadcast_to(jnp.sum(sum(pieces), axis=1, keepdims=True), lanes.shape)
        probabilities = jnp.concatenate(pieces, axis=1)
        shares.append([jnp.exp2(other - top) for other, _ in stats])
        for share, (_, part) in zip(shares[-1], stats):
            total = total + share * part
        terms = jnp.where(lanes == head, top, terms)
        terms = jnp.where(lanes == GROUP + head, total, terms)
        weights.append(probabilities.astype(jnp.bfloat16))
    sums = plain_dot(jnp.concatenate(weights, axis=0), fresh_ref[1]).reshape(GROUP, new_count, HD)
    for head, span in enumerate(heads):
        out_ref[0, :, span] = (
            sums[head] + shares[head][0] * own_ref[0, :, span] + shares[head][1] * mate_ref[0, :, span]
        )
    out_ref[0, :, BLOCK:] = terms


def attend_fresh(queries, fresh, own, mate):
    kv_local, new_count = own.shape[0], queries.shape[0]
    state = pl.BlockSpec((1, new_count, BLOCK + EXTRA), lambda k: (k, 0, 0))
    return pl.pallas_call(
        fresh_kernel,
        grid=(kv_local,),
        out_shape=jax.ShapeDtypeStruct(own.shape, jnp.float32),
        in_specs=[
            pl.BlockSpec((new_count, BLOCK), lambda k: (0, k)),
            pl.BlockSpec((2, new_count, HD), lambda k: (0, 0, k)),
            state,
            state,
        ],
        out_specs=state,
        compiler_params=pltpu.CompilerParams(vmem_limit_bytes=VMEM_LIMIT),
        cost_estimate=SMALL,
    )(queries, fresh, own, mate)


def final_kernel(parts, *refs):
    state_ref, partials, out_ref = refs[0], refs[1 : 1 + parts], refs[-1]
    extra = state_ref[0, :, BLOCK:]
    for head in range(GROUP):
        span = slice(head * HD, (head + 1) * HD)
        top, total = state_stats(extra, head)
        stats = [joined_stats(partial, head) for partial in partials]
        best = top
        for stat in stats:
            best = jnp.maximum(best, stat)
        share = jnp.exp2(top - best)
        mixed, total = share * state_ref[0, :, span], share * total
        for stat, partial in zip(stats, partials):
            share = jnp.exp2(stat - best)
            total = total + share
            mixed = mixed + share * partial[:, span].astype(jnp.float32)
        out_ref[:, span] = (mixed / total).astype(jnp.bfloat16)


def final(shape, kv_head, states, partials, before):
    new_count = states.shape[1]
    whole = pl.BlockSpec((new_count, BLOCK + EXTRA), lambda step: (0, 0))
    given = [] if before is None else [before]
    return pl.pallas_call(
        functools.partial(final_kernel, len(partials)),
        grid=(1,),
        out_shape=jax.ShapeDtypeStruct(shape, jnp.bfloat16),
        in_specs=[pl.BlockSpec((1, new_count, BLOCK + EXTRA), lambda step: (kv_head, 0, 0))]
        + [whole] * len(partials)
        + [ANY] * len(given),
        out_specs=pl.BlockSpec((new_count, BLOCK), lambda step: (0, kv_head)),
        input_output_aliases={1 + len(partials): 0} if given else {},
        compiler_params=pltpu.CompilerParams(vmem_limit_bytes=VMEM_LIMIT),
        cost_estimate=SMALL,
    )(states, *partials, *given)


def write_kernel(holders, new_pages, base, me_ref, table_ref, *refs):
    pages = refs[:holders]
    out_ref, sem = refs[holders + 1], refs[holders + 2]
    me = me_ref[0]

    def each(action):
        for holder in range(holders):
            for page in range(new_pages):

                @pl.when(table_ref[holder, base + page] == me)
                def _(holder=holder, page=page):
                    slot = table_ref[holder, base + new_pages + page]
                    copy = pltpu.make_async_copy(
                        pages[holder].at[:, pl.ds(page * PAGE, PAGE)],
                        out_ref.at[:, slot],
                        sem.at[holder, page],
                    )
                    getattr(copy, action)()

    each("start")
    each("wait")


def write(me, tables, fresh, pool, new_pages, base):
    holders = len(fresh)
    return pl.pallas_call(
        functools.partial(write_kernel, holders, new_pages, base),
        out_shape=jax.ShapeDtypeStruct(pool.shape, pool.dtype),
        in_specs=[SMEM, SMEM]
        + [pl.BlockSpec(memory_space=pltpu.VMEM)] * holders
        + [ANY],
        out_specs=ANY,
        input_output_aliases={2 + holders: 0},
        scratch_shapes=[pltpu.SemaphoreType.DMA((holders, new_pages))],
        compiler_params=pltpu.CompilerParams(vmem_limit_bytes=VMEM_LIMIT),
        cost_estimate=SMALL,
    )(me, tables, *fresh, pool)


def per_device(
    hidden,
    k_weight,
    v_weight,
    k_gain,
    queries,
    kv_pool,
    page_holder,
    page_slot,
    page_count,
    write_owner,
    write_slot,
):
    inst_count = lax.axis_size("inst")
    shards = lax.axis_size("tp")
    groups = lax.axis_size("groups")
    me = lax.axis_index("inst").astype(jnp.int32)
    rank = lax.axis_index("tp").astype(jnp.int32)
    group = lax.axis_index("groups").astype(jnp.int32)
    pages_listed = page_holder.shape[1]
    new_pages = write_owner.shape[1]
    capacity = 3 * pages_listed // (2 * inst_count)
    new_count = hidden.shape[0]
    kv_local = k_weight.shape[1] // HD
    me_list = me.reshape(1)

    def swap(array, step):
        return lax.ppermute(array, "inst", [(i, i ^ step) for i in range(inst_count)])

    def shift(array, step):
        pairs = [(i, i + step) for i in range(shards) if 0 <= i + step < shards]
        return lax.ppermute(array, "tp", pairs)

    def after(array, *done):
        return lax.optimization_barrier((array,) + done)[0]

    heads = list(range(kv_local))
    base = 2 * pages_listed + 1
    own_table = jnp.concatenate(
        [page_holder[0], page_slot[0], page_count, write_owner[0], write_slot[0]]
    )
    own_table = jnp.pad(own_table, (0, 128 - own_table.shape[0]))[None]
    others = range(2, inst_count, 2)

    right, left = [shift(hidden, 1)], [shift(hidden, -1)]
    asked = {0: queries, 1: swap(queries, 1)}
    for step in others:
        asked[step] = swap(queries, step)
    tables = {0: own_table}
    for step in range(1, inst_count):
        tables[step] = swap(own_table, step)
    first = jnp.where(group == 0, k_weight, v_weight)
    second = jnp.where(group == 0, v_weight, k_weight)
    pieces = {0: (first, second), 1: (swap(first, 1), swap(second, 1))}

    common = dict(pool=kv_pool, pages_listed=pages_listed, capacity=capacity)
    own_state, pool_copy = attend(me_list, own_table, [queries], heads, copy_pool=True, **common)

    for step in others:
        pieces[step] = [swap(after(first, own_state), step)]
    for hop in range(1, shards - 1):
        if hop == 1:
            to_right, to_left = after(right[-1], own_state), after(left[-1], own_state)
        right.append(shift(to_right, 1))
        left.append(shift(to_left, -1))
        to_right, to_left = right[-1], left[-1]
        if hop == 1:
            mate_state = attend(
                me_list, after(tables[1], own_state), [asked[1]], heads, **common
            )
            to_right, to_left = after(to_right, mate_state), after(to_left, mate_state)

    from_mate = swap(mate_state, 1)
    for step in others:
        asked[step + 1] = swap(after(asked[step], mate_state), 1)
    for step in others:
        carried = after(pieces[step][0], mate_state)
        if groups == 2:
            other = lax.ppermute(carried, "groups", [(0, 1), (1, 0)])
        else:
            other = swap(second, step)
        pieces[step] = (carried, other)
    partials = [[] for k in heads]
    last = mate_state
    for step in others:
        here, there = [], []
        for k in heads:
            here.append(attend(me_list, after(tables[step], last), [asked[step]], [k], **common))
            if k > 0:
                partials[k - 1].append(
                    swap(merge(here[k - 1], after(there[k - 1], here[k]), 0), step)
                )
            begun = attend(
                me_list, after(tables[step + 1], here[k]), [asked[step + 1]], [k], **common
            )
            last = begun
            there.append(swap(begun, 1))
        partials[-1].append(swap(merge(here[-1], there[-1], 0), step))
    for step in others:
        pieces[step + 1] = tuple(swap(after(piece, last), 1) for piece in pieces[step])
    weights = [piece for step in range(inst_count) for piece in pieces[step]]

    frequency = 1000000.0 ** (-(jnp.arange(HD // 2, dtype=jnp.float32) * 2.0) / HD)
    positions = page_count[0] * PAGE + jnp.arange(new_count, dtype=jnp.int32)
    angles = positions.astype(jnp.float32)[:, None] * frequency[None, :]
    cosine, sine = jnp.cos(angles), jnp.sin(angles)
    fresh = project(
        jnp.stack([rank, me, group]),
        jnp.concatenate([cosine, cosine], axis=1),
        jnp.concatenate([-sine, sine], axis=1),
        k_gain[None, :],
        hidden,
        right,
        left,
        weights,
    )
    states = attend_fresh(queries, fresh, own_state, from_mate)
    attention_out = None
    for k in heads:
        attention_out = final(queries.shape, k, states, partials[k], attention_out)
    pages = {0: fresh, 1: swap(fresh, 1)}
    for step in range(2, inst_count, 2):
        pages[step] = swap(fresh, step)
        pages[step + 1] = swap(pages[step], 1)
    new_pool = write(
        me_list,
        jnp.concatenate([tables[step] for step in range(inst_count)]),
        [pages[step] for step in range(inst_count)],
        pool_copy,
        new_pages,
        base,
    )
    return (attention_out, new_pool)


def solution(mesh):
    return jax.shard_map(
        per_device,
        mesh=mesh,
        in_specs=(
            P(("groups", "inst"), "tp"),
            P("inst", "tp"),
            P("inst", "tp"),
            P(),
            P(("groups", "inst"), "tp"),
            P(None, ("groups", "inst"), None, "tp"),
            P(("groups", "inst"), None),
            P(("groups", "inst"), None),
            P(("groups", "inst")),
            P(("groups", "inst"), None),
            P(("groups", "inst"), None),
        ),
        out_specs=(P(("groups", "inst"), "tp"), P(None, ("groups", "inst"), None, "tp")),
        check_vma=False,
    )
```

```python
import functools
import math

import jax
import jax.numpy as jnp
from jax import lax
from jax.experimental import pallas as pl
from jax.experimental.pallas import tpu as pltpu
from jax.sharding import PartitionSpec as P

HD = 128
PAGE = 128
GROUP = 8
BLOCK = GROUP * HD
EXTRA = 128
TOTALS = 64
EMPTY = -1e30
LOG2E = 1.4426950408889634
SCALE = LOG2E / math.sqrt(HD)
CHUNK = 4
ANY = pl.BlockSpec(memory_space=pl.ANY)
SMEM = pl.BlockSpec(memory_space=pltpu.SMEM)
VMEM_LIMIT = 63 * 1024 * 1024


def cost(microseconds):
    return pl.CostEstimate(
        flops=int(microseconds * 1e9), bytes_accessed=int(microseconds * 3e6), transcendentals=0
    )


def row_dot(a, b):
    return lax.dot_general(a, b, (((1,), (1,)), ((), ())), preferred_element_type=jnp.float32)


def plain_dot(a, b):
    return lax.dot_general(a, b, (((1,), (0,)), ((), ())), preferred_element_type=jnp.float32)


def split_stats(stat, lane, lanes, terms):
    high = stat.astype(jnp.bfloat16).astype(jnp.float32)
    rest = stat - high
    middle = rest.astype(jnp.bfloat16).astype(jnp.float32)
    terms = jnp.where(lanes == lane, high, terms)
    terms = jnp.where(lanes == lane + 1, middle, terms)
    return jnp.where(lanes == lane + 2, rest - middle, terms)


def joined_stats(extra, lane):
    term = lax.broadcasted_iota(jnp.int32, (EXTRA, HD), 0)
    picked = jnp.where((term >= lane) & (term < lane + 3), 1.0, 0.0).astype(jnp.bfloat16)
    return plain_dot(extra, picked)


def state_stats(extra, head):
    return joined_stats(extra, 3 * head), joined_stats(extra, TOTALS + 3 * head)


def attend_kernel(plan, refs):
    items, requests, kv_heads, offsets = plan["items"], plan["requests"], plan["kv_heads"], plan["offsets"]
    pages_listed, copy_pool = plan["pages_listed"], plan["copy_pool"]
    refs = list(refs)
    me_ref, table_ref = refs.pop(0), refs.pop(0)
    q_refs = [refs.pop(0) for _ in range(requests)]
    pool_ref, out_ref = refs.pop(0), refs.pop(0)
    new_pool_ref = refs.pop(0) if copy_pool else None
    q_buf, kv_buf, acc, maxima, totals, extra, slots, q_sem, kv_sem, out_sem = refs[:10]
    width = len(kv_heads)
    new_count = q_buf.shape[2]
    rows = GROUP * new_count
    shape = (GROUP, new_count, HD)
    lanes = lax.broadcasted_iota(jnp.int32, (new_count, EXTRA), 1)

    def q_copies(item):
        return [
            pltpu.make_async_copy(
                q_refs[item // width].at[:, pl.ds(offsets[item] + head * HD, HD)],
                q_buf.at[item, head],
                q_sem.at[item, head],
            )
            for head in range(GROUP)
        ]

    def page_copies(request, place, slot):
        return [
            pltpu.make_async_copy(
                pool_ref.at[:, slot, :, pl.ds(kv_head * HD, HD)],
                kv_buf.at[request, column, :, place],
                kv_sem.at[request, column, place],
            )
            for column, kv_head in enumerate(kv_heads)
        ]

    def out_copies(item):
        return [
            pltpu.make_async_copy(
                acc.at[item, head] if head < GROUP else extra.at[item],
                out_ref.at[item, :, pl.ds(head * HD, HD)],
                out_sem.at[item, head],
            )
            for head in range(GROUP + 1)
        ]

    for item in range(items):
        for copy in q_copies(item):
            copy.start()
    me = me_ref[0]
    for request in range(requests):
        count = table_ref[request, 2 * pages_listed]

        def look(page, found, request=request, count=count):
            mine = (page < count) & (table_ref[request, page] == me)

            @pl.when(mine)
            def _():
                for copy in page_copies(request, found, table_ref[request, pages_listed + page]):
                    copy.start()

            return found + mine.astype(jnp.int32)

        slots[request] = lax.fori_loop(0, count, look, 0)
    pool_in, pool_out = [], []
    if copy_pool:
        pool_buf, pool_sem = refs[10:]
        slot_total = pool_ref.shape[1]
        parts = pool_sem.shape[1]
        step = slot_total // parts
        for index in range(2):
            for part in range(parts):
                piece = (index, pl.ds(part * step, step))
                sem = pool_sem.at[index, part]
                pool_in.append(pltpu.make_async_copy(pool_ref.at[piece], pool_buf.at[piece], sem))
                pool_out.append(
                    pltpu.make_async_copy(pool_buf.at[piece], new_pool_ref.at[piece], sem)
                )
        for copy in pool_in:
            copy.start()

    def one_item(item, carry):
        request = item // width
        column = item % width
        found = slots[request]
        acc[item] = jnp.zeros(shape, jnp.float32)
        totals[...] = jnp.zeros(shape, jnp.float32)
        maxima[...] = jnp.full(shape, EMPTY, jnp.float32)

        @pl.when(item == 0)
        def _():
            for each in range(items):
                for copy in q_copies(each):
                    copy.wait()

        @pl.when(column == 0)
        def _():
            def arrived(place, carry):
                for copy in page_copies(request, place, 0):
                    copy.wait()
                return carry

            lax.fori_loop(0, found, arrived, 0)

        def chunk(first, count):
            keys = kv_buf[request, column, 0, pl.ds(first, count)].reshape(count * PAGE, HD)
            values = kv_buf[request, column, 1, pl.ds(first, count)].reshape(count * PAGE, HD)
            scores = row_dot(q_buf[item].reshape(rows, HD), keys)
            old = maxima[...].reshape(rows, HD)
            top = jnp.maximum(old, jnp.max(scores, axis=1, keepdims=True) * SCALE)
            rescale = jnp.exp2(old - top)
            total = totals[...].reshape(rows, HD) * rescale
            pieces = []
            for part in range(count):
                piece = jnp.exp2(scores[:, part * PAGE : (part + 1) * PAGE] * SCALE - top)
                total = total + piece
                pieces.append(piece.astype(jnp.bfloat16))
            weights = jnp.concatenate(pieces, axis=1) if count > 1 else pieces[0]
            maxima[...] = top.reshape(shape)
            totals[...] = total.reshape(shape)
            acc[item] = acc[item] * rescale.reshape(shape) + plain_dot(weights, values).reshape(shape)

        whole = found // CHUNK
        left = found % CHUNK

        def step(index, carry):
            chunk(index * CHUNK, CHUNK)
            return carry

        lax.fori_loop(0, whole, step, 0)
        for count in range(1, CHUNK):

            @pl.when(left == count)
            def _(count=count):
                chunk(whole * CHUNK, count)

        copies = out_copies(item)
        for copy in copies[:GROUP]:
            copy.start()
        terms = jnp.zeros((new_count, EXTRA), jnp.float32)
        for head in range(GROUP):
            total = jnp.sum(totals[head], axis=1, keepdims=True)
            terms = split_stats(maxima[head], 3 * head, lanes, terms)
            terms = split_stats(total, TOTALS + 3 * head, lanes, terms)
        extra[item] = terms
        copies[GROUP].start()
        if copy_pool:

            @pl.when(item == 0)
            def _():
                for copy_in, copy_out in zip(pool_in, pool_out):
                    copy_in.wait()
                    copy_out.start()

        return carry

    lax.fori_loop(0, items, one_item, 0)
    for item in range(items):
        for copy in out_copies(item):
            copy.wait()
    for copy in pool_out:
        copy.wait()


def attend(me, tables, asked, kv_heads, pool, pages_listed, capacity, copy_pool=False):
    requests, width, new_count = tables.shape[0], len(kv_heads), asked[0].shape[0]
    items = requests * width
    out_shape = [jax.ShapeDtypeStruct((items, new_count, BLOCK + EXTRA), jnp.float32)]
    out_specs = [ANY]
    scratch = [
        pltpu.VMEM((items, GROUP, new_count, HD), jnp.bfloat16),
        pltpu.VMEM((requests, width, 2, capacity, PAGE, HD), jnp.bfloat16),
        pltpu.VMEM((items, GROUP, new_count, HD), jnp.float32),
        pltpu.VMEM((GROUP, new_count, HD), jnp.float32),
        pltpu.VMEM((GROUP, new_count, HD), jnp.float32),
        pltpu.VMEM((items, new_count, EXTRA), jnp.float32),
        pltpu.SMEM((requests,), jnp.int32),
        pltpu.SemaphoreType.DMA((items, GROUP)),
        pltpu.SemaphoreType.DMA((requests, width, capacity)),
        pltpu.SemaphoreType.DMA((items, GROUP + 1)),
    ]
    if copy_pool:
        out_shape.append(jax.ShapeDtypeStruct(pool.shape, pool.dtype))
        out_specs.append(ANY)
        parts = next(part for part in (6, 3, 2, 1) if pool.shape[1] % part == 0)
        scratch += [pltpu.VMEM(pool.shape, pool.dtype), pltpu.SemaphoreType.DMA((2, parts))]
    plan = dict(
        items=items, requests=requests, kv_heads=kv_heads,
        offsets=[kv_head * BLOCK for kv_head in kv_heads] * requests,
        pages_listed=pages_listed, copy_pool=copy_pool,
    )
    result = pl.pallas_call(
        lambda *refs: attend_kernel(plan, refs),
        out_shape=out_shape,
        in_specs=[SMEM, SMEM] + [ANY] * (requests + 1),
        out_specs=out_specs,
        scratch_shapes=scratch,
        compiler_params=pltpu.CompilerParams(vmem_limit_bytes=VMEM_LIMIT),
        cost_estimate=cost(1.5 + 5.5 * items),
    )(me, tables, *asked, pool)
    return result if copy_pool else result[0]


def merge_kernel(a_ref, b_ref, out_ref):
    new_count = a_ref.shape[1]
    lanes = lax.broadcasted_iota(jnp.int32, (new_count, EXTRA), 1)
    extra_a, extra_b = [ref[0, :, BLOCK:].astype(jnp.bfloat16) for ref in (a_ref, b_ref)]
    terms = jnp.zeros((new_count, EXTRA), jnp.float32)
    for head in range(GROUP):
        span = slice(head * HD, (head + 1) * HD)
        top_a, total_a = state_stats(extra_a, head)
        top_b, total_b = state_stats(extra_b, head)
        top = jnp.maximum(top_a, top_b)
        share_a, share_b = jnp.exp2(top_a - top), jnp.exp2(top_b - top)
        total = share_a * total_a + share_b * total_b
        some = total > 0.0
        safe = jnp.where(some, total, 1.0)
        mixed = (share_a * a_ref[0, :, span] + share_b * b_ref[0, :, span]) / safe
        out_ref[:, span] = mixed.astype(jnp.bfloat16)
        stat = jnp.where(some, top + jnp.log2(safe), EMPTY)
        terms = split_stats(stat, 3 * head, lanes, terms)
    out_ref[:, BLOCK:] = terms.astype(jnp.bfloat16)


def merge(a, b):
    return pl.pallas_call(
        merge_kernel,
        out_shape=jax.ShapeDtypeStruct(a.shape[1:], jnp.bfloat16),
        compiler_params=pltpu.CompilerParams(vmem_limit_bytes=VMEM_LIMIT),
        cost_estimate=cost(3.0),
    )(a, b)


def project_kernel(shards, rank_ref, cos_ref, sin_ref, gain_ref, *refs):
    own_ref, right, left = refs[0], refs[1:shards], refs[shards : 2 * shards - 1]
    weight_ref, out_ref, features, gathered, feature_sem, weight_sem = refs[2 * shards - 1 :]
    rank = rank_ref[0]
    span = features.shape[2]

    def weight_copy(shard):
        rows = pl.ds(shard * span, span)
        return pltpu.make_async_copy(weight_ref.at[rows], gathered.at[rows], weight_sem.at[shard])

    for shard in range(shards):

        @pl.when(rank == shard)
        def _(shard=shard):
            pltpu.make_async_copy(own_ref, features.at[shard], feature_sem.at[shard]).start()

        for step in range(1, shards):
            if shard + step < shards:

                @pl.when(rank == shard + step)
                def _(shard=shard, step=step):
                    pltpu.make_async_copy(
                        right[step - 1], features.at[shard], feature_sem.at[shard]
                    ).start()

            if shard - step >= 0:

                @pl.when(rank == shard - step)
                def _(shard=shard, step=step):
                    pltpu.make_async_copy(
                        left[step - 1], features.at[shard], feature_sem.at[shard]
                    ).start()

        weight_copy(shard).start()
    raw = 0.0
    for shard in range(shards):
        pltpu.make_async_copy(own_ref, features.at[shard], feature_sem.at[shard]).wait()
        weight_copy(shard).wait()
        raw = raw + plain_dot(features[shard], gathered[shard * span : (shard + 1) * span])
    width = raw.shape[1] // 2
    columns = []
    for head in range(width // HD):
        one = raw[:, head * HD : (head + 1) * HD]
        mean = jnp.sum(one * one, axis=1, keepdims=True) * (1.0 / HD)
        one = one * lax.rsqrt(mean + 1e-06) * gain_ref[...]
        columns.append(one * cos_ref[...] + pltpu.roll(one, HD // 2, 1) * sin_ref[...])
    new_keys = jnp.concatenate(columns, axis=1) if len(columns) > 1 else columns[0]
    out_ref[0] = new_keys.astype(jnp.bfloat16)
    out_ref[1] = raw[:, width:].astype(jnp.bfloat16)


def project(rank, cos, sin, gain, own, right, left, weight):
    shards = len(right) + 1
    new_count, span = own.shape
    vmem = pl.BlockSpec(memory_space=pltpu.VMEM)
    return pl.pallas_call(
        functools.partial(project_kernel, shards),
        out_shape=jax.ShapeDtypeStruct((2, new_count, weight.shape[1] // 2), jnp.bfloat16),
        in_specs=[SMEM, vmem, vmem, vmem] + [ANY] * (2 * shards),
        out_specs=vmem,
        scratch_shapes=[
            pltpu.VMEM((shards, new_count, span), jnp.bfloat16),
            pltpu.VMEM(weight.shape, weight.dtype),
            pltpu.SemaphoreType.DMA((shards,)),
            pltpu.SemaphoreType.DMA((shards,)),
        ],
        compiler_params=pltpu.CompilerParams(vmem_limit_bytes=VMEM_LIMIT),
        cost_estimate=cost(5.0),
    )(rank, cos, sin, gain, own, *right, *left, weight)


def fresh_kernel(q_ref, fresh_ref, own_ref, mate_ref, out_ref):
    new_count = q_ref.shape[0]
    rows = GROUP * new_count
    row = lax.broadcasted_iota(jnp.int32, (new_count, new_count), 0)
    column = lax.broadcasted_iota(jnp.int32, (new_count, new_count), 1)
    lanes = lax.broadcasted_iota(jnp.int32, (new_count, EXTRA), 1)
    heads = [slice(head * HD, (head + 1) * HD) for head in range(GROUP)]
    stacked = jnp.concatenate([q_ref[:, span] for span in heads], axis=0)
    scores = row_dot(stacked, fresh_ref[0]).reshape(GROUP, new_count, new_count)
    scores = jnp.where((column <= row)[None], scores * SCALE, EMPTY)
    extras = [ref[0, :, BLOCK:].astype(jnp.bfloat16) for ref in (own_ref, mate_ref)]
    terms = jnp.zeros((new_count, EXTRA), jnp.float32)
    weights, shares = [], []
    for head in range(GROUP):
        stats = [state_stats(extra, head) for extra in extras]
        top = jnp.broadcast_to(jnp.max(scores[head], axis=1, keepdims=True), lanes.shape)
        for other, _ in stats:
            top = jnp.maximum(top, other)
        pieces = [jnp.exp2(scores[head, :, start : start + HD] - top) for start in range(0, new_count, HD)]
        total = jnp.broadcast_to(jnp.sum(sum(pieces), axis=1, keepdims=True), lanes.shape)
        probabilities = jnp.concatenate(pieces, axis=1)
        shares.append([jnp.exp2(other - top) for other, _ in stats])
        for share, (_, part) in zip(shares[-1], stats):
            total = total + share * part
        terms = split_stats(top, 3 * head, lanes, terms)
        terms = split_stats(total, TOTALS + 3 * head, lanes, terms)
        weights.append(probabilities.astype(jnp.bfloat16))
    sums = plain_dot(jnp.concatenate(weights, axis=0), fresh_ref[1]).reshape(GROUP, new_count, HD)
    for head, span in enumerate(heads):
        out_ref[0, :, span] = (
            sums[head] + shares[head][0] * own_ref[0, :, span] + shares[head][1] * mate_ref[0, :, span]
        )
    out_ref[0, :, BLOCK:] = terms


def attend_fresh(queries, fresh, own, mate):
    kv_local, new_count = own.shape[0], queries.shape[0]
    state = pl.BlockSpec((1, new_count, BLOCK + EXTRA), lambda k: (k, 0, 0))
    return pl.pallas_call(
        fresh_kernel,
        grid=(kv_local,),
        out_shape=jax.ShapeDtypeStruct(own.shape, jnp.float32),
        in_specs=[
            pl.BlockSpec((new_count, BLOCK), lambda k: (0, k)),
            pl.BlockSpec((2, new_count, HD), lambda k: (0, 0, k)),
            state,
            state,
        ],
        out_specs=state,
        compiler_params=pltpu.CompilerParams(vmem_limit_bytes=VMEM_LIMIT),
        cost_estimate=cost(8.0),
    )(queries, fresh, own, mate)


def final_kernel(parts, *refs):
    state_ref, partials, out_ref = refs[0], refs[1 : 1 + parts], refs[-1]
    extra = state_ref[0, :, BLOCK:].astype(jnp.bfloat16)
    for head in range(GROUP):
        span = slice(head * HD, (head + 1) * HD)
        top, total = state_stats(extra, head)
        stats = [joined_stats(partial[:, BLOCK:], 3 * head) for partial in partials]
        best = top
        for stat in stats:
            best = jnp.maximum(best, stat)
        share = jnp.exp2(top - best)
        mixed, total = share * state_ref[0, :, span], share * total
        for stat, partial in zip(stats, partials):
            share = jnp.exp2(stat - best)
            total = total + share
            mixed = mixed + share * partial[:, span].astype(jnp.float32)
        out_ref[:, span] = (mixed / total).astype(jnp.bfloat16)


def final(shape, kv_head, states, partials, before):
    new_count = states.shape[1]
    whole = pl.BlockSpec((new_count, BLOCK + EXTRA), lambda step: (0, 0))
    given = [] if before is None else [before]
    return pl.pallas_call(
        functools.partial(final_kernel, len(partials)),
        grid=(1,),
        out_shape=jax.ShapeDtypeStruct(shape, jnp.bfloat16),
        in_specs=[pl.BlockSpec((1, new_count, BLOCK + EXTRA), lambda step: (kv_head, 0, 0))]
        + [whole] * len(partials)
        + [ANY] * len(given),
        out_specs=pl.BlockSpec((new_count, BLOCK), lambda step: (0, kv_head)),
        input_output_aliases={1 + len(partials): 0} if given else {},
        compiler_params=pltpu.CompilerParams(vmem_limit_bytes=VMEM_LIMIT),
        cost_estimate=cost(3.0),
    )(states, *partials, *given)


def write_kernel(holders, new_pages, base, me_ref, table_ref, *refs):
    pages = refs[:holders]
    out_ref, sem = refs[holders + 1], refs[holders + 2]
    me = me_ref[0]

    def each(action):
        for holder in range(holders):
            for page in range(new_pages):

                @pl.when(table_ref[holder, base + page] == me)
                def _(holder=holder, page=page):
                    slot = table_ref[holder, base + new_pages + page]
                    copy = pltpu.make_async_copy(
                        pages[holder].at[:, pl.ds(page * PAGE, PAGE)],
                        out_ref.at[:, slot],
                        sem.at[holder, page],
                    )
                    getattr(copy, action)()

    each("start")
    each("wait")


def write(me, tables, fresh, pool, new_pages, base):
    holders = len(fresh)
    return pl.pallas_call(
        functools.partial(write_kernel, holders, new_pages, base),
        out_shape=jax.ShapeDtypeStruct(pool.shape, pool.dtype),
        in_specs=[SMEM, SMEM]
        + [pl.BlockSpec(memory_space=pltpu.VMEM)] * holders
        + [ANY],
        out_specs=ANY,
        input_output_aliases={2 + holders: 0},
        scratch_shapes=[pltpu.SemaphoreType.DMA((holders, new_pages))],
        compiler_params=pltpu.CompilerParams(vmem_limit_bytes=VMEM_LIMIT),
        cost_estimate=cost(2.0),
    )(me, tables, *fresh, pool)


def per_device(
    hidden,
    k_weight,
    v_weight,
    k_gain,
    queries,
    kv_pool,
    page_holder,
    page_slot,
    page_count,
    write_owner,
    write_slot,
):
    inst_count = lax.axis_size("inst")
    shards = lax.axis_size("tp")
    me = lax.axis_index("inst").astype(jnp.int32)
    rank = lax.axis_index("tp").astype(jnp.int32)
    pages_listed = page_holder.shape[1]
    new_pages = write_owner.shape[1]
    capacity = 3 * pages_listed // (2 * inst_count)
    new_count = hidden.shape[0]
    kv_local = k_weight.shape[1] // HD
    me_list = me.reshape(1)

    def swap(array, step):
        return lax.ppermute(array, "inst", [(i, i ^ step) for i in range(inst_count)])

    def shift(array, step):
        pairs = [(i, i + step) for i in range(shards) if 0 <= i + step < shards]
        return lax.ppermute(array, "tp", pairs)

    def after(array, *done):
        return lax.optimization_barrier((array,) + done)[0]

    heads = list(range(kv_local))
    base = 2 * pages_listed + 1
    own_table = jnp.concatenate(
        [page_holder[0], page_slot[0], page_count, write_owner[0], write_slot[0]]
    )
    own_table = jnp.pad(own_table, (0, 128 - own_table.shape[0]))[None]
    others = range(2, inst_count, 2)

    gathered = lax.all_gather(own_table, "inst", axis=0, tiled=True)
    asked = {0: queries, 1: swap(queries, 1)}
    for step in others:
        asked[step] = swap(queries, step)
    right, left = [shift(hidden, 1)], [shift(hidden, -1)]
    weight = lax.all_gather(
        jnp.concatenate([k_weight, v_weight], axis=1), "inst", axis=0, tiled=True
    )
    tables = {
        step: lax.dynamic_slice_in_dim(gathered, me ^ step, 1, axis=0) for step in range(inst_count)
    }

    def forward(done):
        arrived = (right[-1], left[-1])
        if len(right) + 1 < shards:
            right.append(shift(after(right[-1], done), 1))
            left.append(shift(after(left[-1], done), -1))
        return arrived

    common = dict(pool=kv_pool, pages_listed=pages_listed, capacity=capacity)
    own_state, pool_copy = attend(me_list, tables[0], [queries], heads, copy_pool=True, **common)
    forward(own_state)
    mate_state = attend(me_list, after(tables[1], own_state), [asked[1]], heads, **common)
    arrived = forward(mate_state)
    last = mate_state
    from_mate = swap(mate_state, 1)

    partials = [[] for k in heads]
    waiting = None
    for step in others:
        asked[step + 1] = swap(after(asked[step], last), 1)
        for k in heads:
            here = attend(
                me_list, after(tables[step], last, *arrived), [asked[step]], [k], **common
            )
            last = here
            if waiting is not None:
                merged = merge(waiting[0], after(waiting[1], last))
                partials[waiting[2]].append(swap(merged, waiting[3]))
                last = merged
            last = attend(
                me_list, after(tables[step + 1], last), [asked[step + 1]], [k], **common
            )
            waiting = (here, swap(last, 1), k, step)
            if k == 0:
                arrived = forward(last)
    while len(right) + 1 < shards:
        forward(last)

    frequency = 1000000.0 ** (-(jnp.arange(HD // 2, dtype=jnp.float32) * 2.0) / HD)
    positions = page_count[0] * PAGE + jnp.arange(new_count, dtype=jnp.int32)
    angles = positions.astype(jnp.float32)[:, None] * frequency[None, :]
    cosine, sine = jnp.cos(angles), jnp.sin(angles)
    fresh = project(
        rank.reshape(1),
        jnp.concatenate([cosine, cosine], axis=1),
        jnp.concatenate([-sine, sine], axis=1),
        k_gain[None, :],
        after(hidden, last),
        right,
        left,
        weight,
    )
    merged = merge(waiting[0], after(waiting[1], fresh))
    partials[waiting[2]].append(swap(merged, waiting[3]))
    states = attend_fresh(queries, fresh, own_state, from_mate)
    attention_out = None
    for k in heads:
        attention_out = final(queries.shape, k, states, partials[k], attention_out)
    pages = {0: fresh, 1: swap(fresh, 1)}
    for step in range(2, inst_count, 2):
        pages[step] = swap(fresh, step)
        pages[step + 1] = swap(pages[step], 1)
    new_pool = write(
        me_list,
        jnp.concatenate([tables[step] for step in range(inst_count)]),
        [pages[step] for step in range(inst_count)],
        pool_copy,
        new_pages,
        base,
    )
    return (attention_out, new_pool)


def solution(mesh):
    return jax.shard_map(
        per_device,
        mesh=mesh,
        in_specs=(
            P(("groups", "inst"), "tp"),
            P("inst", "tp"),
            P("inst", "tp"),
            P(),
            P(("groups", "inst"), "tp"),
            P(None, ("groups", "inst"), None, "tp"),
            P(("groups", "inst"), None),
            P(("groups", "inst"), None),
            P(("groups", "inst")),
            P(("groups", "inst"), None),
            P(("groups", "inst"), None),
        ),
        out_specs=(P(("groups", "inst"), "tp"), P(None, ("groups", "inst"), None, "tp")),
        check_vma=False,
    )
```

```python
import functools
import math

import jax
import jax.numpy as jnp
from jax import lax
from jax.experimental import pallas as pl
from jax.experimental.pallas import tpu as pltpu
from jax.sharding import PartitionSpec as P

HD = 128
PAGE = 128
GROUP = 8
BLOCK = GROUP * HD
EXTRA = 128
TOTALS = 64
EMPTY = -1e30
LOG2E = 1.4426950408889634
SCALE = LOG2E / math.sqrt(HD)
CHUNK = 4
ANY = pl.BlockSpec(memory_space=pl.ANY)
SMEM = pl.BlockSpec(memory_space=pltpu.SMEM)
VMEM_LIMIT = 63 * 1024 * 1024


def cost(microseconds):
    return pl.CostEstimate(
        flops=int(microseconds * 1e9), bytes_accessed=int(microseconds * 3e6), transcendentals=0
    )


def row_dot(a, b):
    return lax.dot_general(a, b, (((1,), (1,)), ((), ())), preferred_element_type=jnp.float32)


def plain_dot(a, b):
    return lax.dot_general(a, b, (((1,), (0,)), ((), ())), preferred_element_type=jnp.float32)


def split_stats(stat, lane, lanes, terms):
    high = stat.astype(jnp.bfloat16).astype(jnp.float32)
    rest = stat - high
    middle = rest.astype(jnp.bfloat16).astype(jnp.float32)
    terms = jnp.where(lanes == lane, high, terms)
    terms = jnp.where(lanes == lane + 1, middle, terms)
    return jnp.where(lanes == lane + 2, rest - middle, terms)


def joined_stats(extra, lane):
    term = lax.broadcasted_iota(jnp.int32, (EXTRA, HD), 0)
    picked = jnp.where((term >= lane) & (term < lane + 3), 1.0, 0.0).astype(jnp.bfloat16)
    return plain_dot(extra, picked)


def state_stats(extra, head):
    return joined_stats(extra, 3 * head), joined_stats(extra, TOTALS + 3 * head)


def attend_kernel(plan, refs):
    requests, kv_heads, pages_listed = plan["requests"], plan["kv_heads"], plan["pages_listed"]
    copy_pool, resume = plan["copy_pool"], plan["resume"]
    width = len(kv_heads)
    items = requests * width
    refs = list(refs)
    me_ref, table_ref = refs.pop(0), refs.pop(0)
    q_refs = [refs.pop(0) for _ in range(requests)]
    state_ref = refs.pop(0) if resume else None
    pool_ref = refs.pop(0)
    out_refs = [refs.pop(0) for _ in range(items)]
    new_pool_ref = refs.pop(0) if copy_pool else None
    q_buf, kv_buf, acc, maxima, totals, slots, q_sem, kv_sem, out_sem = refs[:9]
    refs = refs[9:]
    if resume:
        send_buf = refs.pop(0)
    new_count = q_buf.shape[2]
    rows = GROUP * new_count
    shape = (GROUP, new_count, HD)
    lanes = lax.broadcasted_iota(jnp.int32, (new_count, HD), 1)

    def q_copies(item):
        offset = kv_heads[item % width] * BLOCK
        return [
            pltpu.make_async_copy(
                q_refs[item // width].at[:, pl.ds(offset + head * HD, HD)],
                q_buf.at[item, head],
                q_sem.at[item, head],
            )
            for head in range(GROUP)
        ]

    def page_copies(request, place, slot):
        return [
            pltpu.make_async_copy(
                pool_ref.at[:, slot, :, pl.ds(kv_head * HD, HD)],
                kv_buf.at[request, column, :, place],
                kv_sem.at[request, column, place],
            )
            for column, kv_head in enumerate(kv_heads)
        ]

    def out_copy(item, index):
        source, target = send_buf if resume else acc, out_refs[item]
        part = [pl.ds(0, GROUP), pl.ds(GROUP, 1)][index]
        return pltpu.make_async_copy(
            source.at[item, part], target.at[0, part], out_sem.at[item, index]
        )

    for item in range(items):
        for copy in q_copies(item):
            copy.start()
    if resume:
        state_copy = pltpu.make_async_copy(state_ref, acc, out_sem.at[0, 0])
        state_copy.start()
    me = me_ref[0]
    for request in range(requests):
        count = table_ref[request, 2 * pages_listed]

        def look(page, found, request=request, count=count):
            mine = (page < count) & (table_ref[request, page] == me)

            @pl.when(mine)
            def _():
                for copy in page_copies(request, found, table_ref[request, pages_listed + page]):
                    copy.start()

            return found + mine.astype(jnp.int32)

        slots[request] = lax.fori_loop(0, count, look, 0)
    pool_in, pool_out = [], []
    if copy_pool:
        pool_buf, pool_sem = refs
        slot_total = pool_ref.shape[1]
        parts = pool_sem.shape[1]
        step = slot_total // parts
        for index in range(2):
            for part in range(parts):
                piece = (index, pl.ds(part * step, step))
                sem = pool_sem.at[index, part]
                pool_in.append(pltpu.make_async_copy(pool_ref.at[piece], pool_buf.at[piece], sem))
                pool_out.append(
                    pltpu.make_async_copy(pool_buf.at[piece], new_pool_ref.at[piece], sem)
                )
        for copy in pool_in:
            copy.start()
    for item in range(items):
        for copy in q_copies(item):
            copy.wait()
    if resume:
        state_copy.wait()

    def one_item(item, carry):
        request = item // width
        column = item % width
        found = slots[request]
        sums = pl.ds(0, GROUP)
        if resume:
            extra = acc[item, GROUP].astype(jnp.bfloat16)
            for head in range(GROUP):
                maxima[head], total = state_stats(extra, head)
                totals[head] = jnp.where(lanes == 0, total, 0.0)
        else:
            acc[item, sums] = jnp.zeros(shape, jnp.float32)
            totals[...] = jnp.zeros(shape, jnp.float32)
            maxima[...] = jnp.full(shape, EMPTY, jnp.float32)

        @pl.when(column == 0)
        def _():
            def arrived(place, carry):
                for copy in page_copies(request, place, 0):
                    copy.wait()
                return carry

            lax.fori_loop(0, found, arrived, 0)

        def chunk(first, count):
            keys = kv_buf[request, column, 0, pl.ds(first, count)].reshape(count * PAGE, HD)
            values = kv_buf[request, column, 1, pl.ds(first, count)].reshape(count * PAGE, HD)
            scores = row_dot(q_buf[item].reshape(rows, HD), keys)
            old = maxima[...].reshape(rows, HD)
            top = jnp.maximum(old, jnp.max(scores, axis=1, keepdims=True) * SCALE)
            rescale = jnp.exp2(old - top)
            total = totals[...].reshape(rows, HD) * rescale
            pieces = []
            for part in range(count):
                piece = jnp.exp2(scores[:, part * PAGE : (part + 1) * PAGE] * SCALE - top)
                total = total + piece
                pieces.append(piece.astype(jnp.bfloat16))
            weights = jnp.concatenate(pieces, axis=1) if count > 1 else pieces[0]
            maxima[...] = top.reshape(shape)
            totals[...] = total.reshape(shape)
            acc[item, sums] = acc[item, sums] * rescale.reshape(shape) + plain_dot(
                weights, values
            ).reshape(shape)

        whole = found // CHUNK
        left = found % CHUNK

        def step(index, carry):
            chunk(index * CHUNK, CHUNK)
            return carry

        lax.fori_loop(0, whole, step, 0)
        for count in range(1, CHUNK):

            @pl.when(left == count)
            def _(count=count):
                chunk(whole * CHUNK, count)

        def send(index):
            for each in range(items):

                @pl.when(item == each)
                def _(each=each):
                    out_copy(each, index).start()

        if not resume:
            send(0)
        terms = jnp.zeros((new_count, HD), jnp.float32)
        for head in range(GROUP):
            total = jnp.sum(totals[head], axis=1, keepdims=True)
            if resume:
                some = total > 0.0
                safe = jnp.where(some, total, 1.0)
                send_buf[item, head] = (acc[item, head] * (1.0 / safe)).astype(jnp.bfloat16)
                stat = jnp.where(some, maxima[head] + jnp.log2(safe), EMPTY)
                terms = split_stats(stat, 3 * head, lanes, terms)
            else:
                terms = split_stats(maxima[head], 3 * head, lanes, terms)
                terms = split_stats(total, TOTALS + 3 * head, lanes, terms)
        if resume:
            send_buf[item, GROUP] = terms.astype(jnp.bfloat16)
            send(0)
        else:
            acc[item, GROUP] = terms
        send(1)
        if copy_pool:

            @pl.when(item == 0)
            def _():
                for copy_in, copy_out in zip(pool_in, pool_out):
                    copy_in.wait()
                    copy_out.start()

        return carry

    lax.fori_loop(0, items, one_item, 0)
    for item in range(items):
        for index in range(2):
            out_copy(item, index).wait()
    for copy in pool_out:
        copy.wait()


def attend(me, tables, asked, kv_heads, pool, pages_listed, capacity, state=None, copy_pool=False):
    requests, width, new_count = tables.shape[0], len(kv_heads), asked[0].shape[0]
    items = requests * width
    resume = state is not None
    blocks = (GROUP + 1, new_count, HD)
    kind = jnp.bfloat16 if resume else jnp.float32
    out_shape = [jax.ShapeDtypeStruct((1,) + blocks, kind) for _ in range(items)]
    scratch = [
        pltpu.VMEM((items, GROUP, new_count, HD), jnp.bfloat16),
        pltpu.VMEM((requests, width, 2, capacity, PAGE, HD), jnp.bfloat16),
        pltpu.VMEM((items,) + blocks, jnp.float32),
        pltpu.VMEM((GROUP, new_count, HD), jnp.float32),
        pltpu.VMEM((GROUP, new_count, HD), jnp.float32),
        pltpu.SMEM((requests,), jnp.int32),
        pltpu.SemaphoreType.DMA((items, GROUP)),
        pltpu.SemaphoreType.DMA((requests, width, capacity)),
        pltpu.SemaphoreType.DMA((items, 2)),
    ]
    if resume:
        scratch.append(pltpu.VMEM((items,) + blocks, jnp.bfloat16))
    if copy_pool:
        out_shape.append(jax.ShapeDtypeStruct(pool.shape, pool.dtype))
        parts = next(part for part in (6, 3, 2, 1) if pool.shape[1] % part == 0)
        scratch += [pltpu.VMEM(pool.shape, pool.dtype), pltpu.SemaphoreType.DMA((2, parts))]
    plan = dict(
        requests=requests, kv_heads=kv_heads, pages_listed=pages_listed, copy_pool=copy_pool,
        resume=resume,
    )
    return pl.pallas_call(
        lambda *refs: attend_kernel(plan, refs),
        out_shape=out_shape,
        in_specs=[SMEM, SMEM] + [ANY] * (requests + resume + 1),
        out_specs=[ANY] * len(out_shape),
        scratch_shapes=scratch,
        compiler_params=pltpu.CompilerParams(vmem_limit_bytes=VMEM_LIMIT),
        cost_estimate=cost(1.5 + 5.5 * items),
    )(me, tables, *asked, *([state] if resume else []), pool)


def project_kernel(shards, rank_ref, cos_ref, sin_ref, gain_ref, *refs):
    hidden_refs, weight_refs = refs[:shards], refs[shards : shards + 2]
    out_ref, features, gathered, feature_sem, weight_sem = refs[shards + 2 :]
    span = features.shape[2]
    width = weight_refs[0].shape[1]

    def copies(shard):
        rows = pl.ds(shard * span, span)
        return [
            pltpu.make_async_copy(
                weight_refs[kind].at[rows],
                gathered.at[rows, pl.ds(kind * width, width)],
                weight_sem.at[kind, shard],
            )
            for kind in range(2)
        ]

    for step in range(shards):
        shard = lax.rem(rank_ref[0] + shards - step, shards)
        pltpu.make_async_copy(hidden_refs[step], features.at[shard], feature_sem.at[step]).start()
    for shard in range(shards):
        for copy in copies(shard):
            copy.start()
    for step in range(shards):
        pltpu.make_async_copy(hidden_refs[step], features.at[0], feature_sem.at[step]).wait()
    raw = 0.0
    for shard in range(shards):
        for copy in copies(shard):
            copy.wait()
        raw = raw + plain_dot(features[shard], gathered[shard * span : (shard + 1) * span])
    columns = []
    for head in range(width // HD):
        one = raw[:, head * HD : (head + 1) * HD]
        mean = jnp.sum(one * one, axis=1, keepdims=True) * (1.0 / HD)
        one = one * lax.rsqrt(mean + 1e-06) * gain_ref[...]
        columns.append(one * cos_ref[...] + pltpu.roll(one, HD // 2, 1) * sin_ref[...])
    new_keys = jnp.concatenate(columns, axis=1) if len(columns) > 1 else columns[0]
    out_ref[0] = new_keys.astype(jnp.bfloat16)
    out_ref[1] = raw[:, width:].astype(jnp.bfloat16)


def project(rank, cos, sin, gain, hidden, weights):
    shards = len(hidden)
    new_count, span = hidden[0].shape
    depth, width = weights[0].shape
    vmem = pl.BlockSpec(memory_space=pltpu.VMEM)
    return pl.pallas_call(
        functools.partial(project_kernel, shards),
        out_shape=jax.ShapeDtypeStruct((2, new_count, width), jnp.bfloat16),
        in_specs=[SMEM, vmem, vmem, vmem] + [ANY] * (shards + 2),
        out_specs=vmem,
        scratch_shapes=[
            pltpu.VMEM((shards, new_count, span), jnp.bfloat16),
            pltpu.VMEM((depth, 2 * width), jnp.bfloat16),
            pltpu.SemaphoreType.DMA((shards,)),
            pltpu.SemaphoreType.DMA((2, shards)),
        ],
        compiler_params=pltpu.CompilerParams(vmem_limit_bytes=VMEM_LIMIT),
        cost_estimate=cost(5.0),
    )(rank, cos, sin, gain, *hidden, *weights)


def final_kernel(parts, q_ref, fresh_ref, *refs):
    states, partials, out_ref = refs[:2], refs[2 : 2 + parts], refs[-1]
    new_count = q_ref.shape[0]
    row = lax.broadcasted_iota(jnp.int32, (new_count, new_count), 0)
    column = lax.broadcasted_iota(jnp.int32, (new_count, new_count), 1)
    heads = [slice(head * HD, (head + 1) * HD) for head in range(GROUP)]
    stacked = jnp.concatenate([q_ref[:, span] for span in heads], axis=0)
    scores = row_dot(stacked, fresh_ref[0]).reshape(GROUP, new_count, new_count)
    scores = jnp.where((column <= row)[None], scores * SCALE, EMPTY)
    extras = [ref[0, GROUP].astype(jnp.bfloat16) for ref in states]
    weights, shares, divisors = [], [], []
    for head in range(GROUP):
        stats = [state_stats(extra, head) for extra in extras]
        stats += [(joined_stats(partial[0, GROUP], 3 * head), 1.0) for partial in partials]
        top = jnp.broadcast_to(jnp.max(scores[head], axis=1, keepdims=True), (new_count, HD))
        for other, _ in stats:
            top = jnp.maximum(top, other)
        pieces = [
            jnp.exp2(scores[head, :, start : start + HD] - top) for start in range(0, new_count, HD)
        ]
        total = jnp.broadcast_to(jnp.sum(sum(pieces), axis=1, keepdims=True), (new_count, HD))
        shares.append([jnp.exp2(other - top) for other, _ in stats])
        for share, (_, part) in zip(shares[-1], stats):
            total = total + share * part
        divisors.append(total)
        weights.append(jnp.concatenate(pieces, axis=1).astype(jnp.bfloat16))
    sums = plain_dot(jnp.concatenate(weights, axis=0), fresh_ref[1]).reshape(GROUP, new_count, HD)
    for head, span in enumerate(heads):
        mixed = sums[head]
        for share, ref in zip(shares[head], states + partials):
            mixed = mixed + share * ref[0, head].astype(jnp.float32)
        out_ref[:, span] = (mixed / divisors[head]).astype(jnp.bfloat16)


def final(kv_head, queries, fresh, states, partials, before):
    new_count = queries.shape[0]
    blocks = (1, GROUP + 1, new_count, HD)
    given = [] if before is None else [before]
    return pl.pallas_call(
        functools.partial(final_kernel, len(partials)),
        grid=(1,),
        out_shape=jax.ShapeDtypeStruct(queries.shape, jnp.bfloat16),
        in_specs=[
            pl.BlockSpec((new_count, BLOCK), lambda step: (0, kv_head)),
            pl.BlockSpec((2, new_count, HD), lambda step: (0, 0, kv_head)),
        ]
        + [pl.BlockSpec(blocks, lambda step: (0, 0, 0, 0))] * (len(states) + len(partials))
        + [ANY] * len(given),
        out_specs=pl.BlockSpec((new_count, BLOCK), lambda step: (0, kv_head)),
        input_output_aliases={2 + len(states) + len(partials): 0} if given else {},
        compiler_params=pltpu.CompilerParams(vmem_limit_bytes=VMEM_LIMIT),
        cost_estimate=cost(4.5),
    )(queries, fresh, *states, *partials, *given)


def write_kernel(holders, new_pages, base, me_ref, table_ref, *refs):
    pages = refs[:holders]
    out_ref, sem = refs[holders + 1], refs[holders + 2]
    me = me_ref[0]

    def each(action):
        for holder in range(holders):
            for page in range(new_pages):

                @pl.when(table_ref[holder, base + page] == me)
                def _(holder=holder, page=page):
                    slot = table_ref[holder, base + new_pages + page]
                    copy = pltpu.make_async_copy(
                        pages[holder].at[:, pl.ds(page * PAGE, PAGE)],
                        out_ref.at[:, slot],
                        sem.at[holder, page],
                    )
                    getattr(copy, action)()

    each("start")
    each("wait")


def write(me, tables, fresh, pool, new_pages, base):
    holders = len(fresh)
    return pl.pallas_call(
        functools.partial(write_kernel, holders, new_pages, base),
        out_shape=jax.ShapeDtypeStruct(pool.shape, pool.dtype),
        in_specs=[SMEM, SMEM]
        + [pl.BlockSpec(memory_space=pltpu.VMEM)] * holders
        + [ANY],
        out_specs=ANY,
        input_output_aliases={2 + holders: 0},
        scratch_shapes=[pltpu.SemaphoreType.DMA((holders, new_pages))],
        compiler_params=pltpu.CompilerParams(vmem_limit_bytes=VMEM_LIMIT),
        cost_estimate=cost(2.0),
    )(me, tables, *fresh, pool)


def per_device(
    hidden,
    k_weight,
    v_weight,
    k_gain,
    queries,
    kv_pool,
    page_holder,
    page_slot,
    page_count,
    write_owner,
    write_slot,
):
    inst_count = lax.axis_size("inst")
    shards = lax.axis_size("tp")
    me = lax.axis_index("inst").astype(jnp.int32)
    rank = lax.axis_index("tp").astype(jnp.int32)
    pages_listed = page_holder.shape[1]
    new_pages = write_owner.shape[1]
    capacity = 3 * pages_listed // (2 * inst_count)
    new_count = hidden.shape[0]
    kv_local = k_weight.shape[1] // HD
    me_list = me.reshape(1)

    def swap(array, step):
        return lax.ppermute(array, "inst", [(i, i ^ step) for i in range(inst_count)])

    def shift(array, step):
        return lax.ppermute(array, "tp", [(i, (i + step) % shards) for i in range(shards)])

    def after(array, *done):
        return lax.optimization_barrier((array,) + done)[0]

    heads = list(range(kv_local))
    base = 2 * pages_listed + 1
    own_table = jnp.concatenate(
        [page_holder[0], page_slot[0], page_count, write_owner[0], write_slot[0]]
    )
    own_table = jnp.pad(own_table, (0, 128 - own_table.shape[0]))[None]
    others = range(2, inst_count, 2)

    gathered = lax.all_gather(own_table, "inst", axis=0, tiled=True)
    sent = after(queries, gathered)
    asked = {0: queries, 1: swap(sent, 1)}
    for step in others:
        asked[step] = swap(sent, step)
    features = [hidden]
    for step in range(1, shards):
        features.append(shift(after(hidden, gathered), step))
    near, far = [features[1], features[-1]], features[2:-1]
    weights = [
        lax.all_gather(after(weight, gathered), "inst", axis=0, tiled=True)
        for weight in (k_weight, v_weight)
    ]
    tables = {
        step: lax.dynamic_slice_in_dim(gathered, me ^ step, 1, axis=0) for step in range(inst_count)
    }

    common = dict(pool=kv_pool, pages_listed=pages_listed, capacity=capacity)
    *found, pool_copy = attend(
        me_list, jnp.concatenate([tables[0], tables[1]]), [queries, asked[1]], heads,
        copy_pool=True, **common,
    )
    own_states, mate_states = found[:kv_local], found[kv_local:]
    last = mate_states[-1]

    partials = [[] for k in heads]
    for step in others:
        asked[step + 1] = swap(after(asked[step], last, *near), 1)
        begun = attend(
            me_list, after(tables[step + 1], last), [asked[step + 1]], heads, **common
        )
        last = begun[-1]
        halves = [swap(after(state, *far), 1) for state in begun]
        if step == 2:
            from_mate = [swap(after(state, last), 1) for state in mate_states]
        for k in heads:
            (last,) = attend(
                me_list, after(tables[step], last), [asked[step]], [k], state=halves[k],
                **common,
            )
            partials[k].append(swap(last, step))

    frequency = 1000000.0 ** (-(jnp.arange(HD // 2, dtype=jnp.float32) * 2.0) / HD)
    positions = page_count[0] * PAGE + jnp.arange(new_count, dtype=jnp.int32)
    angles = positions.astype(jnp.float32)[:, None] * frequency[None, :]
    cosine, sine = jnp.cos(angles), jnp.sin(angles)
    fresh = project(
        rank.reshape(1),
        jnp.concatenate([cosine, cosine], axis=1),
        jnp.concatenate([-sine, sine], axis=1),
        k_gain[None, :],
        [after(hidden, last)] + features[1:],
        weights,
    )
    attention_out = None
    for k in heads:
        attention_out = final(
            k, queries, fresh, [own_states[k], from_mate[k]], partials[k], attention_out
        )
    pages = {0: fresh, 1: swap(fresh, 1)}
    for step in range(2, inst_count, 2):
        pages[step] = swap(fresh, step)
        pages[step + 1] = swap(pages[step], 1)
    new_pool = write(
        me_list,
        jnp.concatenate([tables[step] for step in range(inst_count)]),
        [pages[step] for step in range(inst_count)],
        pool_copy,
        new_pages,
        base,
    )
    return (attention_out, new_pool)


def solution(mesh):
    return jax.shard_map(
        per_device,
        mesh=mesh,
        in_specs=(
            P(("groups", "inst"), "tp"),
            P("inst", "tp"),
            P("inst", "tp"),
            P(),
            P(("groups", "inst"), "tp"),
            P(None, ("groups", "inst"), None, "tp"),
            P(("groups", "inst"), None),
            P(("groups", "inst"), None),
            P(("groups", "inst")),
            P(("groups", "inst"), None),
            P(("groups", "inst"), None),
        ),
        out_specs=(P(("groups", "inst"), "tp"), P(None, ("groups", "inst"), None, "tp")),
        check_vma=False,
    )
```

```python
import functools
import math

import jax
import jax.numpy as jnp
from jax import lax
from jax.experimental import pallas as pl
from jax.experimental.pallas import tpu as pltpu
from jax.sharding import PartitionSpec as P

HD = 128
PAGE = 128
GROUP = 8
BLOCK = GROUP * HD
EXTRA = 128
TOTALS = 64
EMPTY = -1e30
LOG2E = 1.4426950408889634
SCALE = LOG2E / math.sqrt(HD)
CHUNK = 4
ANY = pl.BlockSpec(memory_space=pl.ANY)
SMEM = pl.BlockSpec(memory_space=pltpu.SMEM)
VMEM_LIMIT = 63 * 1024 * 1024


def cost(microseconds):
    return pl.CostEstimate(
        flops=int(microseconds * 1e9), bytes_accessed=int(microseconds * 3e6), transcendentals=0
    )


def row_dot(a, b):
    return lax.dot_general(a, b, (((1,), (1,)), ((), ())), preferred_element_type=jnp.float32)


def plain_dot(a, b):
    return lax.dot_general(a, b, (((1,), (0,)), ((), ())), preferred_element_type=jnp.float32)


def split_stats(stat, lane, lanes, terms):
    high = stat.astype(jnp.bfloat16).astype(jnp.float32)
    rest = stat - high
    middle = rest.astype(jnp.bfloat16).astype(jnp.float32)
    terms = jnp.where(lanes == lane, high, terms)
    terms = jnp.where(lanes == lane + 1, middle, terms)
    return jnp.where(lanes == lane + 2, rest - middle, terms)


def joined_stats(extra, lane):
    term = lax.broadcasted_iota(jnp.int32, (EXTRA, HD), 0)
    picked = jnp.where((term >= lane) & (term < lane + 3), 1.0, 0.0).astype(jnp.bfloat16)
    return plain_dot(extra, picked)


def state_stats(extra, head):
    return joined_stats(extra, 3 * head), joined_stats(extra, TOTALS + 3 * head)


def attend_kernel(plan, refs):
    steps, kv_heads, pages_listed = plan["steps"], plan["kv_heads"], plan["pages_listed"]
    requests = len(steps)
    copy_pool, resume = plan["copy_pool"], plan["resume"]
    width = len(kv_heads)
    items = requests * width
    refs = list(refs)
    me_ref, table_ref = refs.pop(0), refs.pop(0)
    q_refs = [refs.pop(0) for _ in range(requests)]
    state_ref = refs.pop(0) if resume else None
    pool_ref = refs.pop(0)
    out_refs = [refs.pop(0) for _ in range(items)]
    new_pool_ref = refs.pop(0) if copy_pool else None
    q_buf, kv_buf, acc, maxima, totals, slots, q_sem, kv_sem, out_sem = refs[:9]
    refs = refs[9:]
    if resume:
        send_buf = refs.pop(0)
    new_count = q_buf.shape[2]
    rows = GROUP * new_count
    shape = (GROUP, new_count, HD)
    lanes = lax.broadcasted_iota(jnp.int32, (new_count, HD), 1)

    def q_copies(item):
        offset = kv_heads[item % width] * BLOCK
        return [
            pltpu.make_async_copy(
                q_refs[item // width].at[:, pl.ds(offset + head * HD, HD)],
                q_buf.at[item, head],
                q_sem.at[item, head],
            )
            for head in range(GROUP)
        ]

    def page_copies(request, place, slot):
        return [
            pltpu.make_async_copy(
                pool_ref.at[:, slot, :, pl.ds(kv_head * HD, HD)],
                kv_buf.at[request, column, :, place],
                kv_sem.at[request, column, place],
            )
            for column, kv_head in enumerate(kv_heads)
        ]

    def out_copy(item, index):
        source, target = send_buf if resume else acc, out_refs[item]
        part = [pl.ds(0, GROUP), pl.ds(GROUP, 1)][index]
        return pltpu.make_async_copy(
            source.at[item, part], target.at[0, part], out_sem.at[item, index]
        )

    for item in range(items):
        for copy in q_copies(item):
            copy.start()
    if resume:
        state_copy = pltpu.make_async_copy(state_ref, acc, out_sem.at[0, 0])
        state_copy.start()
    me = me_ref[0]
    for request, apart in enumerate(steps):
        whose = me ^ apart
        count = table_ref[whose, 2 * pages_listed]

        def look(page, found, request=request, whose=whose, count=count):
            mine = (page < count) & (table_ref[whose, page] == me)

            @pl.when(mine)
            def _():
                for copy in page_copies(request, found, table_ref[whose, pages_listed + page]):
                    copy.start()

            return found + mine.astype(jnp.int32)

        slots[request] = lax.fori_loop(0, count, look, 0)
    pool_in, pool_out = [], []
    if copy_pool:
        pool_buf, pool_sem = refs
        slot_total = pool_ref.shape[1]
        parts = pool_sem.shape[1]
        step = slot_total // parts
        for index in range(2):
            for part in range(parts):
                piece = (index, pl.ds(part * step, step))
                sem = pool_sem.at[index, part]
                pool_in.append(pltpu.make_async_copy(pool_ref.at[piece], pool_buf.at[piece], sem))
                pool_out.append(
                    pltpu.make_async_copy(pool_buf.at[piece], new_pool_ref.at[piece], sem)
                )
        for copy in pool_in:
            copy.start()
    for item in range(items):
        for copy in q_copies(item):
            copy.wait()
    if resume:
        state_copy.wait()

    def one_item(item, carry):
        request = item // width
        column = item % width
        found = slots[request]
        sums = pl.ds(0, GROUP)
        if resume:
            extra = acc[item, GROUP].astype(jnp.bfloat16)
            for head in range(GROUP):
                maxima[head], total = state_stats(extra, head)
                totals[head] = jnp.where(lanes == 0, total, 0.0)
        else:
            acc[item, sums] = jnp.zeros(shape, jnp.float32)
            totals[...] = jnp.zeros(shape, jnp.float32)
            maxima[...] = jnp.full(shape, EMPTY, jnp.float32)

        @pl.when(column == 0)
        def _():
            def arrived(place, carry):
                for copy in page_copies(request, place, 0):
                    copy.wait()
                return carry

            lax.fori_loop(0, found, arrived, 0)

        def chunk(first, count):
            keys = kv_buf[request, column, 0, pl.ds(first, count)].reshape(count * PAGE, HD)
            values = kv_buf[request, column, 1, pl.ds(first, count)].reshape(count * PAGE, HD)
            scores = row_dot(q_buf[item].reshape(rows, HD), keys)
            old = maxima[...].reshape(rows, HD)
            top = jnp.maximum(old, jnp.max(scores, axis=1, keepdims=True) * SCALE)
            rescale = jnp.exp2(old - top)
            total = totals[...].reshape(rows, HD) * rescale
            pieces = []
            for part in range(count):
                piece = jnp.exp2(scores[:, part * PAGE : (part + 1) * PAGE] * SCALE - top)
                total = total + piece
                pieces.append(piece.astype(jnp.bfloat16))
            weights = jnp.concatenate(pieces, axis=1) if count > 1 else pieces[0]
            maxima[...] = top.reshape(shape)
            totals[...] = total.reshape(shape)
            acc[item, sums] = acc[item, sums] * rescale.reshape(shape) + plain_dot(
                weights, values
            ).reshape(shape)

        whole = found // CHUNK
        left = found % CHUNK

        def step(index, carry):
            chunk(index * CHUNK, CHUNK)
            return carry

        lax.fori_loop(0, whole, step, 0)
        for count in range(1, CHUNK):

            @pl.when(left == count)
            def _(count=count):
                chunk(whole * CHUNK, count)

        def send(index):
            for each in range(items):

                @pl.when(item == each)
                def _(each=each):
                    out_copy(each, index).start()

        if not resume:
            send(0)
        terms = jnp.zeros((new_count, HD), jnp.float32)
        for head in range(GROUP):
            total = jnp.sum(totals[head], axis=1, keepdims=True)
            if resume:
                some = total > 0.0
                safe = jnp.where(some, total, 1.0)
                send_buf[item, head] = (acc[item, head] * (1.0 / safe)).astype(jnp.bfloat16)
                stat = jnp.where(some, maxima[head] + jnp.log2(safe), EMPTY)
                terms = split_stats(stat, 3 * head, lanes, terms)
            else:
                terms = split_stats(maxima[head], 3 * head, lanes, terms)
                terms = split_stats(total, TOTALS + 3 * head, lanes, terms)
        if resume:
            send_buf[item, GROUP] = terms.astype(jnp.bfloat16)
            send(0)
        else:
            acc[item, GROUP] = terms
        send(1)
        if copy_pool:

            @pl.when(item == 0)
            def _():
                for copy_in, copy_out in zip(pool_in, pool_out):
                    copy_in.wait()
                    copy_out.start()

        return carry

    lax.fori_loop(0, items, one_item, 0)
    for item in range(items):
        for index in range(2):
            out_copy(item, index).wait()
    for copy in pool_out:
        copy.wait()


def attend(
    me, tables, steps, asked, kv_heads, pool, pages_listed, capacity, takes, state=None, copy_pool=False
):
    requests, width, new_count = len(steps), len(kv_heads), asked[0].shape[0]
    items = requests * width
    resume = state is not None
    blocks = (GROUP + 1, new_count, HD)
    kind = jnp.bfloat16 if resume else jnp.float32
    out_shape = [jax.ShapeDtypeStruct((1,) + blocks, kind) for _ in range(items)]
    scratch = [
        pltpu.VMEM((items, GROUP, new_count, HD), jnp.bfloat16),
        pltpu.VMEM((requests, width, 2, capacity, PAGE, HD), jnp.bfloat16),
        pltpu.VMEM((items,) + blocks, jnp.float32),
        pltpu.VMEM((GROUP, new_count, HD), jnp.float32),
        pltpu.VMEM((GROUP, new_count, HD), jnp.float32),
        pltpu.SMEM((requests,), jnp.int32),
        pltpu.SemaphoreType.DMA((items, GROUP)),
        pltpu.SemaphoreType.DMA((requests, width, capacity)),
        pltpu.SemaphoreType.DMA((items, 2)),
    ]
    if resume:
        scratch.append(pltpu.VMEM((items,) + blocks, jnp.bfloat16))
    if copy_pool:
        out_shape.append(jax.ShapeDtypeStruct(pool.shape, pool.dtype))
        parts = next(part for part in (6, 3, 2, 1) if pool.shape[1] % part == 0)
        scratch += [pltpu.VMEM(pool.shape, pool.dtype), pltpu.SemaphoreType.DMA((2, parts))]
    plan = dict(
        steps=steps, kv_heads=kv_heads, pages_listed=pages_listed, copy_pool=copy_pool,
        resume=resume,
    )
    return pl.pallas_call(
        lambda *refs: attend_kernel(plan, refs),
        out_shape=out_shape,
        in_specs=[SMEM, SMEM] + [ANY] * (requests + resume + 1),
        out_specs=[ANY] * len(out_shape),
        scratch_shapes=scratch,
        compiler_params=pltpu.CompilerParams(vmem_limit_bytes=VMEM_LIMIT),
        cost_estimate=cost(takes),
    )(me, tables, *asked, *([state] if resume else []), pool)


def project_kernel(shards, holders, rank_ref, cos_ref, sin_ref, gain_ref, *refs):
    hidden_refs, weight_ref = refs[:shards], refs[shards]
    out_ref, features, gathered, feature_sem, weight_sem = refs[shards + 1 :]
    span = features.shape[2]
    depth, width = gathered.shape[0], gathered.shape[1] // 2
    groups = weight_sem.shape[0]
    rows = depth // (groups * holders)

    def copy(group, holder):
        return pltpu.make_async_copy(
            weight_ref.at[pl.ds((group * holders + holder) * rows, rows)],
            gathered.at[pl.ds((holder * groups + group) * rows, rows)],
            weight_sem.at[group, holder],
        )

    for step in range(shards):
        shard = lax.rem(rank_ref[0] + shards - step, shards)
        pltpu.make_async_copy(hidden_refs[step], features.at[shard], feature_sem.at[step]).start()
    for holder in range(holders):
        for group in range(groups):
            copy(group, holder).start()
    for step in range(shards):
        pltpu.make_async_copy(hidden_refs[step], features.at[0], feature_sem.at[step]).wait()
    raw = 0.0
    for shard in range(shards):
        for holder in range(holders):
            if holder * groups * rows // span == shard:
                for group in range(groups):
                    copy(group, holder).wait()
        raw = raw + plain_dot(features[shard], gathered[shard * span : (shard + 1) * span])
    columns = []
    for head in range(width // HD):
        one = raw[:, head * HD : (head + 1) * HD]
        mean = jnp.sum(one * one, axis=1, keepdims=True) * (1.0 / HD)
        one = one * lax.rsqrt(mean + 1e-06) * gain_ref[...]
        columns.append(one * cos_ref[...] + pltpu.roll(one, HD // 2, 1) * sin_ref[...])
    new_keys = jnp.concatenate(columns, axis=1) if len(columns) > 1 else columns[0]
    out_ref[0] = new_keys.astype(jnp.bfloat16)
    out_ref[1] = raw[:, width:].astype(jnp.bfloat16)


def project(rank, cos, sin, gain, hidden, weight, groups, holders):
    shards = len(hidden)
    new_count, span = hidden[0].shape
    vmem = pl.BlockSpec(memory_space=pltpu.VMEM)
    return pl.pallas_call(
        functools.partial(project_kernel, shards, holders),
        out_shape=jax.ShapeDtypeStruct((2, new_count, weight.shape[1] // 2), jnp.bfloat16),
        in_specs=[SMEM, vmem, vmem, vmem] + [ANY] * (shards + 1),
        out_specs=vmem,
        scratch_shapes=[
            pltpu.VMEM((shards, new_count, span), jnp.bfloat16),
            pltpu.VMEM(weight.shape, weight.dtype),
            pltpu.SemaphoreType.DMA((shards,)),
            pltpu.SemaphoreType.DMA((groups, holders)),
        ],
        compiler_params=pltpu.CompilerParams(vmem_limit_bytes=VMEM_LIMIT),
        cost_estimate=cost(0.2),
    )(rank, cos, sin, gain, *hidden, weight)


def final_kernel(parts, q_ref, fresh_ref, *refs):
    states, partials, out_ref = refs[:2], refs[2 : 2 + parts], refs[-1]
    new_count = q_ref.shape[0]
    row = lax.broadcasted_iota(jnp.int32, (new_count, new_count), 0)
    column = lax.broadcasted_iota(jnp.int32, (new_count, new_count), 1)
    heads = [slice(head * HD, (head + 1) * HD) for head in range(GROUP)]
    stacked = jnp.concatenate([q_ref[:, span] for span in heads], axis=0)
    scores = row_dot(stacked, fresh_ref[0]).reshape(GROUP, new_count, new_count)
    scores = jnp.where((column <= row)[None], scores * SCALE, EMPTY)
    extras = [ref[0, GROUP].astype(jnp.bfloat16) for ref in states]
    weights, shares, divisors = [], [], []
    for head in range(GROUP):
        stats = [state_stats(extra, head) for extra in extras]
        stats += [(joined_stats(partial[0, GROUP], 3 * head), 1.0) for partial in partials]
        top = jnp.broadcast_to(jnp.max(scores[head], axis=1, keepdims=True), (new_count, HD))
        for other, _ in stats:
            top = jnp.maximum(top, other)
        pieces = [
            jnp.exp2(scores[head, :, start : start + HD] - top) for start in range(0, new_count, HD)
        ]
        total = jnp.broadcast_to(jnp.sum(sum(pieces), axis=1, keepdims=True), (new_count, HD))
        shares.append([jnp.exp2(other - top) for other, _ in stats])
        for share, (_, part) in zip(shares[-1], stats):
            total = total + share * part
        divisors.append(total)
        weights.append(jnp.concatenate(pieces, axis=1).astype(jnp.bfloat16))
    sums = plain_dot(jnp.concatenate(weights, axis=0), fresh_ref[1]).reshape(GROUP, new_count, HD)
    for head, span in enumerate(heads):
        mixed = sums[head]
        for share, ref in zip(shares[head], states + partials):
            mixed = mixed + share * ref[0, head].astype(jnp.float32)
        out_ref[:, span] = (mixed / divisors[head]).astype(jnp.bfloat16)


def final(kv_head, queries, fresh, states, partials, before):
    new_count = queries.shape[0]
    blocks = (1, GROUP + 1, new_count, HD)
    given = [] if before is None else [before]
    return pl.pallas_call(
        functools.partial(final_kernel, len(partials)),
        grid=(1,),
        out_shape=jax.ShapeDtypeStruct(queries.shape, jnp.bfloat16),
        in_specs=[
            pl.BlockSpec((new_count, BLOCK), lambda step: (0, kv_head)),
            pl.BlockSpec((2, new_count, HD), lambda step: (0, 0, kv_head)),
        ]
        + [pl.BlockSpec(blocks, lambda step: (0, 0, 0, 0))] * (len(states) + len(partials))
        + [ANY] * len(given),
        out_specs=pl.BlockSpec((new_count, BLOCK), lambda step: (0, kv_head)),
        input_output_aliases={2 + len(states) + len(partials): 0} if given else {},
        compiler_params=pltpu.CompilerParams(vmem_limit_bytes=VMEM_LIMIT),
        cost_estimate=cost(0.2),
    )(queries, fresh, *states, *partials, *given)


def write_kernel(holders, new_pages, base, me_ref, table_ref, *refs):
    pages = refs[:holders]
    out_ref, sem = refs[holders + 1], refs[holders + 2]
    me = me_ref[0]

    def each(action):
        for holder in range(holders):
            for page in range(new_pages):

                @pl.when(table_ref[me ^ holder, base + page] == me)
                def _(holder=holder, page=page):
                    slot = table_ref[me ^ holder, base + new_pages + page]
                    copy = pltpu.make_async_copy(
                        pages[holder].at[:, pl.ds(page * PAGE, PAGE)],
                        out_ref.at[:, slot],
                        sem.at[holder, page],
                    )
                    getattr(copy, action)()

    each("start")
    each("wait")


def write(me, tables, fresh, pool, new_pages, base):
    holders = len(fresh)
    return pl.pallas_call(
        functools.partial(write_kernel, holders, new_pages, base),
        out_shape=jax.ShapeDtypeStruct(pool.shape, pool.dtype),
        in_specs=[SMEM, SMEM]
        + [pl.BlockSpec(memory_space=pltpu.VMEM)] * holders
        + [ANY],
        out_specs=ANY,
        input_output_aliases={2 + holders: 0},
        scratch_shapes=[pltpu.SemaphoreType.DMA((holders, new_pages))],
        compiler_params=pltpu.CompilerParams(vmem_limit_bytes=VMEM_LIMIT),
        cost_estimate=cost(0.2),
    )(me, tables, *fresh, pool)


def per_device(
    hidden,
    k_weight,
    v_weight,
    k_gain,
    queries,
    kv_pool,
    page_holder,
    page_slot,
    page_count,
    write_owner,
    write_slot,
):
    inst_count = lax.axis_size("inst")
    shards = lax.axis_size("tp")
    me = lax.axis_index("inst").astype(jnp.int32)
    rank = lax.axis_index("tp").astype(jnp.int32)
    groups = lax.axis_size("groups")
    group = lax.axis_index("groups").astype(jnp.int32)
    pages_listed = page_holder.shape[1]
    new_pages = write_owner.shape[1]
    capacity = 3 * pages_listed // (2 * inst_count)
    new_count = hidden.shape[0]
    kv_local = k_weight.shape[1] // HD
    me_list = me.reshape(1)

    def swap(array, step):
        return lax.ppermute(array, "inst", [(i, i ^ step) for i in range(inst_count)])

    def shift(array, step):
        return lax.ppermute(array, "tp", [(i, (i + step) % shards) for i in range(shards)])

    def after(array, *done):
        return lax.optimization_barrier((array,) + done)[0]

    heads = list(range(kv_local))
    base = 2 * pages_listed + 1
    own_table = jnp.concatenate(
        [page_holder[0], page_slot[0], page_count, write_owner[0], write_slot[0]]
    )
    own_table = jnp.pad(own_table, (0, 128 - own_table.shape[0]))[None]
    others = range(2, inst_count, 2)

    tables = lax.all_gather(own_table, "inst", axis=0, tiled=True)
    sent = after(queries, tables)
    asked = {0: queries, 1: swap(sent, 1)}
    for step in others:
        asked[step] = swap(sent, step)
    features = [hidden]
    forwarded = shards == 4
    for step in range(1, shards):
        direct = not forwarded or step != 2
        features.append(shift(after(hidden, tables), step) if direct else None)
    near = [features[1], features[-1]]
    share = k_weight.shape[0] // groups
    weight = jnp.concatenate(
        [lax.dynamic_slice_in_dim(one, group * share, share) for one in (k_weight, v_weight)],
        axis=1,
    )
    weight = lax.all_gather(after(weight, tables), ("groups", "inst"), axis=0, tiled=True)

    common = dict(pool=kv_pool, pages_listed=pages_listed, capacity=capacity)
    *found, pool_copy = attend(
        me_list, tables, [0, 1], [queries, asked[1]], heads, copy_pool=True, takes=22.0, **common
    )
    own_states, mate_states = found[:kv_local], found[kv_local:]
    last = mate_states[-1]

    frequency = 1000000.0 ** (-(jnp.arange(HD // 2, dtype=jnp.float32) * 2.0) / HD)
    positions = page_count[0] * PAGE + jnp.arange(new_count, dtype=jnp.int32)
    angles = positions.astype(jnp.float32)[:, None] * frequency[None, :]
    cosine, sine = jnp.cos(angles), jnp.sin(angles)
    partials = [[] for k in heads]
    fresh = None
    for step in others:
        asked[step + 1] = swap(after(asked[step], last, *near), 1)
        if forwarded and features[2] is None:
            ahead = lax.ppermute(after(features[1], last), "tp", [(1, 2), (2, 3)])
            back = lax.ppermute(after(features[3], last), "tp", [(1, 0), (2, 1)])
            features[2] = jnp.where(rank >= 2, ahead, back)
            near = [ahead, back]
        begun = attend(
            me_list, after(tables, last), [step + 1], [asked[step + 1]], heads, takes=12.0, **common
        )
        last = begun[-1]
        halves = [swap(after(state, *near), 1) for state in begun]
        if fresh is None:
            from_mate = [swap(after(state, last), 1) for state in mate_states]
            fresh = project(
                rank.reshape(1),
                jnp.concatenate([cosine, cosine], axis=1),
                jnp.concatenate([-sine, sine], axis=1),
                k_gain[None, :],
                [after(hidden, last)] + features[1:],
                weight,
                groups,
                inst_count,
            )
            last = fresh
            pages = {0: fresh, 1: swap(fresh, 1)}
            for apart in others:
                pages[apart] = swap(fresh, apart)
        for k in heads:
            sent_first = [pages[apart] for apart in others] if k > 0 else []
            (last,) = attend(
                me_list, after(tables, last, *sent_first), [step], [asked[step]], [k],
                state=halves[k], takes=0.2, **common,
            )
            partials[k].append(swap(last, step))

    attention_out = None
    for k in heads:
        attention_out = final(
            k, after(queries, last), fresh, [own_states[k], from_mate[k]], partials[k], attention_out
        )
    for step in others:
        pages[step + 1] = swap(after(pages[step], last), 1)
    new_pool = write(
        me_list,
        tables,
        [pages[step] for step in range(inst_count)],
        pool_copy,
        new_pages,
        base,
    )
    return (attention_out, new_pool)


def solution(mesh):
    return jax.shard_map(
        per_device,
        mesh=mesh,
        in_specs=(
            P(("groups", "inst"), "tp"),
            P("inst", "tp"),
            P("inst", "tp"),
            P(),
            P(("groups", "inst"), "tp"),
            P(None, ("groups", "inst"), None, "tp"),
            P(("groups", "inst"), None),
            P(("groups", "inst"), None),
            P(("groups", "inst")),
            P(("groups", "inst"), None),
            P(("groups", "inst"), None),
        ),
        out_specs=(P(("groups", "inst"), "tp"), P(None, ("groups", "inst"), None, "tp")),
        check_vma=False,
    )
```

```python
import functools
import math

import jax
import jax.numpy as jnp
from jax import lax
from jax.experimental import pallas as pl
from jax.experimental.pallas import tpu as pltpu
from jax.sharding import PartitionSpec as P

HD = 128
PAGE = 128
GROUP = 8
BLOCK = GROUP * HD
EXTRA = 128
TOTALS = 64
STATS = 32
EMPTY = -1e30
LOG2E = 1.4426950408889634
SCALE = LOG2E / math.sqrt(HD)
CHUNK = 8
REST = (4, 2, 1)
ANY = pl.BlockSpec(memory_space=pl.ANY)
SMEM = pl.BlockSpec(memory_space=pltpu.SMEM)
VMEM_LIMIT = 63 * 1024 * 1024


def cost(microseconds):
    return pl.CostEstimate(
        flops=int(microseconds * 1e9), bytes_accessed=int(microseconds * 3e6), transcendentals=0
    )


def row_dot(a, b):
    return lax.dot_general(a, b, (((1,), (1,)), ((), ())), preferred_element_type=jnp.float32)


def plain_dot(a, b):
    return lax.dot_general(a, b, (((1,), (0,)), ((), ())), preferred_element_type=jnp.float32)


def split_stats(stat, lane, lanes, terms):
    high = stat.astype(jnp.bfloat16).astype(jnp.float32)
    rest = stat - high
    middle = rest.astype(jnp.bfloat16).astype(jnp.float32)
    terms = jnp.where(lanes == lane, high, terms)
    terms = jnp.where(lanes == lane + 1, middle, terms)
    return jnp.where(lanes == lane + 2, rest - middle, terms)


def joined_stats(extra, lane):
    term = lax.broadcasted_iota(jnp.int32, (EXTRA, HD), 0)
    picked = jnp.where((term >= lane) & (term < lane + 3), 1.0, 0.0).astype(jnp.bfloat16)
    return plain_dot(extra, picked)


def turned_stats(turned, lane):
    term = lax.broadcasted_iota(jnp.int32, (STATS, HD), 0)
    picked = jnp.where((term >= lane) & (term < lane + 3), 1.0, 0.0).astype(jnp.bfloat16)
    return lax.dot_general(
        turned, picked, (((0,), (0,)), ((), ())), preferred_element_type=jnp.float32
    )


def state_stats(extra, head):
    return joined_stats(extra, 3 * head), joined_stats(extra, TOTALS + 3 * head)


def attend_kernel(plan, refs):
    steps, kv_heads, pages_listed = plan["steps"], plan["kv_heads"], plan["pages_listed"]
    requests = len(steps)
    copy_pool, resume = plan["copy_pool"], plan["resume"]
    width = len(kv_heads)
    items = requests * width
    refs = list(refs)
    me_ref, table_ref = refs.pop(0), refs.pop(0)
    q_refs = [refs.pop(0) for _ in range(requests)]
    state_ref = refs.pop(0) if resume else None
    pool_ref = refs.pop(0)
    out_refs = [refs.pop(0) for _ in range(items)]
    new_pool_ref = refs.pop(0) if copy_pool else None
    q_buf, q_two, kv_buf, acc, maxima, totals, slots, q_sem, kv_sem, out_sem = refs[:10]
    refs = refs[10:]
    if resume:
        send_buf = refs.pop(0)
    new_count = q_buf.shape[2]
    rows = GROUP * new_count
    shape = (GROUP, new_count, HD)
    lanes = lax.broadcasted_iota(jnp.int32, (new_count, HD), 1)

    def q_copies(item):
        offset = kv_heads[item % width] * BLOCK
        return [
            pltpu.make_async_copy(
                q_refs[item // width].at[:, pl.ds(offset + head * HD, HD)],
                q_buf.at[item, head],
                q_sem.at[item, head],
            )
            for head in range(GROUP)
        ]

    def page_copies(request, place, slot):
        return [
            pltpu.make_async_copy(
                pool_ref.at[:, slot, :, pl.ds(kv_head * HD, HD)],
                kv_buf.at[request, column, :, place],
                kv_sem.at[request, column, place],
            )
            for column, kv_head in enumerate(kv_heads)
        ]

    def out_copy(item, index):
        if resume:
            part = [pl.ds(0, rows), pl.ds(rows, send_buf.shape[1] - rows)][index]
            source, target = send_buf.at[item, part], out_refs[item].at[part]
        else:
            part = [pl.ds(0, GROUP), pl.ds(GROUP, 1)][index]
            source, target = acc.at[item, part], out_refs[item].at[0, part]
        return pltpu.make_async_copy(source, target, out_sem.at[item, index])

    for item in range(items):
        for copy in q_copies(item):
            copy.start()
    if resume:
        state_copy = pltpu.make_async_copy(state_ref, acc, out_sem.at[0, 0])
        state_copy.start()
    me = me_ref[0]
    for request, apart in enumerate(steps):
        whose = me ^ apart
        count = table_ref[whose, 2 * pages_listed]

        def look(page, found, request=request, whose=whose, count=count):
            mine = (page < count) & (table_ref[whose, page] == me)

            @pl.when(mine)
            def _():
                for copy in page_copies(request, found, table_ref[whose, pages_listed + page]):
                    copy.start()

            return found + mine.astype(jnp.int32)

        slots[request] = lax.fori_loop(0, count, look, 0)
    pool_in, pool_out = [], []
    if copy_pool:
        pool_buf, pool_sem = refs
        slot_total = pool_ref.shape[1]
        parts = pool_sem.shape[1]
        step = slot_total // parts
        for index in range(2):
            for part in range(parts):
                piece = (index, pl.ds(part * step, step))
                sem = pool_sem.at[index, part]
                pool_in.append(pltpu.make_async_copy(pool_ref.at[piece], pool_buf.at[piece], sem))
                pool_out.append(
                    pltpu.make_async_copy(pool_buf.at[piece], new_pool_ref.at[piece], sem)
                )
        for copy in pool_in:
            copy.start()
    for item in range(items):
        for copy in q_copies(item):
            copy.wait()
    if resume:
        state_copy.wait()

    def one_item(item, carry):
        request = item // width
        column = item % width
        found = slots[request]
        sums = pl.ds(0, GROUP)
        scaled = q_buf[item].reshape(rows, HD).astype(jnp.float32) * SCALE
        high = scaled.astype(jnp.bfloat16)
        q_two[:, :HD] = high
        q_two[:, HD:] = (scaled - high.astype(jnp.float32)).astype(jnp.bfloat16)
        if resume:
            extra = acc[item, GROUP].astype(jnp.bfloat16)
            for head in range(GROUP):
                maxima[head], total = state_stats(extra, head)
                totals[head] = jnp.where(lanes == 0, total, 0.0)
        else:
            acc[item, sums] = jnp.zeros(shape, jnp.float32)
            totals[...] = jnp.zeros(shape, jnp.float32)
            maxima[...] = jnp.full(shape, EMPTY, jnp.float32)

        @pl.when(column == 0)
        def _():
            def arrived(place, carry):
                for copy in page_copies(request, place, 0):
                    copy.wait()
                return carry

            lax.fori_loop(0, found, arrived, 0)

        def chunk(first, count):
            keys = kv_buf[request, column, 0, pl.ds(first, count)].reshape(count * PAGE, HD)
            values = kv_buf[request, column, 1, pl.ds(first, count)].reshape(count * PAGE, HD)
            scores = row_dot(q_two[...], jnp.concatenate([keys, keys], axis=1))
            old = maxima[...].reshape(rows, HD)
            top = jnp.maximum(old, jnp.max(scores, axis=1, keepdims=True))
            rescale = jnp.exp2(old - top)
            total = totals[...].reshape(rows, HD) * rescale
            pieces = []
            for part in range(count):
                piece = jnp.exp2(scores[:, part * PAGE : (part + 1) * PAGE] - top)
                total = total + piece
                pieces.append(piece.astype(jnp.bfloat16))
            weights = jnp.concatenate(pieces, axis=1) if count > 1 else pieces[0]
            maxima[...] = top.reshape(shape)
            totals[...] = total.reshape(shape)
            acc[item, sums] = acc[item, sums] * rescale.reshape(shape) + plain_dot(
                weights, values
            ).reshape(shape)

        whole = found // CHUNK
        left = found % CHUNK

        def step(index, carry):
            chunk(index * CHUNK, CHUNK)
            return carry

        lax.fori_loop(0, whole, step, 0)
        done = whole * CHUNK
        for count in REST:

            @pl.when((left & count) != 0)
            def _(count=count, done=done):
                chunk(done, count)

            done = done + (left & count)

        def send(index):
            for each in range(items):

                @pl.when(item == each)
                def _(each=each):
                    out_copy(each, index).start()

        if not resume:
            send(0)
        terms = jnp.zeros((new_count, HD), jnp.float32)
        for head in range(GROUP):
            total = jnp.sum(totals[head], axis=1, keepdims=True)
            if resume:
                some = total > 0.0
                safe = jnp.where(some, total, 1.0)
                send_buf[item, head * new_count : (head + 1) * new_count] = (
                    acc[item, head] * (1.0 / safe)
                ).astype(jnp.bfloat16)
                stat = jnp.where(some, maxima[head] + jnp.log2(safe), EMPTY)
                terms = split_stats(stat, 3 * head, lanes, terms)
            else:
                terms = split_stats(maxima[head], 3 * head, lanes, terms)
                terms = split_stats(total, TOTALS + 3 * head, lanes, terms)
        if resume:
            turned = terms.T[:STATS].astype(jnp.bfloat16)
            for piece in range(new_count // HD):
                send_buf[item, rows + piece * STATS : rows + (piece + 1) * STATS] = turned[
                    :, piece * HD : (piece + 1) * HD
                ]
            send(0)
        else:
            acc[item, GROUP] = terms
        send(1)
        if copy_pool:

            @pl.when(item == 0)
            def _():
                for copy_in, copy_out in zip(pool_in, pool_out):
                    copy_in.wait()
                    copy_out.start()

        return carry

    lax.fori_loop(0, items, one_item, 0)
    for item in range(items):
        for index in range(2):
            out_copy(item, index).wait()
    for copy in pool_out:
        copy.wait()


def attend(
    me, tables, steps, asked, kv_heads, pool, pages_listed, capacity, takes, state=None, copy_pool=False
):
    requests, width, new_count = len(steps), len(kv_heads), asked[0].shape[0]
    items = requests * width
    resume = state is not None
    blocks = (GROUP + 1, new_count, HD)
    parcel = (GROUP * new_count + STATS * new_count // HD, HD)
    if resume:
        out_shape = [jax.ShapeDtypeStruct(parcel, jnp.bfloat16) for _ in range(items)]
    else:
        out_shape = [jax.ShapeDtypeStruct((1,) + blocks, jnp.float32) for _ in range(items)]
    scratch = [
        pltpu.VMEM((items, GROUP, new_count, HD), jnp.bfloat16),
        pltpu.VMEM((GROUP * new_count, 2 * HD), jnp.bfloat16),
        pltpu.VMEM((requests, width, 2, capacity, PAGE, HD), jnp.bfloat16),
        pltpu.VMEM((items,) + blocks, jnp.float32),
        pltpu.VMEM((GROUP, new_count, HD), jnp.float32),
        pltpu.VMEM((GROUP, new_count, HD), jnp.float32),
        pltpu.SMEM((requests,), jnp.int32),
        pltpu.SemaphoreType.DMA((items, GROUP)),
        pltpu.SemaphoreType.DMA((requests, width, capacity)),
        pltpu.SemaphoreType.DMA((items, 2)),
    ]
    if resume:
        scratch.append(pltpu.VMEM((items,) + parcel, jnp.bfloat16))
    if copy_pool:
        out_shape.append(jax.ShapeDtypeStruct(pool.shape, pool.dtype))
        parts = next(part for part in (6, 3, 2, 1) if pool.shape[1] % part == 0)
        scratch += [pltpu.VMEM(pool.shape, pool.dtype), pltpu.SemaphoreType.DMA((2, parts))]
    plan = dict(
        steps=steps, kv_heads=kv_heads, pages_listed=pages_listed, copy_pool=copy_pool,
        resume=resume,
    )
    return pl.pallas_call(
        lambda *refs: attend_kernel(plan, refs),
        out_shape=out_shape,
        in_specs=[SMEM, SMEM] + [ANY] * (requests + resume + 1),
        out_specs=[ANY] * len(out_shape),
        scratch_shapes=scratch,
        compiler_params=pltpu.CompilerParams(vmem_limit_bytes=VMEM_LIMIT),
        cost_estimate=cost(takes),
    )(me, tables, *asked, *([state] if resume else []), pool)


def project_kernel(shards, forwarded, rank_ref, cos_ref, sin_ref, gain_ref, *refs):
    hidden_refs, weight_ref = refs[:-6], refs[-6]
    out_ref, features, gathered, feature_sem, weight_sem = refs[-5:]
    rank = rank_ref[0]
    span = features.shape[2]
    depth, width = gathered.shape[0], gathered.shape[1] // 2

    def copies(shard):
        return [
            pltpu.make_async_copy(
                weight_ref.at[pl.ds(kind * depth + shard * span, span)],
                gathered.at[pl.ds(shard * span, span), pl.ds(kind * width, width)],
                weight_sem.at[kind, shard],
            )
            for kind in range(2)
        ]

    def feature_copy(step, ref):
        shard = lax.rem(rank + shards - step, shards)
        return pltpu.make_async_copy(ref, features.at[shard], feature_sem.at[step])

    for step in range(shards):
        if forwarded and step == 2:
            @pl.when(rank >= 2)
            def _():
                feature_copy(2, hidden_refs[2]).start()

            @pl.when(rank < 2)
            def _():
                feature_copy(2, hidden_refs[shards]).start()

        else:
            feature_copy(step, hidden_refs[step]).start()
    for shard in range(shards):
        for copy in copies(shard):
            copy.start()
    for step in range(shards):
        feature_copy(step, hidden_refs[step]).wait()
    raw = 0.0
    for shard in range(shards):
        for copy in copies(shard):
            copy.wait()
        raw = raw + plain_dot(features[shard], gathered[shard * span : (shard + 1) * span])
    columns = []
    for head in range(width // HD):
        one = raw[:, head * HD : (head + 1) * HD]
        mean = jnp.sum(one * one, axis=1, keepdims=True) * (1.0 / HD)
        one = one * lax.rsqrt(mean + 1e-06) * gain_ref[...]
        columns.append(one * cos_ref[...] + pltpu.roll(one, HD // 2, 1) * sin_ref[...])
    new_keys = jnp.concatenate(columns, axis=1) if len(columns) > 1 else columns[0]
    out_ref[0] = new_keys.astype(jnp.bfloat16)
    out_ref[1] = raw[:, width:].astype(jnp.bfloat16)


def project(rank, cos, sin, gain, hidden, weight, shards):
    new_count, span = hidden[0].shape
    depth, width = weight.shape[0] // 2, weight.shape[1]
    vmem = pl.BlockSpec(memory_space=pltpu.VMEM)
    return pl.pallas_call(
        functools.partial(project_kernel, shards, len(hidden) > shards),
        out_shape=jax.ShapeDtypeStruct((2, new_count, width), jnp.bfloat16),
        in_specs=[SMEM, vmem, vmem, vmem] + [ANY] * (len(hidden) + 1),
        out_specs=vmem,
        scratch_shapes=[
            pltpu.VMEM((shards, new_count, span), jnp.bfloat16),
            pltpu.VMEM((depth, 2 * width), jnp.bfloat16),
            pltpu.SemaphoreType.DMA((shards,)),
            pltpu.SemaphoreType.DMA((2, shards)),
        ],
        compiler_params=pltpu.CompilerParams(vmem_limit_bytes=VMEM_LIMIT),
        cost_estimate=cost(0.2),
    )(rank, cos, sin, gain, *hidden, weight)


def final_kernel(parts, q_ref, fresh_ref, *refs):
    states, partials, out_ref = refs[:2], refs[2 : 2 + parts], refs[-1]
    new_count = q_ref.shape[0]
    rows = GROUP * new_count
    row = lax.broadcasted_iota(jnp.int32, (new_count, new_count), 0)
    column = lax.broadcasted_iota(jnp.int32, (new_count, new_count), 1)
    heads = [slice(head * HD, (head + 1) * HD) for head in range(GROUP)]
    stacked = jnp.concatenate([q_ref[:, span] for span in heads], axis=0)
    scores = row_dot(stacked, fresh_ref[0]).reshape(GROUP, new_count, new_count)
    scores = jnp.where((column <= row)[None], scores * SCALE, EMPTY)
    extras = [ref[0, GROUP].astype(jnp.bfloat16) for ref in states]
    turned = [
        jnp.concatenate(
            [partial[start : start + STATS] for start in range(rows, partial.shape[0], STATS)], axis=1
        )
        for partial in partials
    ]
    weights, shares, divisors = [], [], []
    for head in range(GROUP):
        stats = [state_stats(extra, head) for extra in extras]
        stats += [(turned_stats(part, 3 * head), 1.0) for part in turned]
        top = jnp.broadcast_to(jnp.max(scores[head], axis=1, keepdims=True), (new_count, HD))
        for other, _ in stats:
            top = jnp.maximum(top, other)
        pieces = [
            jnp.exp2(scores[head, :, start : start + HD] - top) for start in range(0, new_count, HD)
        ]
        total = jnp.broadcast_to(jnp.sum(sum(pieces), axis=1, keepdims=True), (new_count, HD))
        shares.append([jnp.exp2(other - top) for other, _ in stats])
        for share, (_, part) in zip(shares[-1], stats):
            total = total + share * part
        divisors.append(total)
        weights.append(jnp.concatenate(pieces, axis=1).astype(jnp.bfloat16))
    sums = plain_dot(jnp.concatenate(weights, axis=0), fresh_ref[1]).reshape(GROUP, new_count, HD)
    for head, span in enumerate(heads):
        mixed = sums[head]
        block = slice(head * new_count, (head + 1) * new_count)
        given = [ref[0, head] for ref in states] + [ref[block] for ref in partials]
        for share, part in zip(shares[head], given):
            mixed = mixed + share * part.astype(jnp.float32)
        out_ref[:, span] = (mixed / divisors[head]).astype(jnp.bfloat16)


def final(kv_head, queries, fresh, states, partials, before):
    new_count = queries.shape[0]
    blocks = (1, GROUP + 1, new_count, HD)
    given = [] if before is None else [before]
    return pl.pallas_call(
        functools.partial(final_kernel, len(partials)),
        grid=(1,),
        out_shape=jax.ShapeDtypeStruct(queries.shape, jnp.bfloat16),
        in_specs=[
            pl.BlockSpec((new_count, BLOCK), lambda step: (0, kv_head)),
            pl.BlockSpec((2, new_count, HD), lambda step: (0, 0, kv_head)),
        ]
        + [pl.BlockSpec(blocks, lambda step: (0, 0, 0, 0))] * len(states)
        + [pl.BlockSpec(partial.shape, lambda step: (0, 0)) for partial in partials]
        + [ANY] * len(given),
        out_specs=pl.BlockSpec((new_count, BLOCK), lambda step: (0, kv_head)),
        input_output_aliases={2 + len(states) + len(partials): 0} if given else {},
        compiler_params=pltpu.CompilerParams(vmem_limit_bytes=VMEM_LIMIT),
        cost_estimate=cost(0.2),
    )(queries, fresh, *states, *partials, *given)


def write_kernel(holders, new_pages, base, me_ref, table_ref, *refs):
    pages = refs[:holders]
    out_ref, sem = refs[holders + 1], refs[holders + 2]
    me = me_ref[0]

    def each(action):
        for holder in range(holders):
            for page in range(new_pages):

                @pl.when(table_ref[me ^ holder, base + page] == me)
                def _(holder=holder, page=page):
                    slot = table_ref[me ^ holder, base + new_pages + page]
                    copy = pltpu.make_async_copy(
                        pages[holder].at[:, pl.ds(page * PAGE, PAGE)],
                        out_ref.at[:, slot],
                        sem.at[holder, page],
                    )
                    getattr(copy, action)()

    each("start")
    each("wait")


def write(me, tables, fresh, pool, new_pages, base):
    holders = len(fresh)
    return pl.pallas_call(
        functools.partial(write_kernel, holders, new_pages, base),
        out_shape=jax.ShapeDtypeStruct(pool.shape, pool.dtype),
        in_specs=[SMEM, SMEM]
        + [pl.BlockSpec(memory_space=pltpu.VMEM)] * holders
        + [ANY],
        out_specs=ANY,
        input_output_aliases={2 + holders: 0},
        scratch_shapes=[pltpu.SemaphoreType.DMA((holders, new_pages))],
        compiler_params=pltpu.CompilerParams(vmem_limit_bytes=8 * 1024 * 1024),
        cost_estimate=cost(0.2),
    )(me, tables, *fresh, pool)


def per_device(
    hidden,
    k_weight,
    v_weight,
    k_gain,
    queries,
    kv_pool,
    page_holder,
    page_slot,
    page_count,
    write_owner,
    write_slot,
):
    inst_count = lax.axis_size("inst")
    shards = lax.axis_size("tp")
    me = lax.axis_index("inst").astype(jnp.int32)
    rank = lax.axis_index("tp").astype(jnp.int32)
    groups = lax.axis_size("groups")
    group = lax.axis_index("groups").astype(jnp.int32)
    pages_listed = page_holder.shape[1]
    new_pages = write_owner.shape[1]
    capacity = 3 * pages_listed // (2 * inst_count)
    new_count = hidden.shape[0]
    kv_local = k_weight.shape[1] // HD
    me_list = me.reshape(1)

    def swap(array, step):
        return lax.ppermute(array, "inst", [(i, i ^ step) for i in range(inst_count)])

    def shift(array, step):
        return lax.ppermute(array, "tp", [(i, (i + step) % shards) for i in range(shards)])

    def after(array, *done):
        return lax.optimization_barrier((array,) + done)[0]

    heads = list(range(kv_local))
    base = 2 * pages_listed + 1
    own_table = jnp.concatenate(
        [page_holder[0], page_slot[0], page_count, write_owner[0], write_slot[0]]
    )
    own_table = jnp.pad(own_table, (0, 128 - own_table.shape[0]))[None]
    others = range(2, inst_count, 2)

    tables = lax.all_gather(own_table, "inst", axis=0, tiled=True)
    sent = after(queries, tables)
    asked = {0: queries, 1: swap(sent, 1)}
    for step in others:
        asked[step] = swap(sent, step)
    features = [hidden]
    forwarded = shards == 4
    for step in range(1, shards):
        direct = not forwarded or step != 2
        features.append(shift(after(hidden, tables), step) if direct else None)
    near = [features[1], features[-1]]
    if groups == 2:
        chosen = jnp.where(group == 0, k_weight, v_weight)
        weight = lax.all_gather(after(chosen, tables), ("groups", "inst"), axis=0, tiled=True)
    else:
        weight = jnp.concatenate(
            [lax.all_gather(one, "inst", axis=0, tiled=True) for one in (k_weight, v_weight)]
        )

    common = dict(pool=kv_pool, pages_listed=pages_listed, capacity=capacity)
    *found, pool_copy = attend(
        me_list, tables, [0, 1], [queries, asked[1]], heads, copy_pool=True, takes=22.0, **common
    )
    own_states, mate_states = found[:kv_local], found[kv_local:]
    last = mate_states[-1]

    frequency = 1000000.0 ** (-(jnp.arange(HD // 2, dtype=jnp.float32) * 2.0) / HD)
    positions = page_count[0] * PAGE + jnp.arange(new_count, dtype=jnp.int32)
    angles = positions.astype(jnp.float32)[:, None] * frequency[None, :]
    cosine, sine = jnp.cos(angles), jnp.sin(angles)
    cosine = jnp.concatenate([cosine, cosine], axis=1)
    sine = jnp.concatenate([-sine, sine], axis=1)
    partials = [[] for k in heads]
    fresh = None
    for step in others:
        asked[step + 1] = swap(after(asked[step], last, *near), 1)
        if forwarded and features[2] is None:
            ahead = lax.ppermute(after(features[1], last), "tp", [(1, 2), (2, 3)])
            back = lax.ppermute(after(features[3], last), "tp", [(1, 0), (2, 1)])
            features[2] = ahead
            features.append(back)
            near = [ahead, back]
        begun = attend(
            me_list, after(tables, last, cosine, sine), [step + 1], [asked[step + 1]], heads,
            takes=12.0, **common
        )
        last = begun[-1]
        halves = [swap(after(state, *near), 1) for state in begun]
        if fresh is None:
            from_mate = [swap(after(state, last), 1) for state in mate_states]
            fresh = project(
                rank.reshape(1),
                cosine,
                sine,
                k_gain[None, :],
                [after(hidden, last)] + features[1:],
                weight,
                shards,
            )
            last = fresh
            pages = {0: fresh, 1: swap(fresh, 1)}
            for apart in others:
                pages[apart] = swap(fresh, apart)
        for k in heads:
            sent_first = [pages[apart] for apart in others] if k > 0 else []
            (last,) = attend(
                me_list, after(tables, last, *sent_first), [step], [asked[step]], [k],
                state=halves[k], takes=0.2, **common,
            )
            partials[k].append(swap(last, step))

    attention_out = None
    for k in heads:
        attention_out = final(
            k, after(queries, last), fresh, [own_states[k], from_mate[k]], partials[k], attention_out
        )
    for step in others:
        pages[step + 1] = swap(after(pages[step], last), 1)
    new_pool = write(
        me_list,
        tables,
        [pages[step] for step in range(inst_count)],
        pool_copy,
        new_pages,
        base,
    )
    return (attention_out, new_pool)


def solution(mesh):
    return jax.shard_map(
        per_device,
        mesh=mesh,
        in_specs=(
            P(("groups", "inst"), "tp"),
            P("inst", "tp"),
            P("inst", "tp"),
            P(),
            P(("groups", "inst"), "tp"),
            P(None, ("groups", "inst"), None, "tp"),
            P(("groups", "inst"), None),
            P(("groups", "inst"), None),
            P(("groups", "inst")),
            P(("groups", "inst"), None),
            P(("groups", "inst"), None),
        ),
        out_specs=(P(("groups", "inst"), "tp"), P(None, ("groups", "inst"), None, "tp")),
        check_vma=False,
    )
```

```python
import functools
import math

import jax
import jax.numpy as jnp
from jax import lax
from jax.experimental import pallas as pl
from jax.experimental.pallas import tpu as pltpu
from jax.sharding import PartitionSpec as P

HD = 128
PAGE = 128
GROUP = 8
BLOCK = GROUP * HD
EXTRA = 128
TOTALS = 64
STATS = 32
EMPTY = -1e30
LOG2E = 1.4426950408889634
SCALE = LOG2E / math.sqrt(HD)
CHUNK = 8
REST = (4, 2, 1)
ANY = pl.BlockSpec(memory_space=pl.ANY)
SMEM = pl.BlockSpec(memory_space=pltpu.SMEM)
VMEM_LIMIT = 63 * 1024 * 1024


def cost(microseconds):
    return pl.CostEstimate(
        flops=int(microseconds * 1e9), bytes_accessed=int(microseconds * 3e6), transcendentals=0
    )


def row_dot(a, b):
    return lax.dot_general(a, b, (((1,), (1,)), ((), ())), preferred_element_type=jnp.float32)


def plain_dot(a, b):
    return lax.dot_general(a, b, (((1,), (0,)), ((), ())), preferred_element_type=jnp.float32)


def split_stats(stat, lane, lanes, terms):
    high = stat.astype(jnp.bfloat16).astype(jnp.float32)
    rest = stat - high
    middle = rest.astype(jnp.bfloat16).astype(jnp.float32)
    terms = jnp.where(lanes == lane, high, terms)
    terms = jnp.where(lanes == lane + 1, middle, terms)
    return jnp.where(lanes == lane + 2, rest - middle, terms)


def joined_stats(extra, lane):
    term = lax.broadcasted_iota(jnp.int32, (EXTRA, HD), 0)
    picked = jnp.where((term >= lane) & (term < lane + 3), 1.0, 0.0).astype(jnp.bfloat16)
    return plain_dot(extra, picked)


def turned_stats(turned, lane):
    term = lax.broadcasted_iota(jnp.int32, (STATS, HD), 0)
    picked = jnp.where((term >= lane) & (term < lane + 3), 1.0, 0.0).astype(jnp.bfloat16)
    return lax.dot_general(
        turned, picked, (((0,), (0,)), ((), ())), preferred_element_type=jnp.float32
    )


def state_stats(extra, head):
    return joined_stats(extra, 3 * head), joined_stats(extra, TOTALS + 3 * head)


def attend_kernel(plan, refs):
    wanted, pages_listed, copy_pool = plan["wanted"], plan["pages_listed"], plan["copy_pool"]
    items = len(wanted)
    refs = list(refs)
    me_ref, table_ref = refs.pop(0), refs.pop(0)
    q_refs = [refs.pop(0) for _ in range(items)]
    pool_ref = refs.pop(0)
    out_refs = [refs.pop(0) for _ in range(items)]
    new_pool_ref = refs.pop(0) if copy_pool else None
    q_buf, q_two, kv_buf, acc, maxima, totals, slots, q_sem, kv_sem, out_sem = refs[:10]
    refs = refs[10:]
    new_count = q_buf.shape[2]
    rows = GROUP * new_count
    shape = (GROUP, new_count, HD)
    sums = pl.ds(0, GROUP)
    lanes = lax.broadcasted_iota(jnp.int32, (new_count, HD), 1)

    def q_copies(item):
        offset = wanted[item][1] * BLOCK
        return [
            pltpu.make_async_copy(
                q_refs[item].at[:, pl.ds(offset + head * HD, HD)],
                q_buf.at[item, head],
                q_sem.at[item, head],
            )
            for head in range(GROUP)
        ]

    def page_copy(item, kv_head, place, slot):
        return pltpu.make_async_copy(
            pool_ref.at[:, slot, :, pl.ds(kv_head * HD, HD)],
            kv_buf.at[item, :, place],
            kv_sem.at[item, place],
        )

    def out_copy(item, index):
        part = [sums, pl.ds(GROUP, 1)][index]
        return pltpu.make_async_copy(
            acc.at[item, part], out_refs[item].at[0, part], out_sem.at[item, index]
        )

    for item in range(items):
        for copy in q_copies(item):
            copy.start()
    me = me_ref[0]
    for item, (apart, kv_head) in enumerate(wanted):
        whose = me ^ apart
        count = table_ref[whose, 2 * pages_listed]

        def look(page, found, item=item, kv_head=kv_head, whose=whose, count=count):
            mine = (page < count) & (table_ref[whose, page] == me)

            @pl.when(mine)
            def _():
                page_copy(item, kv_head, found, table_ref[whose, pages_listed + page]).start()

            return found + mine.astype(jnp.int32)

        slots[item] = lax.fori_loop(0, count, look, 0)
    pool_in, pool_out = [], []
    if copy_pool:
        pool_buf, pool_sem = refs
        slot_total = pool_ref.shape[1]
        parts = pool_sem.shape[1]
        step = slot_total // parts
        for index in range(2):
            for part in range(parts):
                piece = (index, pl.ds(part * step, step))
                sem = pool_sem.at[index, part]
                pool_in.append(pltpu.make_async_copy(pool_ref.at[piece], pool_buf.at[piece], sem))
                pool_out.append(
                    pltpu.make_async_copy(pool_buf.at[piece], new_pool_ref.at[piece], sem)
                )
        for copy in pool_in:
            copy.start()
    for item in range(items):
        for copy in q_copies(item):
            copy.wait()

    def one_item(item, carry):
        found = slots[item]
        scaled = q_buf[item].reshape(rows, HD).astype(jnp.float32) * SCALE
        high = scaled.astype(jnp.bfloat16)
        q_two[:, :HD] = high
        q_two[:, HD:] = (scaled - high.astype(jnp.float32)).astype(jnp.bfloat16)
        acc[item, sums] = jnp.zeros(shape, jnp.float32)
        totals[...] = jnp.zeros(shape, jnp.float32)
        maxima[...] = jnp.full(shape, EMPTY, jnp.float32)

        def arrived(place, carry):
            page_copy(item, 0, place, 0).wait()
            return carry

        lax.fori_loop(0, found, arrived, 0)

        def chunk(first, count):
            keys = kv_buf[item, 0, pl.ds(first, count)].reshape(count * PAGE, HD)
            values = kv_buf[item, 1, pl.ds(first, count)].reshape(count * PAGE, HD)
            scores = row_dot(q_two[...], jnp.concatenate([keys, keys], axis=1))
            old = maxima[...].reshape(rows, HD)
            top = jnp.maximum(old, jnp.max(scores, axis=1, keepdims=True))
            rescale = jnp.exp2(old - top)
            total = totals[...].reshape(rows, HD) * rescale
            pieces = []
            for part in range(count):
                piece = jnp.exp2(scores[:, part * PAGE : (part + 1) * PAGE] - top)
                total = total + piece
                pieces.append(piece.astype(jnp.bfloat16))
            weights = jnp.concatenate(pieces, axis=1) if count > 1 else pieces[0]
            maxima[...] = top.reshape(shape)
            totals[...] = total.reshape(shape)
            acc[item, sums] = acc[item, sums] * rescale.reshape(shape) + plain_dot(
                weights, values
            ).reshape(shape)

        whole = found // CHUNK
        left = found % CHUNK

        def step(index, carry):
            chunk(index * CHUNK, CHUNK)
            return carry

        lax.fori_loop(0, whole, step, 0)
        done = whole * CHUNK
        for count in REST:

            @pl.when((left & count) != 0)
            def _(count=count, done=done):
                chunk(done, count)

            done = done + (left & count)

        def send(index):
            for each in range(items):

                @pl.when(item == each)
                def _(each=each):
                    out_copy(each, index).start()

        send(0)
        terms = jnp.zeros((new_count, HD), jnp.float32)
        for head in range(GROUP):
            total = jnp.sum(totals[head], axis=1, keepdims=True)
            terms = split_stats(maxima[head], 3 * head, lanes, terms)
            terms = split_stats(total, TOTALS + 3 * head, lanes, terms)
        acc[item, GROUP] = terms
        send(1)
        if copy_pool:

            @pl.when(item == 0)
            def _():
                for copy_in, copy_out in zip(pool_in, pool_out):
                    copy_in.wait()
                    copy_out.start()

        return carry

    lax.fori_loop(0, items, one_item, 0)
    for item in range(items):
        for index in range(2):
            out_copy(item, index).wait()
    for copy in pool_out:
        copy.wait()


def attend(me, tables, wanted, asked, pool, pages_listed, capacity, takes, copy_pool=False):
    items, new_count = len(wanted), asked[0].shape[0]
    blocks = (GROUP + 1, new_count, HD)
    out_shape = [jax.ShapeDtypeStruct((1,) + blocks, jnp.float32) for _ in range(items)]
    scratch = [
        pltpu.VMEM((items, GROUP, new_count, HD), jnp.bfloat16),
        pltpu.VMEM((GROUP * new_count, 2 * HD), jnp.bfloat16),
        pltpu.VMEM((items, 2, capacity, PAGE, HD), jnp.bfloat16),
        pltpu.VMEM((items,) + blocks, jnp.float32),
        pltpu.VMEM((GROUP, new_count, HD), jnp.float32),
        pltpu.VMEM((GROUP, new_count, HD), jnp.float32),
        pltpu.SMEM((items,), jnp.int32),
        pltpu.SemaphoreType.DMA((items, GROUP)),
        pltpu.SemaphoreType.DMA((items, capacity)),
        pltpu.SemaphoreType.DMA((items, 2)),
    ]
    if copy_pool:
        out_shape.append(jax.ShapeDtypeStruct(pool.shape, pool.dtype))
        parts = next(part for part in (6, 3, 2, 1) if pool.shape[1] % part == 0)
        scratch += [pltpu.VMEM(pool.shape, pool.dtype), pltpu.SemaphoreType.DMA((2, parts))]
    plan = dict(wanted=wanted, pages_listed=pages_listed, copy_pool=copy_pool)
    return pl.pallas_call(
        lambda *refs: attend_kernel(plan, refs),
        out_shape=out_shape,
        in_specs=[SMEM, SMEM] + [ANY] * (items + 1),
        out_specs=[ANY] * len(out_shape),
        scratch_shapes=scratch,
        compiler_params=pltpu.CompilerParams(vmem_limit_bytes=VMEM_LIMIT),
        cost_estimate=cost(takes),
    )(me, tables, *[asked[step] for step, _ in wanted], pool)


def merge_kernel(a_ref, b_ref, out_ref):
    new_count = a_ref.shape[2]
    rows = GROUP * new_count
    lanes = lax.broadcasted_iota(jnp.int32, (new_count, HD), 1)
    extra_a, extra_b = [ref[0, GROUP].astype(jnp.bfloat16) for ref in (a_ref, b_ref)]
    terms = jnp.zeros((new_count, HD), jnp.float32)
    for head in range(GROUP):
        top_a, total_a = state_stats(extra_a, head)
        top_b, total_b = state_stats(extra_b, head)
        top = jnp.maximum(top_a, top_b)
        share_a, share_b = jnp.exp2(top_a - top), jnp.exp2(top_b - top)
        total = share_a * total_a + share_b * total_b
        some = total > 0.0
        safe = jnp.where(some, total, 1.0)
        mixed = (share_a * a_ref[0, head] + share_b * b_ref[0, head]) * (1.0 / safe)
        out_ref[head * new_count : (head + 1) * new_count] = mixed.astype(jnp.bfloat16)
        stat = jnp.where(some, top + jnp.log2(safe), EMPTY)
        terms = split_stats(stat, 3 * head, lanes, terms)
    turned = terms.T[:STATS].astype(jnp.bfloat16)
    for piece in range(new_count // HD):
        out_ref[rows + piece * STATS : rows + (piece + 1) * STATS] = turned[
            :, piece * HD : (piece + 1) * HD
        ]


def merge(a, b):
    new_count = a.shape[2]
    parcel = (GROUP * new_count + STATS * new_count // HD, HD)
    return pl.pallas_call(
        merge_kernel,
        out_shape=jax.ShapeDtypeStruct(parcel, jnp.bfloat16),
        compiler_params=pltpu.CompilerParams(vmem_limit_bytes=VMEM_LIMIT),
        cost_estimate=cost(0.2),
    )(a, b)


def project_kernel(shards, forwarded, rank_ref, cos_ref, sin_ref, gain_ref, *refs):
    hidden_refs, weight_ref = refs[:-6], refs[-6]
    out_ref, features, gathered, feature_sem, weight_sem = refs[-5:]
    rank = rank_ref[0]
    span = features.shape[2]
    depth, width = gathered.shape[0], gathered.shape[1] // 2

    def copies(shard):
        return [
            pltpu.make_async_copy(
                weight_ref.at[pl.ds(kind * depth + shard * span, span)],
                gathered.at[pl.ds(shard * span, span), pl.ds(kind * width, width)],
                weight_sem.at[kind, shard],
            )
            for kind in range(2)
        ]

    def feature_copy(step, ref):
        shard = lax.rem(rank + shards - step, shards)
        return pltpu.make_async_copy(ref, features.at[shard], feature_sem.at[step])

    for step in range(shards):
        if forwarded and step == 2:
            @pl.when(rank >= 2)
            def _():
                feature_copy(2, hidden_refs[2]).start()

            @pl.when(rank < 2)
            def _():
                feature_copy(2, hidden_refs[shards]).start()

        else:
            feature_copy(step, hidden_refs[step]).start()
    for shard in range(shards):
        for copy in copies(shard):
            copy.start()
    for step in range(shards):
        feature_copy(step, hidden_refs[step]).wait()
    raw = 0.0
    for shard in range(shards):
        for copy in copies(shard):
            copy.wait()
        raw = raw + plain_dot(features[shard], gathered[shard * span : (shard + 1) * span])
    columns = []
    for head in range(width // HD):
        one = raw[:, head * HD : (head + 1) * HD]
        mean = jnp.sum(one * one, axis=1, keepdims=True) * (1.0 / HD)
        one = one * lax.rsqrt(mean + 1e-06) * gain_ref[...]
        columns.append(one * cos_ref[...] + pltpu.roll(one, HD // 2, 1) * sin_ref[...])
    new_keys = jnp.concatenate(columns, axis=1) if len(columns) > 1 else columns[0]
    out_ref[0] = new_keys.astype(jnp.bfloat16)
    out_ref[1] = raw[:, width:].astype(jnp.bfloat16)


def project(rank, cos, sin, gain, hidden, weight, shards):
    new_count, span = hidden[0].shape
    depth, width = weight.shape[0] // 2, weight.shape[1]
    vmem = pl.BlockSpec(memory_space=pltpu.VMEM)
    return pl.pallas_call(
        functools.partial(project_kernel, shards, len(hidden) > shards),
        out_shape=jax.ShapeDtypeStruct((2, new_count, width), jnp.bfloat16),
        in_specs=[SMEM, vmem, vmem, vmem] + [ANY] * (len(hidden) + 1),
        out_specs=vmem,
        scratch_shapes=[
            pltpu.VMEM((shards, new_count, span), jnp.bfloat16),
            pltpu.VMEM((depth, 2 * width), jnp.bfloat16),
            pltpu.SemaphoreType.DMA((shards,)),
            pltpu.SemaphoreType.DMA((2, shards)),
        ],
        compiler_params=pltpu.CompilerParams(vmem_limit_bytes=VMEM_LIMIT),
        cost_estimate=cost(0.2),
    )(rank, cos, sin, gain, *hidden, weight)


def final_kernel(parts, q_ref, fresh_ref, *refs):
    states, partials, out_ref = refs[:2], refs[2 : 2 + parts], refs[-1]
    new_count = q_ref.shape[0]
    rows = GROUP * new_count
    row = lax.broadcasted_iota(jnp.int32, (new_count, new_count), 0)
    column = lax.broadcasted_iota(jnp.int32, (new_count, new_count), 1)
    heads = [slice(head * HD, (head + 1) * HD) for head in range(GROUP)]
    stacked = jnp.concatenate([q_ref[:, span] for span in heads], axis=0)
    scores = row_dot(stacked, fresh_ref[0]).reshape(GROUP, new_count, new_count)
    scores = jnp.where((column <= row)[None], scores * SCALE, EMPTY)
    extras = [ref[0, GROUP].astype(jnp.bfloat16) for ref in states]
    turned = [
        jnp.concatenate(
            [partial[start : start + STATS] for start in range(rows, partial.shape[0], STATS)], axis=1
        )
        for partial in partials
    ]
    weights, shares, divisors = [], [], []
    for head in range(GROUP):
        stats = [state_stats(extra, head) for extra in extras]
        stats += [(turned_stats(part, 3 * head), 1.0) for part in turned]
        top = jnp.broadcast_to(jnp.max(scores[head], axis=1, keepdims=True), (new_count, HD))
        for other, _ in stats:
            top = jnp.maximum(top, other)
        pieces = [
            jnp.exp2(scores[head, :, start : start + HD] - top) for start in range(0, new_count, HD)
        ]
        total = jnp.broadcast_to(jnp.sum(sum(pieces), axis=1, keepdims=True), (new_count, HD))
        shares.append([jnp.exp2(other - top) for other, _ in stats])
        for share, (_, part) in zip(shares[-1], stats):
            total = total + share * part
        divisors.append(total)
        weights.append(jnp.concatenate(pieces, axis=1).astype(jnp.bfloat16))
    sums = plain_dot(jnp.concatenate(weights, axis=0), fresh_ref[1]).reshape(GROUP, new_count, HD)
    for head, span in enumerate(heads):
        mixed = sums[head]
        block = slice(head * new_count, (head + 1) * new_count)
        given = [ref[0, head] for ref in states] + [ref[block] for ref in partials]
        for share, part in zip(shares[head], given):
            mixed = mixed + share * part.astype(jnp.float32)
        out_ref[:, span] = (mixed / divisors[head]).astype(jnp.bfloat16)


def final(kv_head, queries, fresh, states, partials, before):
    new_count = queries.shape[0]
    blocks = (1, GROUP + 1, new_count, HD)
    given = [] if before is None else [before]
    return pl.pallas_call(
        functools.partial(final_kernel, len(partials)),
        grid=(1,),
        out_shape=jax.ShapeDtypeStruct(queries.shape, jnp.bfloat16),
        in_specs=[
            pl.BlockSpec((new_count, BLOCK), lambda step: (0, kv_head)),
            pl.BlockSpec((2, new_count, HD), lambda step: (0, 0, kv_head)),
        ]
        + [pl.BlockSpec(blocks, lambda step: (0, 0, 0, 0))] * len(states)
        + [pl.BlockSpec(partial.shape, lambda step: (0, 0)) for partial in partials]
        + [ANY] * len(given),
        out_specs=pl.BlockSpec((new_count, BLOCK), lambda step: (0, kv_head)),
        input_output_aliases={2 + len(states) + len(partials): 0} if given else {},
        compiler_params=pltpu.CompilerParams(vmem_limit_bytes=VMEM_LIMIT),
        cost_estimate=cost(0.2),
    )(queries, fresh, *states, *partials, *given)


def write_kernel(holders, new_pages, base, me_ref, table_ref, *refs):
    pages = refs[:holders]
    out_ref, sem = refs[holders + 1], refs[holders + 2]
    me = me_ref[0]

    def each(action):
        for holder in range(holders):
            for page in range(new_pages):

                @pl.when(table_ref[me ^ holder, base + page] == me)
                def _(holder=holder, page=page):
                    slot = table_ref[me ^ holder, base + new_pages + page]
                    copy = pltpu.make_async_copy(
                        pages[holder].at[:, pl.ds(page * PAGE, PAGE)],
                        out_ref.at[:, slot],
                        sem.at[holder, page],
                    )
                    getattr(copy, action)()

    each("start")
    each("wait")


def write(me, tables, fresh, pool, new_pages, base):
    holders = len(fresh)
    return pl.pallas_call(
        functools.partial(write_kernel, holders, new_pages, base),
        out_shape=jax.ShapeDtypeStruct(pool.shape, pool.dtype),
        in_specs=[SMEM, SMEM]
        + [pl.BlockSpec(memory_space=pltpu.VMEM)] * holders
        + [ANY],
        out_specs=ANY,
        input_output_aliases={2 + holders: 0},
        scratch_shapes=[pltpu.SemaphoreType.DMA((holders, new_pages))],
        compiler_params=pltpu.CompilerParams(vmem_limit_bytes=8 * 1024 * 1024),
        cost_estimate=cost(0.2),
    )(me, tables, *fresh, pool)


def per_device(
    hidden,
    k_weight,
    v_weight,
    k_gain,
    queries,
    kv_pool,
    page_holder,
    page_slot,
    page_count,
    write_owner,
    write_slot,
):
    inst_count = lax.axis_size("inst")
    shards = lax.axis_size("tp")
    me = lax.axis_index("inst").astype(jnp.int32)
    rank = lax.axis_index("tp").astype(jnp.int32)
    groups = lax.axis_size("groups")
    group = lax.axis_index("groups").astype(jnp.int32)
    pages_listed = page_holder.shape[1]
    new_pages = write_owner.shape[1]
    capacity = 3 * pages_listed // (2 * inst_count)
    new_count = hidden.shape[0]
    kv_local = k_weight.shape[1] // HD
    me_list = me.reshape(1)

    def swap(array, step):
        return lax.ppermute(array, "inst", [(i, i ^ step) for i in range(inst_count)])

    def shift(array, step):
        return lax.ppermute(array, "tp", [(i, (i + step) % shards) for i in range(shards)])

    def after(array, *done):
        return lax.optimization_barrier((array,) + done)[0]

    heads = list(range(kv_local))
    base = 2 * pages_listed + 1
    own_table = jnp.concatenate(
        [page_holder[0], page_slot[0], page_count, write_owner[0], write_slot[0]]
    )
    own_table = jnp.pad(own_table, (0, 128 - own_table.shape[0]))[None]
    others = range(2, inst_count, 2)

    tables = lax.all_gather(own_table, "inst", axis=0, tiled=True)
    sent = after(queries, tables)
    asked = {0: queries, 1: swap(sent, 1)}
    for step in others:
        asked[step] = swap(sent, step)
    features = [hidden]
    forwarded = shards == 4
    for step in range(1, shards):
        direct = not forwarded or step != 2
        features.append(shift(after(hidden, tables), step) if direct else None)
    near = [features[1], features[-1]]
    if groups == 2:
        chosen = jnp.where(group == 0, k_weight, v_weight)
        weight = lax.all_gather(after(chosen, tables), ("groups", "inst"), axis=0, tiled=True)
    else:
        weight = jnp.concatenate(
            [lax.all_gather(one, "inst", axis=0, tiled=True) for one in (k_weight, v_weight)]
        )

    common = dict(asked=asked, pool=kv_pool, pages_listed=pages_listed, capacity=capacity)
    *found, pool_copy = attend(
        me_list, tables, [(step, k) for step in (0, 1) for k in heads], copy_pool=True, takes=22.0,
        **common,
    )
    own_states, mate_states = found[:kv_local], found[kv_local:]
    last = mate_states[-1]

    frequency = 1000000.0 ** (-(jnp.arange(HD // 2, dtype=jnp.float32) * 2.0) / HD)
    positions = page_count[0] * PAGE + jnp.arange(new_count, dtype=jnp.int32)
    angles = positions.astype(jnp.float32)[:, None] * frequency[None, :]
    cosine, sine = jnp.cos(angles), jnp.sin(angles)
    cosine = jnp.concatenate([cosine, cosine], axis=1)
    sine = jnp.concatenate([-sine, sine], axis=1)

    partials = [[] for k in heads]
    fresh = None
    for step in others:
        asked[step + 1] = swap(after(asked[step], last, *near), 1)
        waiting = []
        for k in heads:
            if k == 0:
                (here,) = attend(
                    me_list, after(tables, last, cosine, sine), [(step, k)], takes=12.0, **common
                )
                (there,) = attend(
                    me_list, after(tables, here), [(step + 1, k)], takes=12.0, **common
                )
                if forwarded and features[2] is None:
                    ahead = lax.ppermute(after(features[1], here), "tp", [(1, 2), (2, 3)])
                    back = lax.ppermute(after(features[3], here), "tp", [(1, 0), (2, 1)])
                    features[2] = ahead
                    features.append(back)
                    near = [ahead, back]
            else:
                here, there = attend(
                    me_list, after(tables, last), [(step, k), (step + 1, k)], takes=12.0, **common
                )
            last = there
            hold = near if k == heads[-1] else []
            waiting.append((here, swap(after(there, *hold), 1)))
        for k, (here, arrived) in enumerate(waiting):
            last = merge(here, after(arrived, last))
            partials[k].append(swap(last, step))
            if fresh is None:
                fresh = project(
                    rank.reshape(1),
                    cosine,
                    sine,
                    k_gain[None, :],
                    [after(hidden, last)] + features[1:],
                    weight,
                    shards,
                )
                last = fresh
                from_mate = [swap(after(state, last), 1) for state in mate_states]
                pages = {0: fresh, 1: swap(fresh, 1)}
                for apart in others:
                    pages[apart] = swap(fresh, apart)

    attention_out = None
    for k in heads:
        attention_out = final(
            k, after(queries, last), fresh, [own_states[k], from_mate[k]], partials[k], attention_out
        )
        if k == 0:
            written = attention_out
    for step in others:
        pages[step + 1] = swap(after(pages[step], written), 1)
    new_pool = write(
        me_list,
        tables,
        [pages[step] for step in range(inst_count)],
        pool_copy,
        new_pages,
        base,
    )
    return (attention_out, new_pool)


def solution(mesh):
    return jax.shard_map(
        per_device,
        mesh=mesh,
        in_specs=(
            P(("groups", "inst"), "tp"),
            P("inst", "tp"),
            P("inst", "tp"),
            P(),
            P(("groups", "inst"), "tp"),
            P(None, ("groups", "inst"), None, "tp"),
            P(("groups", "inst"), None),
            P(("groups", "inst"), None),
            P(("groups", "inst")),
            P(("groups", "inst"), None),
            P(("groups", "inst"), None),
        ),
        out_specs=(P(("groups", "inst"), "tp"), P(None, ("groups", "inst"), None, "tp")),
        check_vma=False,
    )
```

```python
import functools
import math

import jax
import jax.numpy as jnp
from jax import lax
from jax.experimental import pallas as pl
from jax.experimental.pallas import tpu as pltpu
from jax.sharding import PartitionSpec as P

HD = 128
PAGE = 128
GROUP = 8
BLOCK = GROUP * HD
EXTRA = 128
TOTALS = 64
STATS = 32
EMPTY = -1e30
LOG2E = 1.4426950408889634
SCALE = LOG2E / math.sqrt(HD)
CHUNK = 8
REST = (4, 2, 1)
ANY = pl.BlockSpec(memory_space=pl.ANY)
SMEM = pl.BlockSpec(memory_space=pltpu.SMEM)
VMEM_LIMIT = 63 * 1024 * 1024


def cost(microseconds):
    return pl.CostEstimate(
        flops=int(microseconds * 1e9), bytes_accessed=int(microseconds * 3e6), transcendentals=0
    )


def row_dot(a, b):
    return lax.dot_general(a, b, (((1,), (1,)), ((), ())), preferred_element_type=jnp.float32)


def plain_dot(a, b):
    return lax.dot_general(a, b, (((1,), (0,)), ((), ())), preferred_element_type=jnp.float32)


def split_stats(stat, lane, lanes, terms):
    high = stat.astype(jnp.bfloat16).astype(jnp.float32)
    rest = stat - high
    middle = rest.astype(jnp.bfloat16).astype(jnp.float32)
    terms = jnp.where(lanes == lane, high, terms)
    terms = jnp.where(lanes == lane + 1, middle, terms)
    return jnp.where(lanes == lane + 2, rest - middle, terms)


def joined_stats(extra, lane):
    term = lax.broadcasted_iota(jnp.int32, (EXTRA, HD), 0)
    picked = jnp.where((term >= lane) & (term < lane + 3), 1.0, 0.0).astype(jnp.bfloat16)
    return plain_dot(extra, picked)


def turned_stats(turned, lane):
    term = lax.broadcasted_iota(jnp.int32, (STATS, HD), 0)
    picked = jnp.where((term >= lane) & (term < lane + 3), 1.0, 0.0).astype(jnp.bfloat16)
    return lax.dot_general(
        turned, picked, (((0,), (0,)), ((), ())), preferred_element_type=jnp.float32
    )


def state_stats(extra, head):
    return joined_stats(extra, 3 * head), joined_stats(extra, TOTALS + 3 * head)


def attend_kernel(plan, refs):
    steps, kv_heads, pages_listed = plan["steps"], plan["kv_heads"], plan["pages_listed"]
    requests = len(steps)
    copy_pool, resume = plan["copy_pool"], plan["resume"]
    width = len(kv_heads)
    items = requests * width
    refs = list(refs)
    me_ref, table_ref = refs.pop(0), refs.pop(0)
    q_refs = [refs.pop(0) for _ in range(requests)]
    state_ref = refs.pop(0) if resume else None
    pool_ref = refs.pop(0)
    out_refs = [refs.pop(0) for _ in range(items)]
    new_pool_ref = refs.pop(0) if copy_pool else None
    q_buf, q_two, kv_buf, acc, maxima, totals, slots, q_sem, kv_sem, out_sem = refs[:10]
    refs = refs[10:]
    if resume:
        send_buf = refs.pop(0)
    new_count = q_buf.shape[2]
    rows = GROUP * new_count
    shape = (GROUP, new_count, HD)
    lanes = lax.broadcasted_iota(jnp.int32, (new_count, HD), 1)

    def q_copies(item):
        offset = kv_heads[item % width] * BLOCK
        return [
            pltpu.make_async_copy(
                q_refs[item // width].at[:, pl.ds(offset + head * HD, HD)],
                q_buf.at[item, head],
                q_sem.at[item, head],
            )
            for head in range(GROUP)
        ]

    def page_copies(request, place, slot):
        return [
            pltpu.make_async_copy(
                pool_ref.at[:, slot, :, pl.ds(kv_head * HD, HD)],
                kv_buf.at[request, column, :, place],
                kv_sem.at[request, column, place],
            )
            for column, kv_head in enumerate(kv_heads)
        ]

    def out_copy(item, index):
        if resume:
            part = [pl.ds(0, rows), pl.ds(rows, send_buf.shape[1] - rows)][index]
            source, target = send_buf.at[item, part], out_refs[item].at[part]
        else:
            part = [pl.ds(0, GROUP), pl.ds(GROUP, 1)][index]
            source, target = acc.at[item, part], out_refs[item].at[0, part]
        return pltpu.make_async_copy(source, target, out_sem.at[item, index])

    for item in range(items):
        for copy in q_copies(item):
            copy.start()
    if resume:
        state_copy = pltpu.make_async_copy(state_ref, acc, out_sem.at[0, 0])
        state_copy.start()
    me = me_ref[0]
    for request, apart in enumerate(steps):
        whose = me ^ apart
        count = table_ref[whose, 2 * pages_listed]

        def look(page, found, request=request, whose=whose, count=count):
            mine = (page < count) & (table_ref[whose, page] == me)

            @pl.when(mine)
            def _():
                for copy in page_copies(request, found, table_ref[whose, pages_listed + page]):
                    copy.start()

            return found + mine.astype(jnp.int32)

        slots[request] = lax.fori_loop(0, count, look, 0)
    pool_in, pool_out = [], []
    if copy_pool:
        pool_buf, pool_sem = refs
        slot_total = pool_ref.shape[1]
        parts = pool_sem.shape[1]
        step = slot_total // parts
        for index in range(2):
            for part in range(parts):
                piece = (index, pl.ds(part * step, step))
                sem = pool_sem.at[index, part]
                pool_in.append(pltpu.make_async_copy(pool_ref.at[piece], pool_buf.at[piece], sem))
                pool_out.append(
                    pltpu.make_async_copy(pool_buf.at[piece], new_pool_ref.at[piece], sem)
                )
        for copy in pool_in:
            copy.start()
    for item in range(items):
        for copy in q_copies(item):
            copy.wait()
    if resume:
        state_copy.wait()

    def one_item(item, carry):
        request = item // width
        column = item % width
        found = slots[request]
        sums = pl.ds(0, GROUP)
        scaled = q_buf[item].reshape(rows, HD).astype(jnp.float32) * SCALE
        high = scaled.astype(jnp.bfloat16)
        q_two[:, :HD] = high
        q_two[:, HD:] = (scaled - high.astype(jnp.float32)).astype(jnp.bfloat16)
        if resume:
            extra = acc[item, GROUP].astype(jnp.bfloat16)
            for head in range(GROUP):
                maxima[head], total = state_stats(extra, head)
                totals[head] = jnp.where(lanes == 0, total, 0.0)
        else:
            acc[item, sums] = jnp.zeros(shape, jnp.float32)
            totals[...] = jnp.zeros(shape, jnp.float32)
            maxima[...] = jnp.full(shape, EMPTY, jnp.float32)

        @pl.when(column == 0)
        def _():
            def arrived(place, carry):
                for copy in page_copies(request, place, 0):
                    copy.wait()
                return carry

            lax.fori_loop(0, found, arrived, 0)

        def chunk(first, count):
            keys = kv_buf[request, column, 0, pl.ds(first, count)].reshape(count * PAGE, HD)
            values = kv_buf[request, column, 1, pl.ds(first, count)].reshape(count * PAGE, HD)
            scores = row_dot(q_two[...], jnp.concatenate([keys, keys], axis=1))
            old = maxima[...].reshape(rows, HD)
            top = jnp.maximum(old, jnp.max(scores, axis=1, keepdims=True))
            rescale = jnp.exp2(old - top)
            total = totals[...].reshape(rows, HD) * rescale
            pieces = []
            for part in range(count):
                piece = jnp.exp2(scores[:, part * PAGE : (part + 1) * PAGE] - top)
                total = total + piece
                pieces.append(piece.astype(jnp.bfloat16))
            weights = jnp.concatenate(pieces, axis=1) if count > 1 else pieces[0]
            maxima[...] = top.reshape(shape)
            totals[...] = total.reshape(shape)
            acc[item, sums] = acc[item, sums] * rescale.reshape(shape) + plain_dot(
                weights, values
            ).reshape(shape)

        whole = found // CHUNK
        left = found % CHUNK

        def step(index, carry):
            chunk(index * CHUNK, CHUNK)
            return carry

        lax.fori_loop(0, whole, step, 0)
        done = whole * CHUNK
        for count in REST:

            @pl.when((left & count) != 0)
            def _(count=count, done=done):
                chunk(done, count)

            done = done + (left & count)

        def send(index):
            for each in range(items):

                @pl.when(item == each)
                def _(each=each):
                    out_copy(each, index).start()

        if not resume:
            send(0)
        terms = jnp.zeros((new_count, HD), jnp.float32)
        for head in range(GROUP):
            total = jnp.sum(totals[head], axis=1, keepdims=True)
            if resume:
                some = total > 0.0
                safe = jnp.where(some, total, 1.0)
                send_buf[item, head * new_count : (head + 1) * new_count] = (
                    acc[item, head] * (1.0 / safe)
                ).astype(jnp.bfloat16)
                stat = jnp.where(some, maxima[head] + jnp.log2(safe), EMPTY)
                terms = split_stats(stat, 3 * head, lanes, terms)
            else:
                terms = split_stats(maxima[head], 3 * head, lanes, terms)
                terms = split_stats(total, TOTALS + 3 * head, lanes, terms)
        if resume:
            turned = terms.T[:STATS].astype(jnp.bfloat16)
            for piece in range(new_count // HD):
                send_buf[item, rows + piece * STATS : rows + (piece + 1) * STATS] = turned[
                    :, piece * HD : (piece + 1) * HD
                ]
            send(0)
        else:
            acc[item, GROUP] = terms
        send(1)
        if copy_pool:

            @pl.when(item == 0)
            def _():
                for copy_in, copy_out in zip(pool_in, pool_out):
                    copy_in.wait()
                    copy_out.start()

        return carry

    lax.fori_loop(0, items, one_item, 0)
    for item in range(items):
        for index in range(2):
            out_copy(item, index).wait()
    for copy in pool_out:
        copy.wait()


def attend(
    me, tables, steps, asked, kv_heads, pool, pages_listed, capacity, takes, state=None, copy_pool=False
):
    requests, width, new_count = len(steps), len(kv_heads), asked[0].shape[0]
    items = requests * width
    resume = state is not None
    blocks = (GROUP + 1, new_count, HD)
    parcel = (GROUP * new_count + STATS * new_count // HD, HD)
    if resume:
        out_shape = [jax.ShapeDtypeStruct(parcel, jnp.bfloat16) for _ in range(items)]
    else:
        out_shape = [jax.ShapeDtypeStruct((1,) + blocks, jnp.float32) for _ in range(items)]
    scratch = [
        pltpu.VMEM((items, GROUP, new_count, HD), jnp.bfloat16),
        pltpu.VMEM((GROUP * new_count, 2 * HD), jnp.bfloat16),
        pltpu.VMEM((requests, width, 2, capacity, PAGE, HD), jnp.bfloat16),
        pltpu.VMEM((items,) + blocks, jnp.float32),
        pltpu.VMEM((GROUP, new_count, HD), jnp.float32),
        pltpu.VMEM((GROUP, new_count, HD), jnp.float32),
        pltpu.SMEM((requests,), jnp.int32),
        pltpu.SemaphoreType.DMA((items, GROUP)),
        pltpu.SemaphoreType.DMA((requests, width, capacity)),
        pltpu.SemaphoreType.DMA((items, 2)),
    ]
    if resume:
        scratch.append(pltpu.VMEM((items,) + parcel, jnp.bfloat16))
    if copy_pool:
        out_shape.append(jax.ShapeDtypeStruct(pool.shape, pool.dtype))
        parts = next(part for part in (6, 3, 2, 1) if pool.shape[1] % part == 0)
        scratch += [pltpu.VMEM(pool.shape, pool.dtype), pltpu.SemaphoreType.DMA((2, parts))]
    plan = dict(
        steps=steps, kv_heads=kv_heads, pages_listed=pages_listed, copy_pool=copy_pool,
        resume=resume,
    )
    return pl.pallas_call(
        lambda *refs: attend_kernel(plan, refs),
        out_shape=out_shape,
        in_specs=[SMEM, SMEM] + [ANY] * (requests + resume + 1),
        out_specs=[ANY] * len(out_shape),
        scratch_shapes=scratch,
        compiler_params=pltpu.CompilerParams(vmem_limit_bytes=VMEM_LIMIT),
        cost_estimate=cost(takes),
    )(me, tables, *asked, *([state] if resume else []), pool)


def project_kernel(shards, forwarded, rank_ref, cos_ref, sin_ref, gain_ref, *refs):
    hidden_refs, weight_ref = refs[:-6], refs[-6]
    out_ref, features, gathered, feature_sem, weight_sem = refs[-5:]
    rank = rank_ref[0]
    span = features.shape[2]
    depth, width = gathered.shape[0], gathered.shape[1] // 2

    def copies(shard):
        return [
            pltpu.make_async_copy(
                weight_ref.at[pl.ds(kind * depth + shard * span, span)],
                gathered.at[pl.ds(shard * span, span), pl.ds(kind * width, width)],
                weight_sem.at[kind, shard],
            )
            for kind in range(2)
        ]

    def feature_copy(step, ref):
        shard = lax.rem(rank + shards - step, shards)
        return pltpu.make_async_copy(ref, features.at[shard], feature_sem.at[step])

    for step in range(shards):
        if forwarded and step == 2:
            @pl.when(rank >= 2)
            def _():
                feature_copy(2, hidden_refs[2]).start()

            @pl.when(rank < 2)
            def _():
                feature_copy(2, hidden_refs[shards]).start()

        else:
            feature_copy(step, hidden_refs[step]).start()
    for shard in range(shards):
        for copy in copies(shard):
            copy.start()
    for step in range(shards):
        feature_copy(step, hidden_refs[step]).wait()
    raw = 0.0
    for shard in range(shards):
        for copy in copies(shard):
            copy.wait()
        raw = raw + plain_dot(features[shard], gathered[shard * span : (shard + 1) * span])
    columns = []
    for head in range(width // HD):
        one = raw[:, head * HD : (head + 1) * HD]
        mean = jnp.sum(one * one, axis=1, keepdims=True) * (1.0 / HD)
        one = one * lax.rsqrt(mean + 1e-06) * gain_ref[...]
        columns.append(one * cos_ref[...] + pltpu.roll(one, HD // 2, 1) * sin_ref[...])
    new_keys = jnp.concatenate(columns, axis=1) if len(columns) > 1 else columns[0]
    out_ref[0] = new_keys.astype(jnp.bfloat16)
    out_ref[1] = raw[:, width:].astype(jnp.bfloat16)


def project(rank, cos, sin, gain, hidden, weight, shards):
    new_count, span = hidden[0].shape
    depth, width = weight.shape[0] // 2, weight.shape[1]
    vmem = pl.BlockSpec(memory_space=pltpu.VMEM)
    return pl.pallas_call(
        functools.partial(project_kernel, shards, len(hidden) > shards),
        out_shape=jax.ShapeDtypeStruct((2, new_count, width), jnp.bfloat16),
        in_specs=[SMEM, vmem, vmem, vmem] + [ANY] * (len(hidden) + 1),
        out_specs=vmem,
        scratch_shapes=[
            pltpu.VMEM((shards, new_count, span), jnp.bfloat16),
            pltpu.VMEM((depth, 2 * width), jnp.bfloat16),
            pltpu.SemaphoreType.DMA((shards,)),
            pltpu.SemaphoreType.DMA((2, shards)),
        ],
        compiler_params=pltpu.CompilerParams(vmem_limit_bytes=VMEM_LIMIT),
        cost_estimate=cost(0.2),
    )(rank, cos, sin, gain, *hidden, weight)


def turned_parts(partials, rows):
    return [
        jnp.concatenate(
            [part[start : start + STATS] for start in range(rows, part.shape[0], STATS)], axis=1
        )
        for part in partials
    ]


def fresh_kernel(parts, as_state, q_ref, fresh_ref, *refs):
    states, partials, out_ref = refs[:2], refs[2 : 2 + parts], refs[-1]
    new_count = q_ref.shape[0]
    rows = GROUP * new_count
    row = lax.broadcasted_iota(jnp.int32, (new_count, new_count), 0)
    column = lax.broadcasted_iota(jnp.int32, (new_count, new_count), 1)
    lanes = lax.broadcasted_iota(jnp.int32, (new_count, HD), 1)
    heads = [slice(head * HD, (head + 1) * HD) for head in range(GROUP)]
    stacked = jnp.concatenate([q_ref[:, span] for span in heads], axis=0)
    scores = row_dot(stacked, fresh_ref[0]).reshape(GROUP, new_count, new_count)
    scores = jnp.where((column <= row)[None], scores * SCALE, EMPTY)
    extras = [ref[0, GROUP].astype(jnp.bfloat16) for ref in states]
    turned = turned_parts(partials, rows)
    weights, shares, divisors = [], [], []
    terms = jnp.zeros((new_count, HD), jnp.float32)
    for head in range(GROUP):
        stats = [state_stats(extra, head) for extra in extras]
        stats += [(turned_stats(part, 3 * head), 1.0) for part in turned]
        top = jnp.broadcast_to(jnp.max(scores[head], axis=1, keepdims=True), (new_count, HD))
        for other, _ in stats:
            top = jnp.maximum(top, other)
        pieces = [
            jnp.exp2(scores[head, :, start : start + HD] - top) for start in range(0, new_count, HD)
        ]
        total = jnp.broadcast_to(jnp.sum(sum(pieces), axis=1, keepdims=True), (new_count, HD))
        shares.append([jnp.exp2(other - top) for other, _ in stats])
        for share, (_, part) in zip(shares[-1], stats):
            total = total + share * part
        divisors.append(total)
        weights.append(jnp.concatenate(pieces, axis=1).astype(jnp.bfloat16))
        if as_state:
            terms = split_stats(top, 3 * head, lanes, terms)
            terms = split_stats(total, TOTALS + 3 * head, lanes, terms)
    sums = plain_dot(jnp.concatenate(weights, axis=0), fresh_ref[1]).reshape(GROUP, new_count, HD)
    for head, span in enumerate(heads):
        mixed = sums[head]
        block = slice(head * new_count, (head + 1) * new_count)
        given = [ref[0, head] for ref in states] + [ref[block] for ref in partials]
        for share, part in zip(shares[head], given):
            mixed = mixed + share * part.astype(jnp.float32)
        if as_state:
            out_ref[0, head] = mixed
        else:
            out_ref[:, span] = (mixed / divisors[head]).astype(jnp.bfloat16)
    if as_state:
        out_ref[0, GROUP] = terms


def last_kernel(parts, state_ref, *refs):
    partials, out_ref = refs[:parts], refs[-1]
    new_count = state_ref.shape[2]
    extra = state_ref[0, GROUP].astype(jnp.bfloat16)
    turned = turned_parts(partials, GROUP * new_count)
    for head in range(GROUP):
        top, total = state_stats(extra, head)
        stats = [turned_stats(part, 3 * head) for part in turned]
        best = top
        for stat in stats:
            best = jnp.maximum(best, stat)
        share = jnp.exp2(top - best)
        mixed, total = share * state_ref[0, head], share * total
        block = slice(head * new_count, (head + 1) * new_count)
        for stat, partial in zip(stats, partials):
            share = jnp.exp2(stat - best)
            total = total + share
            mixed = mixed + share * partial[block].astype(jnp.float32)
        out_ref[:, head * HD : (head + 1) * HD] = (mixed / total).astype(jnp.bfloat16)


def attend_fresh(kv_head, queries, fresh, states, partials=(), as_state=False):
    new_count = queries.shape[0]
    blocks = (1, GROUP + 1, new_count, HD)
    out_shape = jax.ShapeDtypeStruct(queries.shape, jnp.bfloat16)
    out_spec = pl.BlockSpec((new_count, BLOCK), lambda step: (0, kv_head))
    if as_state:
        out_shape = jax.ShapeDtypeStruct(blocks, jnp.float32)
        out_spec = pl.BlockSpec(blocks, lambda step: (0, 0, 0, 0))
    return pl.pallas_call(
        functools.partial(fresh_kernel, len(partials), as_state),
        grid=(1,),
        out_shape=out_shape,
        in_specs=[
            pl.BlockSpec((new_count, BLOCK), lambda step: (0, kv_head)),
            pl.BlockSpec((2, new_count, HD), lambda step: (0, 0, kv_head)),
        ]
        + [pl.BlockSpec(blocks, lambda step: (0, 0, 0, 0))] * len(states)
        + [pl.BlockSpec(partial.shape, lambda step: (0, 0)) for partial in partials],
        out_specs=out_spec,
        compiler_params=pltpu.CompilerParams(vmem_limit_bytes=VMEM_LIMIT),
        cost_estimate=cost(0.2),
    )(queries, fresh, *states, *partials)


def finish(kv_head, state, partials, before):
    new_count = before.shape[0]
    blocks = (1, GROUP + 1, new_count, HD)
    return pl.pallas_call(
        functools.partial(last_kernel, len(partials)),
        grid=(1,),
        out_shape=jax.ShapeDtypeStruct(before.shape, jnp.bfloat16),
        in_specs=[pl.BlockSpec(blocks, lambda step: (0, 0, 0, 0))]
        + [pl.BlockSpec(partial.shape, lambda step: (0, 0)) for partial in partials]
        + [ANY],
        out_specs=pl.BlockSpec((new_count, BLOCK), lambda step: (0, kv_head)),
        input_output_aliases={1 + len(partials): 0},
        compiler_params=pltpu.CompilerParams(vmem_limit_bytes=VMEM_LIMIT),
        cost_estimate=cost(0.2),
    )(state, *partials, before)


def write_kernel(holders, new_pages, base, me_ref, table_ref, *refs):
    pages = refs[:holders]
    out_ref, sem = refs[holders + 1], refs[holders + 2]
    me = me_ref[0]

    def each(action):
        for holder in range(holders):
            for page in range(new_pages):

                @pl.when(table_ref[me ^ holder, base + page] == me)
                def _(holder=holder, page=page):
                    slot = table_ref[me ^ holder, base + new_pages + page]
                    copy = pltpu.make_async_copy(
                        pages[holder].at[:, pl.ds(page * PAGE, PAGE)],
                        out_ref.at[:, slot],
                        sem.at[holder, page],
                    )
                    getattr(copy, action)()

    each("start")
    each("wait")


def write(me, tables, fresh, pool, new_pages, base):
    holders = len(fresh)
    return pl.pallas_call(
        functools.partial(write_kernel, holders, new_pages, base),
        out_shape=jax.ShapeDtypeStruct(pool.shape, pool.dtype),
        in_specs=[SMEM, SMEM]
        + [pl.BlockSpec(memory_space=pltpu.VMEM)] * holders
        + [ANY],
        out_specs=ANY,
        input_output_aliases={2 + holders: 0},
        scratch_shapes=[pltpu.SemaphoreType.DMA((holders, new_pages))],
        compiler_params=pltpu.CompilerParams(vmem_limit_bytes=8 * 1024 * 1024),
        cost_estimate=cost(0.2),
    )(me, tables, *fresh, pool)


def per_device(
    hidden,
    k_weight,
    v_weight,
    k_gain,
    queries,
    kv_pool,
    page_holder,
    page_slot,
    page_count,
    write_owner,
    write_slot,
):
    inst_count = lax.axis_size("inst")
    shards = lax.axis_size("tp")
    me = lax.axis_index("inst").astype(jnp.int32)
    rank = lax.axis_index("tp").astype(jnp.int32)
    groups = lax.axis_size("groups")
    group = lax.axis_index("groups").astype(jnp.int32)
    pages_listed = page_holder.shape[1]
    new_pages = write_owner.shape[1]
    capacity = 3 * pages_listed // (2 * inst_count)
    new_count = hidden.shape[0]
    kv_local = k_weight.shape[1] // HD
    me_list = me.reshape(1)

    def swap(array, step):
        return lax.ppermute(array, "inst", [(i, i ^ step) for i in range(inst_count)])

    def shift(array, step):
        return lax.ppermute(array, "tp", [(i, (i + step) % shards) for i in range(shards)])

    def after(array, *done):
        return lax.optimization_barrier((array,) + done)[0]

    heads = list(range(kv_local))
    base = 2 * pages_listed + 1
    own_table = jnp.concatenate(
        [page_holder[0], page_slot[0], page_count, write_owner[0], write_slot[0]]
    )
    own_table = jnp.pad(own_table, (0, 128 - own_table.shape[0]))[None]
    others = range(2, inst_count, 2)

    tables = lax.all_gather(own_table, "inst", axis=0, tiled=True)
    sent = after(queries, tables)
    asked = {0: queries, 1: swap(sent, 1)}
    for step in others:
        asked[step] = swap(sent, step)
    features = [hidden]
    forwarded = shards == 4
    for step in range(1, shards):
        direct = not forwarded or step != 2
        features.append(shift(after(hidden, tables), step) if direct else None)
    near = [features[1], features[-1]]
    if groups == 2:
        chosen = jnp.where(group == 0, k_weight, v_weight)
        weight = lax.all_gather(after(chosen, tables), ("groups", "inst"), axis=0, tiled=True)
    else:
        weight = jnp.concatenate(
            [lax.all_gather(one, "inst", axis=0, tiled=True) for one in (k_weight, v_weight)]
        )

    common = dict(pool=kv_pool, pages_listed=pages_listed, capacity=capacity)
    *found, pool_copy = attend(
        me_list, tables, [0, 1], [queries, asked[1]], heads, copy_pool=True, takes=22.0, **common
    )
    own_states, mate_states = found[:kv_local], found[kv_local:]
    last = mate_states[-1]

    frequency = 1000000.0 ** (-(jnp.arange(HD // 2, dtype=jnp.float32) * 2.0) / HD)
    positions = page_count[0] * PAGE + jnp.arange(new_count, dtype=jnp.int32)
    angles = positions.astype(jnp.float32)[:, None] * frequency[None, :]
    cosine, sine = jnp.cos(angles), jnp.sin(angles)
    cosine = jnp.concatenate([cosine, cosine], axis=1)
    sine = jnp.concatenate([-sine, sine], axis=1)
    partials = [[] for k in heads]
    fresh = None
    for step in others:
        asked[step + 1] = swap(after(asked[step], last, *near), 1)
        if forwarded and features[2] is None:
            ahead = lax.ppermute(after(features[1], last), "tp", [(1, 2), (2, 3)])
            back = lax.ppermute(after(features[3], last), "tp", [(1, 0), (2, 1)])
            features[2] = ahead
            features.append(back)
            near = [ahead, back]
        begun = attend(
            me_list, after(tables, last, cosine, sine), [step + 1], [asked[step + 1]], heads,
            takes=12.0, **common
        )
        last = begun[-1]
        halves = [swap(after(state, *near), 1) for state in begun]
        if fresh is None:
            from_mate = [swap(after(state, last), 1) for state in mate_states]
        for k in heads:
            (last,) = attend(
                me_list, after(tables, last), [step], [asked[step]], [k], state=halves[k],
                takes=0.2, **common,
            )
            partials[k].append(swap(last, step))
            if fresh is None:
                fresh = project(
                    rank.reshape(1),
                    cosine,
                    sine,
                    k_gain[None, :],
                    [after(hidden, last)] + features[1:],
                    weight,
                    shards,
                )
                last = fresh
                pages = {0: fresh, 1: swap(fresh, 1)}
                for apart in others:
                    pages[apart] = swap(fresh, apart)

    attention_out = attend_fresh(
        0, after(queries, last), fresh, [own_states[0], from_mate[0]], partials[0]
    )
    for step in others:
        pages[step + 1] = swap(after(pages[step], attention_out), 1)
    for k in heads[1:]:
        state = attend_fresh(
            k, after(queries, attention_out), fresh, [own_states[k], from_mate[k]], as_state=True
        )
        attention_out = finish(k, state, partials[k], attention_out)
    new_pool = write(
        me_list,
        tables,
        [pages[step] for step in range(inst_count)],
        pool_copy,
        new_pages,
        base,
    )
    return (attention_out, new_pool)


def solution(mesh):
    return jax.shard_map(
        per_device,
        mesh=mesh,
        in_specs=(
            P(("groups", "inst"), "tp"),
            P("inst", "tp"),
            P("inst", "tp"),
            P(),
            P(("groups", "inst"), "tp"),
            P(None, ("groups", "inst"), None, "tp"),
            P(("groups", "inst"), None),
            P(("groups", "inst"), None),
            P(("groups", "inst")),
            P(("groups", "inst"), None),
            P(("groups", "inst"), None),
        ),
        out_specs=(P(("groups", "inst"), "tp"), P(None, ("groups", "inst"), None, "tp")),
        check_vma=False,
    )
```

```python
import functools
import math

import jax
import jax.numpy as jnp
from jax import lax
from jax.experimental import pallas as pl
from jax.experimental.pallas import tpu as pltpu
from jax.sharding import PartitionSpec as P

HD = 128
PAGE = 128
GROUP = 8
BLOCK = GROUP * HD
EXTRA = 128
TOTALS = 64
STATS = 32
EMPTY = -1e30
LOG2E = 1.4426950408889634
SCALE = LOG2E / math.sqrt(HD)
CHUNK = 8
REST = (4, 2, 1)
ANY = pl.BlockSpec(memory_space=pl.ANY)
SMEM = pl.BlockSpec(memory_space=pltpu.SMEM)
VMEM_LIMIT = 63 * 1024 * 1024


def cost(microseconds):
    return pl.CostEstimate(
        flops=int(microseconds * 1e9), bytes_accessed=int(microseconds * 3e6), transcendentals=0
    )


def row_dot(a, b):
    return lax.dot_general(a, b, (((1,), (1,)), ((), ())), preferred_element_type=jnp.float32)


def plain_dot(a, b):
    return lax.dot_general(a, b, (((1,), (0,)), ((), ())), preferred_element_type=jnp.float32)


def split_stats(stat, lane, lanes, terms):
    high = stat.astype(jnp.bfloat16).astype(jnp.float32)
    rest = stat - high
    middle = rest.astype(jnp.bfloat16).astype(jnp.float32)
    terms = jnp.where(lanes == lane, high, terms)
    terms = jnp.where(lanes == lane + 1, middle, terms)
    return jnp.where(lanes == lane + 2, rest - middle, terms)


def joined_stats(extra, lane):
    term = lax.broadcasted_iota(jnp.int32, (EXTRA, HD), 0)
    picked = jnp.where((term >= lane) & (term < lane + 3), 1.0, 0.0).astype(jnp.bfloat16)
    return plain_dot(extra, picked)


def turned_stats(turned, lane):
    term = lax.broadcasted_iota(jnp.int32, (STATS, HD), 0)
    picked = jnp.where((term >= lane) & (term < lane + 3), 1.0, 0.0).astype(jnp.bfloat16)
    return lax.dot_general(
        turned, picked, (((0,), (0,)), ((), ())), preferred_element_type=jnp.float32
    )


def state_stats(extra, head):
    return joined_stats(extra, 3 * head), joined_stats(extra, TOTALS + 3 * head)


def attend_kernel(plan, refs):
    steps, kv_heads, pages_listed = plan["steps"], plan["kv_heads"], plan["pages_listed"]
    requests = len(steps)
    copy_pool, resume = plan["copy_pool"], plan["resume"]
    width = len(kv_heads)
    items = requests * width
    refs = list(refs)
    me_ref, table_ref = refs.pop(0), refs.pop(0)
    q_refs = [refs.pop(0) for _ in range(requests)]
    state_ref = refs.pop(0) if resume else None
    pool_ref = refs.pop(0)
    out_refs = [refs.pop(0) for _ in range(items)]
    new_pool_ref = refs.pop(0) if copy_pool else None
    q_buf, q_two, kv_buf, acc, maxima, totals, slots, q_sem, kv_sem, out_sem = refs[:10]
    refs = refs[10:]
    if resume:
        send_buf = refs.pop(0)
    new_count = q_buf.shape[2]
    rows = GROUP * new_count
    shape = (GROUP, new_count, HD)
    lanes = lax.broadcasted_iota(jnp.int32, (new_count, HD), 1)

    def q_copies(item):
        offset = kv_heads[item % width] * BLOCK
        return [
            pltpu.make_async_copy(
                q_refs[item // width].at[:, pl.ds(offset + head * HD, HD)],
                q_buf.at[item, head],
                q_sem.at[item, head],
            )
            for head in range(GROUP)
        ]

    def page_copies(request, place, slot):
        return [
            pltpu.make_async_copy(
                pool_ref.at[:, slot, :, pl.ds(kv_head * HD, HD)],
                kv_buf.at[request, column, :, place],
                kv_sem.at[request, column, place],
            )
            for column, kv_head in enumerate(kv_heads)
        ]

    def out_copy(item, index):
        if resume:
            part = [pl.ds(0, rows), pl.ds(rows, send_buf.shape[1] - rows)][index]
            source, target = send_buf.at[item, part], out_refs[item].at[part]
        else:
            part = [pl.ds(0, GROUP), pl.ds(GROUP, 1)][index]
            source, target = acc.at[item, part], out_refs[item].at[0, part]
        return pltpu.make_async_copy(source, target, out_sem.at[item, index])

    for item in range(items):
        for copy in q_copies(item):
            copy.start()
    if resume:
        state_copy = pltpu.make_async_copy(state_ref, acc, out_sem.at[0, 0])
        state_copy.start()
    me = me_ref[0]
    for request, apart in enumerate(steps):
        whose = me ^ apart
        count = table_ref[whose, 2 * pages_listed]

        def look(page, found, request=request, whose=whose, count=count):
            mine = (page < count) & (table_ref[whose, page] == me)

            @pl.when(mine)
            def _():
                for copy in page_copies(request, found, table_ref[whose, pages_listed + page]):
                    copy.start()

            return found + mine.astype(jnp.int32)

        slots[request] = lax.fori_loop(0, count, look, 0)
    pool_in, pool_out = [], []
    if copy_pool:
        pool_buf, pool_sem = refs
        slot_total = pool_ref.shape[1]
        parts = pool_sem.shape[1]
        step = slot_total // parts
        for index in range(2):
            for part in range(parts):
                piece = (index, pl.ds(part * step, step))
                sem = pool_sem.at[index, part]
                pool_in.append(pltpu.make_async_copy(pool_ref.at[piece], pool_buf.at[piece], sem))
                pool_out.append(
                    pltpu.make_async_copy(pool_buf.at[piece], new_pool_ref.at[piece], sem)
                )
        for copy in pool_in:
            copy.start()
    for item in range(items):
        for copy in q_copies(item):
            copy.wait()
    if resume:
        state_copy.wait()

    def one_item(item, carry):
        request = item // width
        column = item % width
        found = slots[request]
        sums = pl.ds(0, GROUP)
        scaled = q_buf[item].reshape(rows, HD).astype(jnp.float32) * SCALE
        high = scaled.astype(jnp.bfloat16)
        q_two[:, :HD] = high
        q_two[:, HD:] = (scaled - high.astype(jnp.float32)).astype(jnp.bfloat16)
        if resume:
            extra = acc[item, GROUP].astype(jnp.bfloat16)
            for head in range(GROUP):
                maxima[head], total = state_stats(extra, head)
                totals[head] = jnp.where(lanes == 0, total, 0.0)
        else:
            acc[item, sums] = jnp.zeros(shape, jnp.float32)
            totals[...] = jnp.zeros(shape, jnp.float32)
            maxima[...] = jnp.full(shape, EMPTY, jnp.float32)

        @pl.when(column == 0)
        def _():
            def arrived(place, carry):
                for copy in page_copies(request, place, 0):
                    copy.wait()
                return carry

            lax.fori_loop(0, found, arrived, 0)

        def chunk(first, count):
            keys = kv_buf[request, column, 0, pl.ds(first, count)].reshape(count * PAGE, HD)
            values = kv_buf[request, column, 1, pl.ds(first, count)].reshape(count * PAGE, HD)
            scores = row_dot(q_two[...], jnp.concatenate([keys, keys], axis=1))
            old = maxima[...].reshape(rows, HD)
            top = jnp.maximum(old, jnp.max(scores, axis=1, keepdims=True))
            rescale = jnp.exp2(old - top)
            total = totals[...].reshape(rows, HD) * rescale
            pieces = []
            for part in range(count):
                piece = jnp.exp2(scores[:, part * PAGE : (part + 1) * PAGE] - top)
                total = total + piece
                pieces.append(piece.astype(jnp.bfloat16))
            weights = jnp.concatenate(pieces, axis=1) if count > 1 else pieces[0]
            maxima[...] = top.reshape(shape)
            totals[...] = total.reshape(shape)
            acc[item, sums] = acc[item, sums] * rescale.reshape(shape) + plain_dot(
                weights, values
            ).reshape(shape)

        whole = found // CHUNK
        left = found % CHUNK

        def step(index, carry):
            chunk(index * CHUNK, CHUNK)
            return carry

        lax.fori_loop(0, whole, step, 0)
        done = whole * CHUNK
        for count in REST:

            @pl.when((left & count) != 0)
            def _(count=count, done=done):
                chunk(done, count)

            done = done + (left & count)

        def send(index):
            for each in range(items):

                @pl.when(item == each)
                def _(each=each):
                    out_copy(each, index).start()

        if not resume:
            send(0)
        terms = jnp.zeros((new_count, HD), jnp.float32)
        for head in range(GROUP):
            total = jnp.sum(totals[head], axis=1, keepdims=True)
            if resume:
                some = total > 0.0
                safe = jnp.where(some, total, 1.0)
                send_buf[item, head * new_count : (head + 1) * new_count] = (
                    acc[item, head] * (1.0 / safe)
                ).astype(jnp.bfloat16)
                stat = jnp.where(some, maxima[head] + jnp.log2(safe), EMPTY)
                terms = split_stats(stat, 3 * head, lanes, terms)
            else:
                terms = split_stats(maxima[head], 3 * head, lanes, terms)
                terms = split_stats(total, TOTALS + 3 * head, lanes, terms)
        if resume:
            turned = terms.T[:STATS].astype(jnp.bfloat16)
            for piece in range(new_count // HD):
                send_buf[item, rows + piece * STATS : rows + (piece + 1) * STATS] = turned[
                    :, piece * HD : (piece + 1) * HD
                ]
            send(0)
        else:
            acc[item, GROUP] = terms
        send(1)
        if copy_pool:

            @pl.when(item == 0)
            def _():
                for copy_in, copy_out in zip(pool_in, pool_out):
                    copy_in.wait()
                    copy_out.start()

        return carry

    lax.fori_loop(0, items, one_item, 0)
    for item in range(items):
        for index in range(2):
            out_copy(item, index).wait()
    for copy in pool_out:
        copy.wait()


def attend(
    me, tables, steps, asked, kv_heads, pool, pages_listed, capacity, takes, state=None, copy_pool=False
):
    requests, width, new_count = len(steps), len(kv_heads), asked[0].shape[0]
    items = requests * width
    resume = state is not None
    blocks = (GROUP + 1, new_count, HD)
    parcel = (GROUP * new_count + STATS * new_count // HD, HD)
    if resume:
        out_shape = [jax.ShapeDtypeStruct(parcel, jnp.bfloat16) for _ in range(items)]
    else:
        out_shape = [jax.ShapeDtypeStruct((1,) + blocks, jnp.float32) for _ in range(items)]
    scratch = [
        pltpu.VMEM((items, GROUP, new_count, HD), jnp.bfloat16),
        pltpu.VMEM((GROUP * new_count, 2 * HD), jnp.bfloat16),
        pltpu.VMEM((requests, width, 2, capacity, PAGE, HD), jnp.bfloat16),
        pltpu.VMEM((items,) + blocks, jnp.float32),
        pltpu.VMEM((GROUP, new_count, HD), jnp.float32),
        pltpu.VMEM((GROUP, new_count, HD), jnp.float32),
        pltpu.SMEM((requests,), jnp.int32),
        pltpu.SemaphoreType.DMA((items, GROUP)),
        pltpu.SemaphoreType.DMA((requests, width, capacity)),
        pltpu.SemaphoreType.DMA((items, 2)),
    ]
    if resume:
        scratch.append(pltpu.VMEM((items,) + parcel, jnp.bfloat16))
    if copy_pool:
        out_shape.append(jax.ShapeDtypeStruct(pool.shape, pool.dtype))
        parts = next(part for part in (6, 3, 2, 1) if pool.shape[1] % part == 0)
        scratch += [pltpu.VMEM(pool.shape, pool.dtype), pltpu.SemaphoreType.DMA((2, parts))]
    plan = dict(
        steps=steps, kv_heads=kv_heads, pages_listed=pages_listed, copy_pool=copy_pool,
        resume=resume,
    )
    return pl.pallas_call(
        lambda *refs: attend_kernel(plan, refs),
        out_shape=out_shape,
        in_specs=[SMEM, SMEM] + [ANY] * (requests + resume + 1),
        out_specs=[ANY] * len(out_shape),
        scratch_shapes=scratch,
        compiler_params=pltpu.CompilerParams(vmem_limit_bytes=VMEM_LIMIT),
        cost_estimate=cost(takes),
    )(me, tables, *asked, *([state] if resume else []), pool)


def project_kernel(shards, forwarded, rank_ref, cos_ref, sin_ref, gain_ref, *refs):
    hidden_refs, weight_ref = refs[:-6], refs[-6]
    out_ref, features, gathered, feature_sem, weight_sem = refs[-5:]
    rank = rank_ref[0]
    span = features.shape[2]
    depth, width = gathered.shape[1], gathered.shape[2]

    def copies(shard):
        return [
            pltpu.make_async_copy(
                weight_ref.at[pl.ds(kind * depth + shard * span, span)],
                gathered.at[kind, pl.ds(shard * span, span)],
                weight_sem.at[kind, shard],
            )
            for kind in range(2)
        ]

    def feature_copy(step, ref):
        shard = lax.rem(rank + shards - step, shards)
        return pltpu.make_async_copy(ref, features.at[shard], feature_sem.at[step])

    for step in range(shards):
        if forwarded and step == 2:
            @pl.when(rank >= 2)
            def _():
                feature_copy(2, hidden_refs[2]).start()

            @pl.when(rank < 2)
            def _():
                feature_copy(2, hidden_refs[shards]).start()

        else:
            feature_copy(step, hidden_refs[step]).start()
    for shard in range(shards):
        for copy in copies(shard):
            copy.start()
    for step in range(shards):
        feature_copy(step, hidden_refs[step]).wait()
    raw = [0.0, 0.0]
    for shard in range(shards):
        for kind, copy in enumerate(copies(shard)):
            copy.wait()
            raw[kind] = raw[kind] + plain_dot(
                features[shard], gathered[kind, shard * span : (shard + 1) * span]
            )
    columns = []
    for head in range(width // HD):
        one = raw[0][:, head * HD : (head + 1) * HD]
        mean = jnp.sum(one * one, axis=1, keepdims=True) * (1.0 / HD)
        one = one * lax.rsqrt(mean + 1e-06) * gain_ref[...]
        columns.append(one * cos_ref[...] + pltpu.roll(one, HD // 2, 1) * sin_ref[...])
    new_keys = jnp.concatenate(columns, axis=1) if len(columns) > 1 else columns[0]
    out_ref[0] = new_keys.astype(jnp.bfloat16)
    out_ref[1] = raw[1].astype(jnp.bfloat16)


def project(rank, cos, sin, gain, hidden, weight, shards):
    new_count, span = hidden[0].shape
    depth, width = weight.shape[0] // 2, weight.shape[1]
    vmem = pl.BlockSpec(memory_space=pltpu.VMEM)
    return pl.pallas_call(
        functools.partial(project_kernel, shards, len(hidden) > shards),
        out_shape=jax.ShapeDtypeStruct((2, new_count, width), jnp.bfloat16),
        in_specs=[SMEM, vmem, vmem, vmem] + [ANY] * (len(hidden) + 1),
        out_specs=vmem,
        scratch_shapes=[
            pltpu.VMEM((shards, new_count, span), jnp.bfloat16),
            pltpu.VMEM((2, depth, width), jnp.bfloat16),
            pltpu.SemaphoreType.DMA((shards,)),
            pltpu.SemaphoreType.DMA((2, shards)),
        ],
        compiler_params=pltpu.CompilerParams(vmem_limit_bytes=VMEM_LIMIT),
        cost_estimate=cost(0.2),
    )(rank, cos, sin, gain, *hidden, weight)


def turned_parts(partials, rows):
    return [
        jnp.concatenate(
            [part[start : start + STATS] for start in range(rows, part.shape[0], STATS)], axis=1
        )
        for part in partials
    ]


def fresh_kernel(parts, as_state, q_ref, fresh_ref, *refs):
    states, partials, out_ref = refs[:2], refs[2 : 2 + parts], refs[-1]
    new_count = q_ref.shape[0]
    rows = GROUP * new_count
    row = lax.broadcasted_iota(jnp.int32, (new_count, new_count), 0)
    column = lax.broadcasted_iota(jnp.int32, (new_count, new_count), 1)
    lanes = lax.broadcasted_iota(jnp.int32, (new_count, HD), 1)
    heads = [slice(head * HD, (head + 1) * HD) for head in range(GROUP)]
    stacked = jnp.concatenate([q_ref[:, span] for span in heads], axis=0)
    scores = row_dot(stacked, fresh_ref[0]).reshape(GROUP, new_count, new_count)
    scores = jnp.where((column <= row)[None], scores * SCALE, EMPTY)
    extras = [ref[0, GROUP].astype(jnp.bfloat16) for ref in states]
    turned = turned_parts(partials, rows)
    weights, shares, divisors = [], [], []
    terms = jnp.zeros((new_count, HD), jnp.float32)
    for head in range(GROUP):
        stats = [state_stats(extra, head) for extra in extras]
        stats += [(turned_stats(part, 3 * head), 1.0) for part in turned]
        top = jnp.broadcast_to(jnp.max(scores[head], axis=1, keepdims=True), (new_count, HD))
        for other, _ in stats:
            top = jnp.maximum(top, other)
        pieces = [
            jnp.exp2(scores[head, :, start : start + HD] - top) for start in range(0, new_count, HD)
        ]
        total = jnp.broadcast_to(jnp.sum(sum(pieces), axis=1, keepdims=True), (new_count, HD))
        shares.append([jnp.exp2(other - top) for other, _ in stats])
        for share, (_, part) in zip(shares[-1], stats):
            total = total + share * part
        divisors.append(total)
        weights.append(jnp.concatenate(pieces, axis=1).astype(jnp.bfloat16))
        if as_state:
            terms = split_stats(top, 3 * head, lanes, terms)
            terms = split_stats(total, TOTALS + 3 * head, lanes, terms)
    sums = plain_dot(jnp.concatenate(weights, axis=0), fresh_ref[1]).reshape(GROUP, new_count, HD)
    for head, span in enumerate(heads):
        mixed = sums[head]
        block = slice(head * new_count, (head + 1) * new_count)
        given = [ref[0, head] for ref in states] + [ref[block] for ref in partials]
        for share, part in zip(shares[head], given):
            mixed = mixed + share * part.astype(jnp.float32)
        if as_state:
            out_ref[0, head] = mixed
        else:
            out_ref[:, span] = (mixed / divisors[head]).astype(jnp.bfloat16)
    if as_state:
        out_ref[0, GROUP] = terms


def last_kernel(parts, state_ref, *refs):
    partials, out_ref = refs[:parts], refs[-1]
    new_count = state_ref.shape[2]
    extra = state_ref[0, GROUP].astype(jnp.bfloat16)
    turned = turned_parts(partials, GROUP * new_count)
    for head in range(GROUP):
        top, total = state_stats(extra, head)
        stats = [turned_stats(part, 3 * head) for part in turned]
        best = top
        for stat in stats:
            best = jnp.maximum(best, stat)
        share = jnp.exp2(top - best)
        mixed, total = share * state_ref[0, head], share * total
        block = slice(head * new_count, (head + 1) * new_count)
        for stat, partial in zip(stats, partials):
            share = jnp.exp2(stat - best)
            total = total + share
            mixed = mixed + share * partial[block].astype(jnp.float32)
        out_ref[:, head * HD : (head + 1) * HD] = (mixed / total).astype(jnp.bfloat16)


def attend_fresh(kv_head, queries, fresh, states, partials=(), as_state=False):
    new_count = queries.shape[0]
    blocks = (1, GROUP + 1, new_count, HD)
    out_shape = jax.ShapeDtypeStruct(queries.shape, jnp.bfloat16)
    out_spec = pl.BlockSpec((new_count, BLOCK), lambda step: (0, kv_head))
    if as_state:
        out_shape = jax.ShapeDtypeStruct(blocks, jnp.float32)
        out_spec = pl.BlockSpec(blocks, lambda step: (0, 0, 0, 0))
    return pl.pallas_call(
        functools.partial(fresh_kernel, len(partials), as_state),
        grid=(1,),
        out_shape=out_shape,
        in_specs=[
            pl.BlockSpec((new_count, BLOCK), lambda step: (0, kv_head)),
            pl.BlockSpec((2, new_count, HD), lambda step: (0, 0, kv_head)),
        ]
        + [pl.BlockSpec(blocks, lambda step: (0, 0, 0, 0))] * len(states)
        + [pl.BlockSpec(partial.shape, lambda step: (0, 0)) for partial in partials],
        out_specs=out_spec,
        compiler_params=pltpu.CompilerParams(vmem_limit_bytes=VMEM_LIMIT),
        cost_estimate=cost(0.2),
    )(queries, fresh, *states, *partials)


def finish(kv_head, state, partials, before):
    new_count = before.shape[0]
    blocks = (1, GROUP + 1, new_count, HD)
    return pl.pallas_call(
        functools.partial(last_kernel, len(partials)),
        grid=(1,),
        out_shape=jax.ShapeDtypeStruct(before.shape, jnp.bfloat16),
        in_specs=[pl.BlockSpec(blocks, lambda step: (0, 0, 0, 0))]
        + [pl.BlockSpec(partial.shape, lambda step: (0, 0)) for partial in partials]
        + [ANY],
        out_specs=pl.BlockSpec((new_count, BLOCK), lambda step: (0, kv_head)),
        input_output_aliases={1 + len(partials): 0},
        compiler_params=pltpu.CompilerParams(vmem_limit_bytes=VMEM_LIMIT),
        cost_estimate=cost(0.2),
    )(state, *partials, before)


def write_kernel(holders, new_pages, base, me_ref, table_ref, *refs):
    pages = refs[:holders]
    out_ref, sem = refs[holders + 1], refs[holders + 2]
    me = me_ref[0]

    def each(action):
        for holder in range(holders):
            for page in range(new_pages):

                @pl.when(table_ref[me ^ holder, base + page] == me)
                def _(holder=holder, page=page):
                    slot = table_ref[me ^ holder, base + new_pages + page]
                    copy = pltpu.make_async_copy(
                        pages[holder].at[:, pl.ds(page * PAGE, PAGE)],
                        out_ref.at[:, slot],
                        sem.at[holder, page],
                    )
                    getattr(copy, action)()

    each("start")
    each("wait")


def write(me, tables, fresh, pool, new_pages, base):
    holders = len(fresh)
    return pl.pallas_call(
        functools.partial(write_kernel, holders, new_pages, base),
        out_shape=jax.ShapeDtypeStruct(pool.shape, pool.dtype),
        in_specs=[SMEM, SMEM]
        + [pl.BlockSpec(memory_space=pltpu.VMEM)] * holders
        + [ANY],
        out_specs=ANY,
        input_output_aliases={2 + holders: 0},
        scratch_shapes=[pltpu.SemaphoreType.DMA((holders, new_pages))],
        compiler_params=pltpu.CompilerParams(vmem_limit_bytes=8 * 1024 * 1024),
        cost_estimate=cost(0.2),
    )(me, tables, *fresh, pool)


def per_device(
    hidden,
    k_weight,
    v_weight,
    k_gain,
    queries,
    kv_pool,
    page_holder,
    page_slot,
    page_count,
    write_owner,
    write_slot,
):
    inst_count = lax.axis_size("inst")
    shards = lax.axis_size("tp")
    me = lax.axis_index("inst").astype(jnp.int32)
    rank = lax.axis_index("tp").astype(jnp.int32)
    groups = lax.axis_size("groups")
    group = lax.axis_index("groups").astype(jnp.int32)
    pages_listed = page_holder.shape[1]
    new_pages = write_owner.shape[1]
    capacity = 3 * pages_listed // (2 * inst_count)
    new_count = hidden.shape[0]
    kv_local = k_weight.shape[1] // HD
    me_list = me.reshape(1)

    def swap(array, step):
        return lax.ppermute(array, "inst", [(i, i ^ step) for i in range(inst_count)])

    def shift(array, step):
        return lax.ppermute(array, "tp", [(i, (i + step) % shards) for i in range(shards)])

    def after(array, *done):
        return lax.optimization_barrier((array,) + done)[0]

    heads = list(range(kv_local))
    base = 2 * pages_listed + 1
    own_table = jnp.concatenate(
        [page_holder[0], page_slot[0], page_count, write_owner[0], write_slot[0]]
    )
    own_table = jnp.pad(own_table, (0, 128 - own_table.shape[0]))[None]
    others = range(2, inst_count, 2)

    tables = lax.all_gather(own_table, "inst", axis=0, tiled=True)
    sent = after(queries, tables)
    asked = {0: queries, 1: swap(sent, 1)}
    for step in others:
        asked[step] = swap(sent, step)
    features = [hidden]
    forwarded = shards == 4
    for step in range(1, shards):
        direct = not forwarded or step != 2
        features.append(shift(after(hidden, tables), step) if direct else None)
    near = [features[1], features[-1]]
    if groups == 2:
        chosen = jnp.where(group == 0, k_weight, v_weight)
        weight = lax.all_gather(after(chosen, tables), ("groups", "inst"), axis=0, tiled=True)
    else:
        weight = jnp.concatenate(
            [lax.all_gather(one, "inst", axis=0, tiled=True) for one in (k_weight, v_weight)]
        )

    common = dict(pool=kv_pool, pages_listed=pages_listed, capacity=capacity)
    *found, pool_copy = attend(
        me_list, tables, [0, 1], [queries, asked[1]], heads, copy_pool=True, takes=22.0, **common
    )
    own_states, mate_states = found[:kv_local], found[kv_local:]
    last = mate_states[-1]

    lane = jnp.arange(HD, dtype=jnp.int32)
    frequency = 1000000.0 ** (-((lane % (HD // 2)).astype(jnp.float32) * 2.0) / HD)
    positions = page_count[0] * PAGE + jnp.arange(new_count, dtype=jnp.int32)
    angles = positions.astype(jnp.float32)[:, None] * frequency[None, :]
    cosine = jnp.cos(angles)
    sine = jnp.where(lane < HD // 2, -1.0, 1.0) * jnp.sin(angles)
    partials = [[] for k in heads]
    fresh = None
    for step in others:
        asked[step + 1] = swap(after(asked[step], last, *near), 1)
        if forwarded and features[2] is None:
            ahead = lax.ppermute(after(features[1], last), "tp", [(1, 2), (2, 3)])
            back = lax.ppermute(after(features[3], last), "tp", [(1, 0), (2, 1)])
            features[2] = ahead
            features.append(back)
            near = [ahead, back]
        begun = attend(
            me_list, after(tables, last, cosine, sine), [step + 1], [asked[step + 1]], heads,
            takes=12.0, **common
        )
        last = begun[-1]
        halves = [swap(after(state, *near), 1) for state in begun]
        for k in heads:
            (last,) = attend(
                me_list, after(tables, last), [step], [asked[step]], [k], state=halves[k],
                takes=0.2, **common,
            )
            partials[k].append(swap(last, step))
            if fresh is None:
                from_mate = [swap(after(state, last), 1) for state in mate_states]
                fresh = project(
                    rank.reshape(1),
                    cosine,
                    sine,
                    k_gain[None, :],
                    [after(hidden, last)] + features[1:],
                    weight,
                    shards,
                )
                last = fresh
                pages = {0: fresh, 1: swap(fresh, 1)}
                for apart in others:
                    pages[apart] = swap(fresh, apart)

    attention_out = attend_fresh(
        0, after(queries, last), fresh, [own_states[0], from_mate[0]], partials[0]
    )
    for step in others:
        pages[step + 1] = swap(after(pages[step], attention_out), 1)
    for k in heads[1:]:
        state = attend_fresh(
            k, after(queries, attention_out), fresh, [own_states[k], from_mate[k]], as_state=True
        )
        attention_out = finish(k, state, partials[k], attention_out)
    new_pool = write(
        me_list,
        tables,
        [pages[step] for step in range(inst_count)],
        pool_copy,
        new_pages,
        base,
    )
    return (attention_out, new_pool)


def solution(mesh):
    return jax.shard_map(
        per_device,
        mesh=mesh,
        in_specs=(
            P(("groups", "inst"), "tp"),
            P("inst", "tp"),
            P("inst", "tp"),
            P(),
            P(("groups", "inst"), "tp"),
            P(None, ("groups", "inst"), None, "tp"),
            P(("groups", "inst"), None),
            P(("groups", "inst"), None),
            P(("groups", "inst")),
            P(("groups", "inst"), None),
            P(("groups", "inst"), None),
        ),
        out_specs=(P(("groups", "inst"), "tp"), P(None, ("groups", "inst"), None, "tp")),
        check_vma=False,
    )
```

```python
import functools
import math

import jax
import jax.numpy as jnp
from jax import lax
from jax.experimental import pallas as pl
from jax.experimental.pallas import tpu as pltpu
from jax.sharding import PartitionSpec as P

HD = 128
PAGE = 128
GROUP = 8
BLOCK = GROUP * HD
EXTRA = 128
TOTALS = 64
STATS = 32
EMPTY = -1e30
LOG2E = 1.4426950408889634
SCALE = LOG2E / math.sqrt(HD)
CHUNK = 8
REST = (4, 2, 1)
ANY = pl.BlockSpec(memory_space=pl.ANY)
SMEM = pl.BlockSpec(memory_space=pltpu.SMEM)
VMEM_LIMIT = 63 * 1024 * 1024


def cost(microseconds):
    return pl.CostEstimate(
        flops=int(microseconds * 1e9), bytes_accessed=int(microseconds * 3e6), transcendentals=0
    )


def row_dot(a, b):
    return lax.dot_general(a, b, (((1,), (1,)), ((), ())), preferred_element_type=jnp.float32)


def plain_dot(a, b):
    return lax.dot_general(a, b, (((1,), (0,)), ((), ())), preferred_element_type=jnp.float32)


def split_stats(stat, lane, lanes, terms):
    high = stat.astype(jnp.bfloat16).astype(jnp.float32)
    rest = stat - high
    middle = rest.astype(jnp.bfloat16).astype(jnp.float32)
    terms = jnp.where(lanes == lane, high, terms)
    terms = jnp.where(lanes == lane + 1, middle, terms)
    return jnp.where(lanes == lane + 2, rest - middle, terms)


def joined_stats(extra, lane):
    term = lax.broadcasted_iota(jnp.int32, (EXTRA, HD), 0)
    picked = jnp.where((term >= lane) & (term < lane + 3), 1.0, 0.0).astype(jnp.bfloat16)
    return plain_dot(extra, picked)


def turned_stats(turned, lane):
    term = lax.broadcasted_iota(jnp.int32, (STATS, HD), 0)
    picked = jnp.where((term >= lane) & (term < lane + 3), 1.0, 0.0).astype(jnp.bfloat16)
    return lax.dot_general(
        turned, picked, (((0,), (0,)), ((), ())), preferred_element_type=jnp.float32
    )


def state_stats(extra, head):
    return joined_stats(extra, 3 * head), joined_stats(extra, TOTALS + 3 * head)


def attend_kernel(plan, refs):
    steps, kv_heads, pages_listed = plan["steps"], plan["kv_heads"], plan["pages_listed"]
    requests = len(steps)
    copy_pool, resume = plan["copy_pool"], plan["resume"]
    width = len(kv_heads)
    items = requests * width
    refs = list(refs)
    me_ref, table_ref = refs.pop(0), refs.pop(0)
    q_refs = [refs.pop(0) for _ in range(requests)]
    state_ref = refs.pop(0) if resume else None
    pool_ref = refs.pop(0)
    out_refs = [refs.pop(0) for _ in range(items)]
    new_pool_ref = refs.pop(0) if copy_pool else None
    q_buf, q_two, kv_buf, acc, maxima, totals, slots, q_sem, kv_sem, out_sem = refs[:10]
    refs = refs[10:]
    if resume:
        send_buf = refs.pop(0)
    new_count = q_buf.shape[2]
    rows = GROUP * new_count
    shape = (GROUP, new_count, HD)
    lanes = lax.broadcasted_iota(jnp.int32, (new_count, HD), 1)

    def q_copies(item):
        offset = kv_heads[item % width] * BLOCK
        return [
            pltpu.make_async_copy(
                q_refs[item // width].at[:, pl.ds(offset + head * HD, HD)],
                q_buf.at[item, head],
                q_sem.at[item, head],
            )
            for head in range(GROUP)
        ]

    def page_copies(request, place, slot):
        return [
            pltpu.make_async_copy(
                pool_ref.at[:, slot, :, pl.ds(kv_head * HD, HD)],
                kv_buf.at[request, column, :, place],
                kv_sem.at[request, column, place],
            )
            for column, kv_head in enumerate(kv_heads)
        ]

    def out_copy(item, index):
        if resume:
            part = [pl.ds(0, rows), pl.ds(rows, send_buf.shape[1] - rows)][index]
            source, target = send_buf.at[item, part], out_refs[item].at[part]
        else:
            part = [pl.ds(0, GROUP), pl.ds(GROUP, 1)][index]
            source, target = acc.at[item, part], out_refs[item].at[0, part]
        return pltpu.make_async_copy(source, target, out_sem.at[item, index])

    for item in range(items):
        for copy in q_copies(item):
            copy.start()
    if resume:
        state_copy = pltpu.make_async_copy(state_ref, acc, out_sem.at[0, 0])
        state_copy.start()
    me = me_ref[0]
    for request, apart in enumerate(steps):
        whose = me ^ apart
        count = table_ref[whose, 2 * pages_listed]

        def look(page, found, request=request, whose=whose, count=count):
            mine = (page < count) & (table_ref[whose, page] == me)

            @pl.when(mine)
            def _():
                for copy in page_copies(request, found, table_ref[whose, pages_listed + page]):
                    copy.start()

            return found + mine.astype(jnp.int32)

        slots[request] = lax.fori_loop(0, count, look, 0)
    pool_in, pool_out = [], []
    if copy_pool:
        pool_buf, pool_sem = refs
        slot_total = pool_ref.shape[1]
        parts = pool_sem.shape[1]
        step = slot_total // parts
        for index in range(2):
            for part in range(parts):
                piece = (index, pl.ds(part * step, step))
                sem = pool_sem.at[index, part]
                pool_in.append(pltpu.make_async_copy(pool_ref.at[piece], pool_buf.at[piece], sem))
                pool_out.append(
                    pltpu.make_async_copy(pool_buf.at[piece], new_pool_ref.at[piece], sem)
                )
        for copy in pool_in:
            copy.start()
    for item in range(items):
        for copy in q_copies(item):
            copy.wait()
    if resume:
        state_copy.wait()

    def one_item(item, carry):
        request = item // width
        column = item % width
        found = slots[request]
        sums = pl.ds(0, GROUP)
        scaled = q_buf[item].reshape(rows, HD).astype(jnp.float32) * SCALE
        high = scaled.astype(jnp.bfloat16)
        q_two[:, :HD] = high
        q_two[:, HD:] = (scaled - high.astype(jnp.float32)).astype(jnp.bfloat16)
        if resume:
            extra = acc[item, GROUP].astype(jnp.bfloat16)
            for head in range(GROUP):
                maxima[head], total = state_stats(extra, head)
                totals[head] = jnp.where(lanes == 0, total, 0.0)
        else:
            acc[item, sums] = jnp.zeros(shape, jnp.float32)
            totals[...] = jnp.zeros(shape, jnp.float32)
            maxima[...] = jnp.full(shape, EMPTY, jnp.float32)

        @pl.when(column == 0)
        def _():
            def arrived(place, carry):
                for copy in page_copies(request, place, 0):
                    copy.wait()
                return carry

            lax.fori_loop(0, found, arrived, 0)

        def chunk(first, count):
            keys = kv_buf[request, column, 0, pl.ds(first, count)].reshape(count * PAGE, HD)
            values = kv_buf[request, column, 1, pl.ds(first, count)].reshape(count * PAGE, HD)
            scores = row_dot(q_two[...], jnp.concatenate([keys, keys], axis=1))
            old = maxima[...].reshape(rows, HD)
            top = jnp.maximum(old, jnp.max(scores, axis=1, keepdims=True))
            rescale = jnp.exp2(old - top)
            total = totals[...].reshape(rows, HD) * rescale
            pieces = []
            for part in range(count):
                piece = jnp.exp2(scores[:, part * PAGE : (part + 1) * PAGE] - top)
                total = total + piece
                pieces.append(piece.astype(jnp.bfloat16))
            weights = jnp.concatenate(pieces, axis=1) if count > 1 else pieces[0]
            maxima[...] = top.reshape(shape)
            totals[...] = total.reshape(shape)
            acc[item, sums] = acc[item, sums] * rescale.reshape(shape) + plain_dot(
                weights, values
            ).reshape(shape)

        whole = found // CHUNK
        left = found % CHUNK

        def step(index, carry):
            chunk(index * CHUNK, CHUNK)
            return carry

        lax.fori_loop(0, whole, step, 0)
        done = whole * CHUNK
        for count in REST:

            @pl.when((left & count) != 0)
            def _(count=count, done=done):
                chunk(done, count)

            done = done + (left & count)

        def send(index):
            for each in range(items):

                @pl.when(item == each)
                def _(each=each):
                    out_copy(each, index).start()

        if not resume:
            send(0)
        terms = jnp.zeros((new_count, HD), jnp.float32)
        for head in range(GROUP):
            total = jnp.sum(totals[head], axis=1, keepdims=True)
            if resume:
                some = total > 0.0
                safe = jnp.where(some, total, 1.0)
                send_buf[item, head * new_count : (head + 1) * new_count] = (
                    acc[item, head] * (1.0 / safe)
                ).astype(jnp.bfloat16)
                stat = jnp.where(some, maxima[head] + jnp.log2(safe), EMPTY)
                terms = split_stats(stat, 3 * head, lanes, terms)
            else:
                terms = split_stats(maxima[head], 3 * head, lanes, terms)
                terms = split_stats(total, TOTALS + 3 * head, lanes, terms)
        if resume:
            turned = terms.T[:STATS].astype(jnp.bfloat16)
            for piece in range(new_count // HD):
                send_buf[item, rows + piece * STATS : rows + (piece + 1) * STATS] = turned[
                    :, piece * HD : (piece + 1) * HD
                ]
            send(0)
        else:
            acc[item, GROUP] = terms
        send(1)
        if copy_pool:

            @pl.when(item == 0)
            def _():
                for copy_in, copy_out in zip(pool_in, pool_out):
                    copy_in.wait()
                    copy_out.start()

        return carry

    lax.fori_loop(0, items, one_item, 0)
    for item in range(items):
        for index in range(2):
            out_copy(item, index).wait()
    for copy in pool_out:
        copy.wait()


def attend(
    me, tables, steps, asked, kv_heads, pool, pages_listed, capacity, takes, state=None, copy_pool=False
):
    requests, width, new_count = len(steps), len(kv_heads), asked[0].shape[0]
    items = requests * width
    resume = state is not None
    blocks = (GROUP + 1, new_count, HD)
    parcel = (GROUP * new_count + STATS * new_count // HD, HD)
    if resume:
        out_shape = [jax.ShapeDtypeStruct(parcel, jnp.bfloat16) for _ in range(items)]
    else:
        out_shape = [jax.ShapeDtypeStruct((1,) + blocks, jnp.float32) for _ in range(items)]
    scratch = [
        pltpu.VMEM((items, GROUP, new_count, HD), jnp.bfloat16),
        pltpu.VMEM((GROUP * new_count, 2 * HD), jnp.bfloat16),
        pltpu.VMEM((requests, width, 2, capacity, PAGE, HD), jnp.bfloat16),
        pltpu.VMEM((items,) + blocks, jnp.float32),
        pltpu.VMEM((GROUP, new_count, HD), jnp.float32),
        pltpu.VMEM((GROUP, new_count, HD), jnp.float32),
        pltpu.SMEM((requests,), jnp.int32),
        pltpu.SemaphoreType.DMA((items, GROUP)),
        pltpu.SemaphoreType.DMA((requests, width, capacity)),
        pltpu.SemaphoreType.DMA((items, 2)),
    ]
    if resume:
        scratch.append(pltpu.VMEM((items,) + parcel, jnp.bfloat16))
    if copy_pool:
        out_shape.append(jax.ShapeDtypeStruct(pool.shape, pool.dtype))
        parts = next(part for part in (6, 3, 2, 1) if pool.shape[1] % part == 0)
        scratch += [pltpu.VMEM(pool.shape, pool.dtype), pltpu.SemaphoreType.DMA((2, parts))]
    plan = dict(
        steps=steps, kv_heads=kv_heads, pages_listed=pages_listed, copy_pool=copy_pool,
        resume=resume,
    )
    return pl.pallas_call(
        lambda *refs: attend_kernel(plan, refs),
        out_shape=out_shape,
        in_specs=[SMEM, SMEM] + [ANY] * (requests + resume + 1),
        out_specs=[ANY] * len(out_shape),
        scratch_shapes=scratch,
        compiler_params=pltpu.CompilerParams(vmem_limit_bytes=VMEM_LIMIT),
        cost_estimate=cost(takes),
    )(me, tables, *asked, *([state] if resume else []), pool)


def project_kernel(shards, forwarded, rank_ref, cos_ref, sin_ref, gain_ref, *refs):
    hidden_refs, weight_ref = refs[:-6], refs[-6]
    out_ref, features, gathered, feature_sem, weight_sem = refs[-5:]
    rank = rank_ref[0]
    span = features.shape[2]
    depth, width = gathered.shape[0], gathered.shape[1] // 2

    def copies(shard):
        return [
            pltpu.make_async_copy(
                weight_ref.at[pl.ds(kind * depth + shard * span, span)],
                gathered.at[pl.ds(shard * span, span), pl.ds(kind * width, width)],
                weight_sem.at[kind, shard],
            )
            for kind in range(2)
        ]

    def feature_copy(step, ref):
        shard = lax.rem(rank + shards - step, shards)
        return pltpu.make_async_copy(ref, features.at[shard], feature_sem.at[step])

    for step in range(shards):
        if forwarded and step == 2:
            @pl.when(rank >= 2)
            def _():
                feature_copy(2, hidden_refs[2]).start()

            @pl.when(rank < 2)
            def _():
                feature_copy(2, hidden_refs[shards]).start()

        else:
            feature_copy(step, hidden_refs[step]).start()
    for shard in range(shards):
        for copy in copies(shard):
            copy.start()
    for step in range(shards):
        feature_copy(step, hidden_refs[step]).wait()
    raw = 0.0
    for shard in range(shards):
        for copy in copies(shard):
            copy.wait()
        raw = raw + plain_dot(features[shard], gathered[shard * span : (shard + 1) * span])
    columns = []
    for head in range(width // HD):
        one = raw[:, head * HD : (head + 1) * HD]
        mean = jnp.sum(one * one, axis=1, keepdims=True) * (1.0 / HD)
        one = one * lax.rsqrt(mean + 1e-06) * gain_ref[...]
        columns.append(one * cos_ref[...] + pltpu.roll(one, HD // 2, 1) * sin_ref[...])
    new_keys = jnp.concatenate(columns, axis=1) if len(columns) > 1 else columns[0]
    out_ref[0] = new_keys.astype(jnp.bfloat16)
    out_ref[1] = raw[:, width:].astype(jnp.bfloat16)


def project(rank, cos, sin, gain, hidden, weight, shards):
    new_count, span = hidden[0].shape
    depth, width = weight.shape[0] // 2, weight.shape[1]
    vmem = pl.BlockSpec(memory_space=pltpu.VMEM)
    return pl.pallas_call(
        functools.partial(project_kernel, shards, len(hidden) > shards),
        out_shape=jax.ShapeDtypeStruct((2, new_count, width), jnp.bfloat16),
        in_specs=[SMEM, vmem, vmem, vmem] + [ANY] * (len(hidden) + 1),
        out_specs=vmem,
        scratch_shapes=[
            pltpu.VMEM((shards, new_count, span), jnp.bfloat16),
            pltpu.VMEM((depth, 2 * width), jnp.bfloat16),
            pltpu.SemaphoreType.DMA((shards,)),
            pltpu.SemaphoreType.DMA((2, shards)),
        ],
        compiler_params=pltpu.CompilerParams(vmem_limit_bytes=VMEM_LIMIT),
        cost_estimate=cost(0.2),
    )(rank, cos, sin, gain, *hidden, weight)


def turned_parts(partials, rows):
    return [
        jnp.concatenate(
            [part[start : start + STATS] for start in range(rows, part.shape[0], STATS)], axis=1
        )
        for part in partials
    ]


def fresh_kernel(parts, as_state, q_ref, fresh_ref, *refs):
    states, partials, out_ref = refs[:2], refs[2 : 2 + parts], refs[-1]
    new_count = q_ref.shape[0]
    rows = GROUP * new_count
    row = lax.broadcasted_iota(jnp.int32, (new_count, new_count), 0)
    column = lax.broadcasted_iota(jnp.int32, (new_count, new_count), 1)
    lanes = lax.broadcasted_iota(jnp.int32, (new_count, HD), 1)
    heads = [slice(head * HD, (head + 1) * HD) for head in range(GROUP)]
    stacked = jnp.concatenate([q_ref[:, span] for span in heads], axis=0)
    scores = row_dot(stacked, fresh_ref[0]).reshape(GROUP, new_count, new_count)
    scores = jnp.where((column <= row)[None], scores * SCALE, EMPTY)
    extras = [ref[0, GROUP].astype(jnp.bfloat16) for ref in states]
    turned = turned_parts(partials, rows)
    weights, shares, divisors = [], [], []
    terms = jnp.zeros((new_count, HD), jnp.float32)
    for head in range(GROUP):
        stats = [state_stats(extra, head) for extra in extras]
        stats += [(turned_stats(part, 3 * head), 1.0) for part in turned]
        top = jnp.broadcast_to(jnp.max(scores[head], axis=1, keepdims=True), (new_count, HD))
        for other, _ in stats:
            top = jnp.maximum(top, other)
        pieces = [
            jnp.exp2(scores[head, :, start : start + HD] - top) for start in range(0, new_count, HD)
        ]
        total = jnp.broadcast_to(jnp.sum(sum(pieces), axis=1, keepdims=True), (new_count, HD))
        shares.append([jnp.exp2(other - top) for other, _ in stats])
        for share, (_, part) in zip(shares[-1], stats):
            total = total + share * part
        divisors.append(total)
        weights.append(jnp.concatenate(pieces, axis=1).astype(jnp.bfloat16))
        if as_state:
            terms = split_stats(top, 3 * head, lanes, terms)
            terms = split_stats(total, TOTALS + 3 * head, lanes, terms)
    sums = plain_dot(jnp.concatenate(weights, axis=0), fresh_ref[1]).reshape(GROUP, new_count, HD)
    for head, span in enumerate(heads):
        mixed = sums[head]
        block = slice(head * new_count, (head + 1) * new_count)
        given = [ref[0, head] for ref in states] + [ref[block] for ref in partials]
        for share, part in zip(shares[head], given):
            mixed = mixed + share * part.astype(jnp.float32)
        if as_state:
            out_ref[0, head] = mixed
        else:
            out_ref[:, span] = (mixed / divisors[head]).astype(jnp.bfloat16)
    if as_state:
        out_ref[0, GROUP] = terms


def last_kernel(parts, state_ref, *refs):
    partials, out_ref = refs[:parts], refs[-1]
    new_count = state_ref.shape[2]
    extra = state_ref[0, GROUP].astype(jnp.bfloat16)
    turned = turned_parts(partials, GROUP * new_count)
    for head in range(GROUP):
        top, total = state_stats(extra, head)
        stats = [turned_stats(part, 3 * head) for part in turned]
        best = top
        for stat in stats:
            best = jnp.maximum(best, stat)
        share = jnp.exp2(top - best)
        mixed, total = share * state_ref[0, head], share * total
        block = slice(head * new_count, (head + 1) * new_count)
        for stat, partial in zip(stats, partials):
            share = jnp.exp2(stat - best)
            total = total + share
            mixed = mixed + share * partial[block].astype(jnp.float32)
        out_ref[:, head * HD : (head + 1) * HD] = (mixed / total).astype(jnp.bfloat16)


def attend_fresh(kv_head, queries, fresh, states, partials=(), as_state=False):
    new_count = queries.shape[0]
    blocks = (1, GROUP + 1, new_count, HD)
    out_shape = jax.ShapeDtypeStruct(queries.shape, jnp.bfloat16)
    out_spec = pl.BlockSpec((new_count, BLOCK), lambda step: (0, kv_head))
    if as_state:
        out_shape = jax.ShapeDtypeStruct(blocks, jnp.float32)
        out_spec = pl.BlockSpec(blocks, lambda step: (0, 0, 0, 0))
    return pl.pallas_call(
        functools.partial(fresh_kernel, len(partials), as_state),
        grid=(1,),
        out_shape=out_shape,
        in_specs=[
            pl.BlockSpec((new_count, BLOCK), lambda step: (0, kv_head)),
            pl.BlockSpec((2, new_count, HD), lambda step: (0, 0, kv_head)),
        ]
        + [pl.BlockSpec(blocks, lambda step: (0, 0, 0, 0))] * len(states)
        + [pl.BlockSpec(partial.shape, lambda step: (0, 0)) for partial in partials],
        out_specs=out_spec,
        compiler_params=pltpu.CompilerParams(vmem_limit_bytes=VMEM_LIMIT),
        cost_estimate=cost(0.2),
    )(queries, fresh, *states, *partials)


def finish(kv_head, state, partials, before):
    new_count = before.shape[0]
    blocks = (1, GROUP + 1, new_count, HD)
    return pl.pallas_call(
        functools.partial(last_kernel, len(partials)),
        grid=(1,),
        out_shape=jax.ShapeDtypeStruct(before.shape, jnp.bfloat16),
        in_specs=[pl.BlockSpec(blocks, lambda step: (0, 0, 0, 0))]
        + [pl.BlockSpec(partial.shape, lambda step: (0, 0)) for partial in partials]
        + [ANY],
        out_specs=pl.BlockSpec((new_count, BLOCK), lambda step: (0, kv_head)),
        input_output_aliases={1 + len(partials): 0},
        compiler_params=pltpu.CompilerParams(vmem_limit_bytes=VMEM_LIMIT),
        cost_estimate=cost(0.2),
    )(state, *partials, before)


def write_kernel(holders, new_pages, base, me_ref, table_ref, *refs):
    pages = refs[:holders]
    out_ref, sem = refs[holders + 1], refs[holders + 2]
    me = me_ref[0]

    def each(action):
        for holder in range(holders):
            for page in range(new_pages):

                @pl.when(table_ref[me ^ holder, base + page] == me)
                def _(holder=holder, page=page):
                    slot = table_ref[me ^ holder, base + new_pages + page]
                    copy = pltpu.make_async_copy(
                        pages[holder].at[:, pl.ds(page * PAGE, PAGE)],
                        out_ref.at[:, slot],
                        sem.at[holder, page],
                    )
                    getattr(copy, action)()

    each("start")
    each("wait")


def write(me, tables, fresh, pool, new_pages, base):
    holders = len(fresh)
    return pl.pallas_call(
        functools.partial(write_kernel, holders, new_pages, base),
        out_shape=jax.ShapeDtypeStruct(pool.shape, pool.dtype),
        in_specs=[SMEM, SMEM]
        + [pl.BlockSpec(memory_space=pltpu.VMEM)] * holders
        + [ANY],
        out_specs=ANY,
        input_output_aliases={2 + holders: 0},
        scratch_shapes=[pltpu.SemaphoreType.DMA((holders, new_pages))],
        compiler_params=pltpu.CompilerParams(vmem_limit_bytes=8 * 1024 * 1024),
        cost_estimate=cost(0.2),
    )(me, tables, *fresh, pool)


def per_device(
    hidden,
    k_weight,
    v_weight,
    k_gain,
    queries,
    kv_pool,
    page_holder,
    page_slot,
    page_count,
    write_owner,
    write_slot,
):
    inst_count = lax.axis_size("inst")
    shards = lax.axis_size("tp")
    me = lax.axis_index("inst").astype(jnp.int32)
    rank = lax.axis_index("tp").astype(jnp.int32)
    groups = lax.axis_size("groups")
    group = lax.axis_index("groups").astype(jnp.int32)
    pages_listed = page_holder.shape[1]
    new_pages = write_owner.shape[1]
    capacity = 3 * pages_listed // (2 * inst_count)
    new_count = hidden.shape[0]
    kv_local = k_weight.shape[1] // HD
    me_list = me.reshape(1)

    def swap(array, step):
        return lax.ppermute(array, "inst", [(i, i ^ step) for i in range(inst_count)])

    def shift(array, step):
        return lax.ppermute(array, "tp", [(i, (i + step) % shards) for i in range(shards)])

    def after(array, *done):
        return lax.optimization_barrier((array,) + done)[0]

    heads = list(range(kv_local))
    base = 2 * pages_listed + 1
    own_table = jnp.concatenate(
        [page_holder[0], page_slot[0], page_count, write_owner[0], write_slot[0]]
    )
    own_table = jnp.pad(own_table, (0, 128 - own_table.shape[0]))[None]
    others = range(2, inst_count, 2)

    tables = lax.all_gather(own_table, "inst", axis=0, tiled=True)
    sent = after(queries, tables)
    asked = {0: queries, 1: swap(sent, 1)}
    for step in others:
        asked[step] = swap(sent, step)
    features = [hidden]
    forwarded = shards == 4
    for step in range(1, shards):
        direct = not forwarded or step != 2
        features.append(shift(after(hidden, tables), step) if direct else None)
    near = [features[1], features[-1]]
    if groups == 2:
        chosen = jnp.where(group == 0, k_weight, v_weight)
        weight = lax.all_gather(after(chosen, tables), ("groups", "inst"), axis=0, tiled=True)
    else:
        weight = jnp.concatenate(
            [lax.all_gather(one, "inst", axis=0, tiled=True) for one in (k_weight, v_weight)]
        )

    common = dict(pool=kv_pool, pages_listed=pages_listed, capacity=capacity)
    *found, pool_copy = attend(
        me_list, tables, [0, 1], [queries, asked[1]], heads, copy_pool=True, takes=22.0, **common
    )
    own_states, mate_states = found[:kv_local], found[kv_local:]
    last = mate_states[-1]

    lane = jnp.arange(HD, dtype=jnp.int32)
    frequency = 1000000.0 ** (-((lane % (HD // 2)).astype(jnp.float32) * 2.0) / HD)
    positions = page_count[0] * PAGE + jnp.arange(new_count, dtype=jnp.int32)
    angles = positions.astype(jnp.float32)[:, None] * frequency[None, :]
    cosine = jnp.cos(angles)
    sine = jnp.where(lane < HD // 2, -1.0, 1.0) * jnp.sin(angles)
    partials = [[] for k in heads]
    fresh = None
    for step in others:
        asked[step + 1] = swap(after(asked[step], last, *near), 1)
        if forwarded and features[2] is None:
            ahead = lax.ppermute(after(features[1], last), "tp", [(1, 2), (2, 3)])
            back = lax.ppermute(after(features[3], last), "tp", [(1, 0), (2, 1)])
            features[2] = ahead
            features.append(back)
            near = [ahead, back]
        begun = attend(
            me_list, after(tables, last, cosine, sine), [step + 1], [asked[step + 1]], heads,
            takes=12.0, **common
        )
        last = begun[-1]
        halves = [swap(after(state, *near), 1) for state in begun]
        for k in heads:
            (last,) = attend(
                me_list, after(tables, last), [step], [asked[step]], [k], state=halves[k],
                takes=0.2, **common,
            )
            partials[k].append(swap(last, step))
            if fresh is None:
                from_mate = [swap(after(state, last), 1) for state in mate_states]
                fresh = project(
                    rank.reshape(1),
                    cosine,
                    sine,
                    k_gain[None, :],
                    [after(hidden, last)] + features[1:],
                    weight,
                    shards,
                )
                last = fresh
                pages = {0: fresh, 1: swap(fresh, 1)}
                for apart in others:
                    pages[apart] = swap(fresh, apart)

    attention_out = attend_fresh(
        0, after(queries, last), fresh, [own_states[0], from_mate[0]], partials[0]
    )
    for step in others:
        pages[step + 1] = swap(after(pages[step], attention_out), 1)
    for k in heads[1:]:
        state = attend_fresh(
            k, after(queries, attention_out), fresh, [own_states[k], from_mate[k]], as_state=True
        )
        attention_out = finish(k, state, partials[k], attention_out)
    new_pool = write(
        me_list,
        tables,
        [pages[step] for step in range(inst_count)],
        pool_copy,
        new_pages,
        base,
    )
    return (attention_out, new_pool)


def solution(mesh):
    return jax.shard_map(
        per_device,
        mesh=mesh,
        in_specs=(
            P(("groups", "inst"), "tp"),
            P("inst", "tp"),
            P("inst", "tp"),
            P(),
            P(("groups", "inst"), "tp"),
            P(None, ("groups", "inst"), None, "tp"),
            P(("groups", "inst"), None),
            P(("groups", "inst"), None),
            P(("groups", "inst")),
            P(("groups", "inst"), None),
            P(("groups", "inst"), None),
        ),
        out_specs=(P(("groups", "inst"), "tp"), P(None, ("groups", "inst"), None, "tp")),
        check_vma=False,
    )
```
